32 devices in a mesh: seq: 4 (over z), dp: 8 (over y, x, core).
Axes of the slice: x: 2, y: 2, z: 4, core: 2. Of those that a mesh axis runs over, the one named last changes fastest.
Arguments:
- tokens: bfloat16 [64, 1024, 640], P('dp', 'seq'), may hold values from -6 to 6
- weights: bfloat16 [1280, 1920], P(('seq', 'dp')), may hold values from -0.15625 to 0.15625
- bias: float32 [1920], replicated, may hold values from -3 to 9
- resets: int32 [64, 1024], P('dp', 'seq'), may hold values from 0 to 1, as said below
- upstream: bfloat16 [64, 1024, 640], P('dp', 'seq'), may hold values from -6 to 6
Outputs:
- hidden: bfloat16 [64, 1024, 640], P('dp', 'seq')
- grad_tokens: bfloat16 [64, 1024, 640], P('dp', 'seq')
- grad_weights: float32 [1280, 1920], P(('seq', 'dp'))
- grad_bias: float32 [1920], replicated
The draws below stay inside these ranges and needn't reach their ends.
Inputs may be any that keep to these rules, and one draw needn't show every extreme that they name: In each group of 8 sequences of one dp index, one sequence, drawn from the seed, has no resets; the others may have resets at uneven places.
All inputs are finite; a program needn't handle non-finite values.
Results may differ from the reference program's by a relative error of at most 0.0049.
Values may be sent and summed in bfloat16 or wider, within the bound.
A program may use at most 128 MiB of HBM per device.

```python
import jax
import jax.numpy as jnp
from jax import lax

D = 640
LEN = 1024
S_DEV = 8
SEQS = 64
N_DP = 8


def draw_bias(key, part):
    key = jax.random.fold_in(key, 11)
    key_z, key_f, key_o = jax.random.split(key, 3)
    forget = jax.random.uniform(key_f, (D,), jnp.float32, -1.0, 8.0)
    z_part = jnp.clip(0.5 * jax.random.normal(key_z, (D,), jnp.float32), -3.0, 3.0)
    o_part = jnp.clip(0.5 * jax.random.normal(key_o, (D,), jnp.float32), -3.0, 3.0)
    return jnp.concatenate([z_part, forget, o_part])


def draw_resets(key, part):
    key = jax.random.fold_in(key, 23)
    key_marks, key_pick = jax.random.split(key)
    marks = (jax.random.randint(key_marks, (SEQS, LEN), 0, LEN) < 3).astype(jnp.int32)
    chosen = jax.random.randint(key_pick, (SEQS // S_DEV, 1), 0, S_DEV)
    whole_doc = (jnp.arange(S_DEV)[None, :] == chosen).reshape(SEQS, 1)
    return jnp.where(whole_doc, 0, marks).astype(jnp.int32)


def block_levels(own_key, dims, cuts, low, high):
    gain = 1.0
    for position, parts in cuts:
        draws = jax.random.uniform(jax.random.fold_in(jax.random.fold_in(own_key, 6), position), (parts,), jnp.float32, low / len(cuts), high / len(cuts))
        gain = gain * jnp.repeat(jnp.exp(draws), dims[position] // parts).reshape((-1,) + (1,) * (len(dims) - 1 - position))
    return gain


def centred(key, extent, scale, reach, cuts=(), kind=jnp.bfloat16):
    values = jax.random.normal(key, extent, jnp.float32) * scale
    if len(cuts) > 0:
        values = block_levels(key, extent, cuts, -0.22, 0.18) * values
    return jnp.clip(values, min=-reach, max=reach).astype(kind)


def setup_inputs(seed: int = 0) -> dict:
    streams_of = jax.random.split(jax.random.key(seed), 6)
    tokens = centred(streams_of[0], (SEQS, LEN, D), 1.0, 6.0, ((0, 8), (1, 4)))
    weights = centred(streams_of[1], (2 * D, 3 * D), (2 * D) ** -0.5, 0.15625, ((0, 32),))
    bias = draw_bias(jax.random.fold_in(streams_of[5], 71), 0)
    resets = draw_resets(jax.random.fold_in(streams_of[5], 71), 0)
    upstream = centred(streams_of[4], (SEQS, LEN, D), 1.0, 6.0, ((0, 8), (1, 4)))
    return {"tokens": tokens, "weights": weights, "bias": bias, "resets": resets, "upstream": upstream}


@jax.custom_vjp
def low(v):
    return lax.optimization_barrier(v.astype(jnp.bfloat16)).astype(jnp.float32)

@jax.custom_vjp
def low_back(v):
    return v

def low_keep(v):
    return (low(v), None)

def low_pass(kept, grad):
    return (grad,)

def back_keep(v):
    return (v, None)

def back_low(kept, grad):
    return (low(grad),)
low.defvjp(low_keep, low_pass)
low_back.defvjp(back_keep, back_low)

def combine(earlier, later):
    return (earlier[0] * later[0], later[0] * earlier[1] + later[1])

def forward(tokens, weights, bias, resets):
    keep_mask = (1 - resets).astype(tokens.dtype)[..., None]
    shifted = jnp.concatenate([jnp.zeros_like(tokens[:, :1]), tokens[:, :-1]], axis=1) * keep_mask
    joined = jnp.concatenate([tokens, shifted], axis=2)
    preact = low_back(jnp.einsum('gtk,kn->gtn', joined, weights, precision=lax.Precision.HIGHEST) + bias)
    model_width = tokens.shape[2]
    z_gate = jnp.tanh(preact[..., :model_width])
    f_gate = jax.nn.sigmoid(preact[..., model_width:2 * model_width])
    o_gate = jax.nn.sigmoid(preact[..., 2 * model_width:])
    effective = f_gate * keep_mask
    fresh = (1 - f_gate) * z_gate
    gains, cell_state = lax.associative_scan(combine, (effective, fresh), axis=1)
    return o_gate * cell_state

def reference(tokens, weights, bias, resets, upstream):
    weights_full = weights.astype(jnp.float32)

    def step(carry, item):
        group_tokens, group_resets, group_upstream = item
        output, pull = jax.vjp(lambda a, w, b: forward(a, w, b, group_resets), group_tokens.astype(jnp.float32), weights_full, bias)
        grad_x, grad_w, grad_b = pull(group_upstream.astype(jnp.float32))
        return ((carry[0] + grad_w, carry[1] + grad_b), (output.astype(jnp.bfloat16), grad_x.astype(jnp.bfloat16)))
    start_sums = (jnp.zeros(weights_full.shape, jnp.float32), jnp.zeros(bias.shape, jnp.float32))
    groups = (tokens.reshape(N_DP, S_DEV, LEN, D), resets.reshape(N_DP, S_DEV, LEN), upstream.reshape(N_DP, S_DEV, LEN, D))
    sums, stacked = lax.scan(step, start_sums, groups)
    return (stacked[0].reshape(tokens.shape), stacked[1].reshape(tokens.shape), sums[0], sums[1])
```

```python
import functools

import jax
import jax.numpy as jnp
from jax import lax
from jax.experimental import pallas as pl
from jax.experimental.pallas import tpu as pltpu
from jax.sharding import PartitionSpec as P

MESH = pl.DeviceIdType.MESH
BF = jnp.bfloat16
F32 = jnp.float32
LANES = 128
STEPS = 32
TWO = 16


def cut_chunks(width):
    tiles = width // LANES
    chunks, at = [], 0
    if tiles % 2:
        chunks.append((0, LANES))
        at = LANES
    while at < width:
        chunks.append((at, 2 * LANES))
        at += 2 * LANES
    return chunks


def dot(a, b):
    return jnp.dot(a, b, preferred_element_type=F32)


def layer_kernel(
    span, chunks,
    tok, wts, bias, resets, up,
    hid, gtok, gw, gb,
    raw_t, raw_u, joined, upt, wv, gates, qf, gp, keepb, perm, pinv, hb, gwv, summ, edge,
    in_sem, w_sem, out_sem, gw_sem, sum_send, sum_recv, edge_send, edge_recv,
):
    seqs, steps, width = tok.shape
    rows = seqs * steps
    block = seqs * STEPS
    blocks = steps // STEPS
    me = lax.axis_index("seq")
    col = lax.axis_index("dp")

    barrier = pltpu.get_barrier_semaphore()
    for k in range(1, span):
        pl.semaphore_signal(
            barrier, inc=1, device_id=(lax.rem(me + k, span), col), device_id_type=MESH
        )
    pl.semaphore_wait(barrier, span - 1)

    in_t = pltpu.make_async_copy(tok, raw_t, in_sem.at[0])
    in_u = pltpu.make_async_copy(up, raw_u, in_sem.at[1])
    in_t.start()
    in_u.start()
    w_copies = []
    for c, (at, cw) in enumerate(chunks):
        for g in range(3):
            w_copies.append(
                pltpu.make_async_copy(
                    wts.at[:, pl.ds(g * width + at, cw)],
                    wv.at[:, pl.ds(3 * at + g * cw, cw)],
                    w_sem.at[c, g],
                )
            )
    for copy in w_copies:
        copy.start()

    r = lax.broadcasted_iota(jnp.int32, (block, block), 0)
    q = lax.broadcasted_iota(jnp.int32, (block, block), 1)
    perm[...] = (((q & 31) == (r >> 3)) & ((q >> 5) == (r & 7))).astype(F32).astype(BF)
    pinv[...] = (((r & 31) == (q >> 3)) & ((r >> 5) == (q & 7))).astype(F32).astype(BF)
    keep = 1.0 - resets[...].astype(F32)
    tiled = jnp.broadcast_to(keep[None], (STEPS, seqs, steps)).reshape(block, steps)
    row_t = lax.broadcasted_iota(jnp.int32, (block, steps), 0) >> 3
    lane_t = lax.broadcasted_iota(jnp.int32, (block, steps), 1)
    ones = jnp.ones((steps, LANES), BF)
    for b in range(blocks):
        picked = jnp.where(lane_t == row_t + b * STEPS, tiled, 0.0).astype(BF)
        keepb[b * block : (b + 1) * block, :] = dot(picked, ones)

    def wide_keep(at, count, lanes):
        k = keepb[pl.ds(at, count), :]
        return jnp.concatenate([k] * (lanes // LANES), axis=1)

    in_t.wait()
    last_rows = raw_t[:, steps - STEPS :, :].reshape(block, width)
    edge[0] = dot(perm[block - TWO :, :], last_rows)[TWO - seqs :]
    to_right = pltpu.make_async_remote_copy(
        src_ref=edge.at[0], dst_ref=edge.at[1], send_sem=edge_send.at[0], recv_sem=edge_recv.at[0],
        device_id=(me + 1, col), device_id_type=MESH,
    )

    @pl.when(me < span - 1)
    def _():
        to_right.start()

    @pl.when(me == 0)
    def _():
        edge[1] = jnp.zeros((seqs, width), F32)

    in_u.wait()

    def stage(b, last):
        at = pl.multiple_of(b * block, block)
        src = raw_t[:, pl.ds(pl.multiple_of(b * STEPS, STEPS), STEPS), :].reshape(block, width)
        now = dot(perm[...], src)
        before = jnp.concatenate([last, now[: block - seqs]], axis=0)
        before = before * wide_keep(at, block, width)
        joined[pl.ds(at, block), :width] = now.astype(BF)
        joined[pl.ds(at, block), width:] = before.astype(BF)
        src = raw_u[:, pl.ds(pl.multiple_of(b * STEPS, STEPS), STEPS), :].reshape(block, width)
        upt[pl.ds(at, block), :] = dot(perm[...], src).astype(BF)
        return now[block - seqs :]

    lax.fori_loop(0, blocks, stage, jnp.zeros((seqs, width), F32))

    @pl.when(me > 0)
    def _():
        to_right.wait_recv()

    @pl.when(me < span - 1)
    def _():
        to_right.wait_send()

    first = jnp.concatenate([edge[1], joined[:TWO, :width].astype(F32)[:seqs]], axis=0)
    joined[:TWO, width:] = (first * wide_keep(0, TWO, width)).astype(BF)

    def pass_a(c):
        at, cw = chunks[c]
        base = 3 * at
        size = 2 * block if blocks % 2 == 0 else block
        halves = range(cw // LANES)
        biases = [
            [
                jnp.broadcast_to(
                    bias[0:1, g * width + at + h * LANES : g * width + at + (h + 1) * LANES],
                    (TWO, LANES),
                )
                for h in halves
            ]
            for g in range(3)
        ]
        biases[1] = [0.5 * v for v in biases[1]]
        biases[2] = [0.5 * v for v in biases[2]]

        def body(i, carry):
            carry = [list(v) for v in carry]
            r0 = pl.multiple_of(i * size, size)
            gates[pl.ds(r0, size), base : base + 3 * cw] = dot(
                joined[pl.ds(r0, size), :], wv[:, base : base + 3 * cw]
            )
            for j in range(size // TWO):
                sl = pl.ds(r0 + j * TWO, TWO)
                k = keepb[sl, :]
                for h in halves:
                    zc, fc, oc = (base + g * cw + h * LANES for g in range(3))
                    z = jnp.tanh(gates[sl, zc : zc + LANES] + biases[0][h])
                    f = 0.5 * jnp.tanh(0.5 * gates[sl, fc : fc + LANES] + biases[1][h]) + 0.5
                    o = 0.5 * jnp.tanh(0.5 * gates[sl, oc : oc + LANES] + biases[2][h]) + 0.5
                    gates[sl, zc : zc + LANES] = z
                    gates[sl, fc : fc + LANES] = f
                    gates[sl, oc : oc + LANES] = o
                    g = upt[sl, at + h * LANES : at + (h + 1) * LANES].astype(F32)
                    eff = f * k
                    fresh = (1.0 - f) * z
                    src = g * o
                    gain, state, back = carry[h]
                    for m in (0, seqs):
                        gain = gain * eff[m : m + seqs]
                        state = state * eff[m : m + seqs] + fresh[m : m + seqs]
                        back = back + gain * src[m : m + seqs]
                    carry[h] = [gain, state, back]
            return tuple(tuple(v) for v in carry)

        zero = jnp.zeros((seqs, LANES), F32)
        one = jnp.ones((seqs, LANES), F32)
        done = lax.fori_loop(0, rows // size, body, tuple((one, zero, zero) for _ in halves))
        for h in halves:
            cols = slice(at + h * LANES, at + (h + 1) * LANES)
            for v in range(3):
                summ[me, v * seqs : (v + 1) * seqs, cols] = done[h][v]
        for k in range(1, span):
            exchange(c, k).start()

    def exchange(c, k):
        at, cw = chunks[c]
        here = summ.at[me, :, pl.ds(at, cw)]
        return pltpu.make_async_remote_copy(
            src_ref=here, dst_ref=here, send_sem=sum_send.at[c, k - 1],
            recv_sem=sum_recv.at[c, k - 1],
            device_id=(lax.rem(me + k, span), col), device_id_type=MESH,
        )

    def pass_b(c):
        at, cw = chunks[c]
        base = 3 * at
        halves = range(cw // LANES)
        for k in range(1, span):
            exchange(c, k).wait()
        enter, leave = [], []
        for h in halves:
            cols = slice(at + h * LANES, at + (h + 1) * LANES)
            state = jnp.zeros((seqs, LANES), F32)
            for s in range(span - 1):
                new = summ[s, seqs : 2 * seqs, cols] + summ[s, :seqs, cols] * state
                state = jnp.where(s < me, new, state)
            enter.append(state)
            back = jnp.zeros((seqs, LANES), F32)
            for s in range(span - 1, 0, -1):
                new = summ[s, 2 * seqs :, cols] + summ[s, :seqs, cols] * back
                back = jnp.where(s > me, new, back)
            leave.append(back)

        def forward(i, carry):
            cells, sums = list(carry[0]), list(carry[1])
            r0 = pl.multiple_of(i * block, block)
            for j in range(block // TWO):
                sl = pl.ds(r0 + j * TWO, TWO)
                k = keepb[sl, :]
                for h in halves:
                    zc, fc, oc = (base + g * cw + h * LANES for g in range(3))
                    z = gates[sl, zc : zc + LANES]
                    f = gates[sl, fc : fc + LANES]
                    o = gates[sl, oc : oc + LANES]
                    g = upt[sl, at + h * LANES : at + (h + 1) * LANES].astype(F32)
                    eff = f * k
                    rest = 1.0 - f
                    fresh = rest * z
                    c0 = eff[:seqs] * cells[h] + fresh[:seqs]
                    c1 = eff[seqs:] * c0 + fresh[seqs:]
                    cell = jnp.concatenate([c0, c1], axis=0)
                    prev = jnp.concatenate([cells[h], c0], axis=0)
                    cells[h] = c1
                    hb[j * TWO : (j + 1) * TWO, h * LANES : (h + 1) * LANES] = (o * cell).astype(BF)
                    src = g * o
                    go = src * cell * (1.0 - o)
                    gp[sl, oc : oc + LANES] = go.astype(BF)
                    sums[h] = sums[h] + go
                    gates[sl, zc : zc + LANES] = rest * (1.0 - z * z)
                    gates[sl, fc : fc + LANES] = eff
                    gates[sl, oc : oc + LANES] = src
                    qf[sl, h * LANES : (h + 1) * LANES] = (prev * k - z) * (f * rest)
            out = dot(pinv[...], hb[:, :cw]).astype(BF).reshape(seqs, STEPS, cw)
            raw_t[:, pl.ds(pl.multiple_of(i * STEPS, STEPS), STEPS), at : at + cw] = out
            return tuple(cells), tuple(sums)

        zero = jnp.zeros((TWO, LANES), F32)
        zeros = tuple(zero for _ in halves)
        _, sum_o = lax.fori_loop(0, blocks, forward, (tuple(enter), zeros))

        def backward(n, carry):
            heads, sums_z, sums_f = (list(v) for v in carry)
            r0 = pl.multiple_of((blocks - 1 - n) * block, block)
            for j in range(block // TWO - 1, -1, -1):
                sl = pl.ds(r0 + j * TWO, TWO)
                for h in halves:
                    zc, fc, oc = (base + g * cw + h * LANES for g in range(3))
                    eff = gates[sl, fc : fc + LANES]
                    src = gates[sl, oc : oc + LANES]
                    g1 = src[seqs:] + heads[h]
                    g0 = src[:seqs] + eff[seqs:] * g1
                    heads[h] = eff[:seqs] * g0
                    gc = jnp.concatenate([g0, g1], axis=0)
                    gz = gc * gates[sl, zc : zc + LANES]
                    gf = gc * qf[sl, h * LANES : (h + 1) * LANES]
                    gp[sl, zc : zc + LANES] = gz.astype(BF)
                    gp[sl, fc : fc + LANES] = gf.astype(BF)
                    sums_z[h] = sums_z[h] + gz
                    sums_f[h] = sums_f[h] + gf
            return tuple(heads), tuple(sums_z), tuple(sums_f)

        _, sum_z, sum_f = lax.fori_loop(0, blocks, backward, (tuple(leave), zeros, zeros))
        for h in halves:
            for g, total in enumerate((sum_z, sum_f, sum_o)):
                lane = g * width + at + h * LANES
                gb[0:1, lane : lane + LANES] = jnp.sum(total[h], axis=0, keepdims=True)

    def gw_copies(c):
        at, cw = chunks[c]
        return [
            pltpu.make_async_copy(
                gwv.at[c % 2, :, pl.ds(g * cw, cw)],
                gw.at[:, pl.ds(g * width + at, cw)],
                gw_sem.at[c, g],
            )
            for g in range(3)
        ]

    def pass_c(c):
        at, cw = chunks[c]
        base = 3 * at
        tile = 2 * LANES
        if c >= 2:
            for copy in gw_copies(c - 2):
                copy.wait()

        def body(i, carry):
            r0 = pl.multiple_of(i * tile, tile)
            gwv[c % 2, pl.ds(r0, tile), : 3 * cw] = lax.dot_general(
                joined[:, pl.ds(r0, tile)], gp[:, base : base + 3 * cw],
                (((0,), (0,)), ((), ())), preferred_element_type=F32,
            )
            return carry

        lax.fori_loop(0, 2 * width // tile, body, 0)
        for copy in gw_copies(c):
            copy.start()

    for c in range(len(chunks)):
        for g in range(3):
            w_copies[3 * c + g].wait()
        pass_a(c)
    for c in range(len(chunks)):
        pass_b(c)
        pass_c(c)
    out_h = pltpu.make_async_copy(raw_t, hid, out_sem.at[0])
    out_h.start()

    to_left = pltpu.make_async_remote_copy(
        src_ref=edge.at[2], dst_ref=edge.at[3], send_sem=edge_send.at[1], recv_sem=edge_recv.at[1],
        device_id=(me - 1, col), device_id_type=MESH,
    )

    @pl.when(me == span - 1)
    def _():
        edge[3] = jnp.zeros((seqs, width), F32)

    def put(b):
        at = pl.multiple_of(b * block, block)
        out = dot(pinv[...], gates[pl.ds(at, block), :width].astype(BF)).astype(BF)
        raw_u[:, pl.ds(pl.multiple_of(b * STEPS, STEPS), STEPS), :] = out.reshape(
            seqs, STEPS, width
        )

    def inputs(i, pend):
        r0 = pl.multiple_of(i * block, block)
        both = lax.dot_general(
            gp[pl.ds(r0, block), :], wv[...], (((1,), (1,)), ((), ())), preferred_element_type=F32
        )
        own = both[:, :width]
        late = both[:, width:] * wide_keep(r0, block, width)
        gates[pl.ds(r0, block - seqs), :width] = own[: block - seqs] + late[seqs:]

        @pl.when(i == 0)
        def _():
            edge[2] = late[:seqs]

            @pl.when(me > 0)
            def _():
                to_left.start()

        @pl.when(i > 0)
        def _():
            gates[pl.ds(pl.multiple_of(r0 - seqs, seqs), seqs), :width] = pend + late[:seqs]
            put(i - 1)

        return own[block - seqs :]

    pend = lax.fori_loop(0, blocks, inputs, jnp.zeros((seqs, width), F32))

    @pl.when(me < span - 1)
    def _():
        to_left.wait_recv()

    @pl.when(me > 0)
    def _():
        to_left.wait_send()

    gates[rows - seqs :, :width] = pend + edge[3]
    put(blocks - 1)
    out_t = pltpu.make_async_copy(raw_u, gtok, out_sem.at[1])
    out_t.start()
    for c in range(max(0, len(chunks) - 2), len(chunks)):
        for copy in gw_copies(c):
            copy.wait()
    out_h.wait()
    out_t.wait()


def per_device(tokens, weights, bias, resets, upstream):
    seqs, steps, width = tokens.shape
    rows = seqs * steps
    span = lax.axis_size("seq")
    chunks = cut_chunks(width)
    block = seqs * STEPS
    full = lax.all_gather(weights, ("seq", "dp"), axis=0, tiled=True)
    any_spec = pl.BlockSpec(memory_space=pl.ANY)
    vmem = pl.BlockSpec(memory_space=pltpu.VMEM)
    hid, gtok, gw, gb = pl.pallas_call(
        functools.partial(layer_kernel, span, chunks),
        out_shape=(
            jax.ShapeDtypeStruct(tokens.shape, BF),
            jax.ShapeDtypeStruct(tokens.shape, BF),
            jax.ShapeDtypeStruct((2 * width, 3 * width), F32),
            jax.ShapeDtypeStruct((1, 3 * width), F32),
        ),
        in_specs=[any_spec, any_spec, vmem, vmem, any_spec],
        out_specs=(any_spec, any_spec, any_spec, vmem),
        scratch_shapes=[
            pltpu.VMEM(tokens.shape, BF),
            pltpu.VMEM(tokens.shape, BF),
            pltpu.VMEM((rows, 2 * width), BF),
            pltpu.VMEM((rows, width), BF),
            pltpu.VMEM((2 * width, 3 * width), BF),
            pltpu.VMEM((rows, 3 * width), F32),
            pltpu.VMEM((rows, 2 * LANES), F32),
            pltpu.VMEM((rows, 3 * width), BF),
            pltpu.VMEM((rows, LANES), F32),
            pltpu.VMEM((block, block), BF),
            pltpu.VMEM((block, block), BF),
            pltpu.VMEM((block, 2 * LANES), BF),
            pltpu.VMEM((2, 2 * width, 6 * LANES), F32),
            pltpu.VMEM((span, 3 * seqs, width), F32),
            pltpu.VMEM((4, seqs, width), F32),
            pltpu.SemaphoreType.DMA((2,)),
            pltpu.SemaphoreType.DMA((len(chunks), 3)),
            pltpu.SemaphoreType.DMA((2,)),
            pltpu.SemaphoreType.DMA((len(chunks), 3)),
            pltpu.SemaphoreType.DMA((len(chunks), span - 1)),
            pltpu.SemaphoreType.DMA((len(chunks), span - 1)),
            pltpu.SemaphoreType.DMA((2,)),
            pltpu.SemaphoreType.DMA((2,)),
        ],
        compiler_params=pltpu.CompilerParams(
            collective_id=0, has_side_effects=True, vmem_limit_bytes=60 << 20
        ),
        name="layer",
    )(tokens, full, bias.reshape(1, -1), resets, upstream)
    gw = lax.psum_scatter(gw, ("seq", "dp"), scatter_dimension=0, tiled=True)
    gb = lax.psum(gb[0], ("seq", "dp"))
    return hid, gtok, gw, gb


def solution(mesh):
    spread = P("dp", "seq", None)
    rows = P(("seq", "dp"), None)
    return jax.shard_map(
        per_device,
        mesh=mesh,
        in_specs=(spread, rows, P(), P("dp", "seq"), spread),
        out_specs=(spread, spread, rows, P()),
        check_vma=False,
    )
```

```python
import functools

import jax
import jax.numpy as jnp
from jax import lax
from jax.experimental import pallas as pl
from jax.experimental.pallas import tpu as pltpu
from jax.sharding import PartitionSpec as P

MESH = pl.DeviceIdType.MESH
BF = jnp.bfloat16
F32 = jnp.float32
LANES = 128
TRIO = 3 * LANES
STEPS = 32
TWO = 16


def cut_chunks(width):
    tiles = width // LANES
    chunks, at = [], 0
    if tiles % 2:
        chunks.append((0, LANES))
        at = LANES
    while at < width:
        chunks.append((at, 2 * LANES))
        at += 2 * LANES
    return chunks


def dot(a, b):
    return jnp.dot(a, b, preferred_element_type=F32)


def dot_rows(a, b):
    return lax.dot_general(a, b, (((0,), (0,)), ((), ())), preferred_element_type=F32)


def dot_columns(a, b):
    return lax.dot_general(a, b, (((1,), (1,)), ((), ())), preferred_element_type=F32)


def layer_kernel(
    span, peers, fused, chunks,
    tok, wts, bias, resets, up,
    hid, gtok, gw, gb,
    raw_t, raw_u, joined, upt, wv, gates, qf, gp, keepb, perm, pinv, hb, cbuf, summ, edge,
    in_sem, w_sem, out_sem, sum_send, sum_recv, edge_send, edge_recv,
    *links,
):
    seqs, steps, width = tok.shape
    rows = seqs * steps
    block = seqs * STEPS
    blocks = steps // STEPS
    depth = 2 * width
    half_rows = depth // 2
    n_chunks = len(chunks)
    me = lax.axis_index("seq")
    col = lax.axis_index("dp")
    core = col & 1
    place = col >> 1
    plane = peers // 2
    slab = depth // (span * plane)
    shard = slab // 2
    over = -(-shard // 16) * 16
    partner = (me, col ^ 1)
    if fused:
        (
            own16, pair, sb1, rb1, rb2, own2, rb3, fin, fin_rx, gbs,
            a0_sem, a1_send, a1_recv, a2_send, a2_recv, a3_sem,
            r1_send, r1_recv, r2_send, r2_recv, r3_send, r3_recv, r4_sem, gb_send, gb_recv,
        ) = links

    def remote(src, dst, send, recv, to):
        return pltpu.make_async_remote_copy(
            src_ref=src, dst_ref=dst, send_sem=send, recv_sem=recv,
            device_id=to, device_id_type=MESH,
        )

    def mult(v, m):
        return pl.multiple_of(v, m)

    in_t = pltpu.make_async_copy(tok, raw_t, in_sem.at[0])
    in_u = pltpu.make_async_copy(up, raw_u, in_sem.at[1])
    if fused:
        in_w = pltpu.make_async_copy(wts, own16, w_sem.at[0])
        in_w.start()
    in_t.start()
    in_u.start()

    barrier = pltpu.get_barrier_semaphore()
    friends = [(lax.rem(me + k, span), col) for k in range(1, span)]
    if fused:
        friends += [(me, col ^ (2 * y)) for y in range(1, plane)] + [partner]
    for friend in friends:
        pl.semaphore_signal(barrier, inc=1, device_id=friend, device_id_type=MESH)
    pl.semaphore_wait(barrier, len(friends))

    def carried(c, who):
        at, cw = chunks[c]
        if cw == LANES:
            return over, mult((slab - over) * who, 16), 3 * at
        return slab, 0, mult(3 * at + TRIO * who, LANES)

    def part(c, who, planes, places):
        count, r0, c0 = carried(c, who)
        return wv.at[planes, places, pl.ds(r0, count), pl.ds(c0, TRIO)]

    def a1(c, x):
        here = part(c, core, me, place)
        return remote(here, here, a1_send.at[c, x - 1], a1_recv.at[c, x - 1], (me ^ x, col))

    def a2(c, y):
        here = part(c, core, slice(None), place)
        return remote(here, here, a2_send.at[c, y - 1], a2_recv.at[c, y - 1], (me, col ^ (2 * y)))

    def a3(c):
        if chunks[c][1] == LANES:
            here = wv.at[
                :, :, pl.ds(mult(over * core, 16), slab - over), pl.ds(3 * chunks[c][0], TRIO)
            ]
        else:
            here = part(c, core, slice(None), slice(None))
        return remote(here, here, a3_sem.at[c, 0], a3_sem.at[c, 1], partner)

    def w_copies(c):
        at, cw = chunks[c]
        return [
            pltpu.make_async_copy(
                wts.at[:, pl.ds(g * width + at + h * LANES, LANES)],
                wv.at[:, pl.ds(3 * at + h * TRIO + g * LANES, LANES)],
                w_sem.at[c, g, h],
            )
            for g in range(3)
            for h in range(cw // LANES)
        ]

    if fused:
        in_w.wait()
        pair[core] = own16[...].astype(F32)
        a0 = remote(pair.at[core], pair.at[core], a0_sem.at[0], a0_sem.at[1], partner)
        a0.start()
    else:
        for c in range(n_chunks):
            for copy in w_copies(c):
                copy.start()

    r = lax.broadcasted_iota(jnp.int32, (block, block), 0)
    q = lax.broadcasted_iota(jnp.int32, (block, block), 1)
    perm[...] = (((q & 31) == (r >> 3)) & ((q >> 5) == (r & 7))).astype(F32).astype(BF)
    pinv[...] = (((r & 31) == (q >> 3)) & ((r >> 5) == (q & 7))).astype(F32).astype(BF)

    if fused:
        a0.wait_recv()
        for c, (at, cw) in enumerate(chunks):
            count, top, left = carried(c, core)
            for g in range(3):
                lane = g * width + at + (0 if cw == LANES else core * LANES)
                lanes = pl.ds(mult(lane, LANES), LANES)
                both = jnp.concatenate([pair[0, :, lanes], pair[1, :, lanes]], axis=0)
                if count < slab:
                    both = jnp.where(core == 0, both[:count], both[slab - count :])
                to = pl.ds(mult(left + g * LANES, LANES), LANES)
                wv[me, place, pl.ds(top, count), to] = both.astype(BF)
            for x in range(1, span):
                a1(c, x).start()

    keep = 1.0 - resets[...].astype(F32)
    tiled = jnp.broadcast_to(keep[None], (STEPS, seqs, steps)).reshape(block, steps)
    row_t = lax.broadcasted_iota(jnp.int32, (block, steps), 0) >> 3
    lane_t = lax.broadcasted_iota(jnp.int32, (block, steps), 1)
    ones = jnp.ones((steps, LANES), BF)
    for b in range(blocks):
        picked = jnp.where(lane_t == row_t + b * STEPS, tiled, 0.0).astype(BF)
        keepb[b * block : (b + 1) * block, :] = dot(picked, ones)

    def wide_keep(at, count, lanes):
        k = keepb[pl.ds(at, count), :]
        return jnp.concatenate([k] * (lanes // LANES), axis=1)

    in_t.wait()
    last_rows = raw_t[:, steps - STEPS :, :].reshape(block, width)
    edge[0] = dot(perm[block - TWO :, :], last_rows)[TWO - seqs :]
    to_right = remote(edge.at[0], edge.at[1], edge_send.at[0], edge_recv.at[0], (me + 1, col))

    @pl.when(me < span - 1)
    def _():
        to_right.start()

    @pl.when(me == 0)
    def _():
        edge[1] = jnp.zeros((seqs, width), F32)

    in_u.wait()
    if fused:
        for x in range(1, span):
            a1(0, x).wait_recv()
        for y in range(1, plane):
            a2(0, y).start()

    def stage(b, last):
        at = mult(b * block, block)
        src = raw_t[:, pl.ds(mult(b * STEPS, STEPS), STEPS), :].reshape(block, width)
        now = dot(perm[...], src)
        before = jnp.concatenate([last, now[: block - seqs]], axis=0)
        before = before * wide_keep(at, block, width)
        joined[pl.ds(at, block), :width] = now.astype(BF)
        joined[pl.ds(at, block), width:] = before.astype(BF)
        src = raw_u[:, pl.ds(mult(b * STEPS, STEPS), STEPS), :].reshape(block, width)
        upt[pl.ds(at, block), :] = dot(perm[...], src).astype(BF)
        return now[block - seqs :]

    lax.fori_loop(0, blocks, stage, jnp.zeros((seqs, width), F32))

    @pl.when(me > 0)
    def _():
        to_right.wait_recv()

    @pl.when(me < span - 1)
    def _():
        to_right.wait_send()

    first = jnp.concatenate([edge[1], joined[:TWO, :width].astype(F32)[:seqs]], axis=0)
    joined[:TWO, width:] = (first * wide_keep(0, TWO, width)).astype(BF)

    def weights_of(base, count):
        if fused:
            return wv[:, :, :, base : base + count].reshape(depth, count)
        return wv[:, base : base + count]

    def pass_a(c):
        at, cw = chunks[c]
        base = 3 * at
        size = 2 * block if blocks % 2 == 0 else block
        halves = range(cw // LANES)

        def bias_rows(g, h):
            lane = g * width + at + h * LANES
            return jnp.broadcast_to(bias[0:1, lane : lane + LANES], (TWO, LANES))

        bias_z = [bias_rows(0, h) for h in halves]
        bias_f = [0.5 * bias_rows(1, h) for h in halves]
        bias_o = [0.5 * bias_rows(2, h) for h in halves]

        def body(i, carry):
            carry = [list(v) for v in carry]
            r0 = mult(i * size, size)
            gates[pl.ds(r0, size), base : base + 3 * cw] = dot(
                joined[pl.ds(r0, size), :], weights_of(base, 3 * cw)
            )
            for j in range(size // TWO):
                sl = pl.ds(r0 + j * TWO, TWO)
                k = keepb[sl, :]
                for h in halves:
                    zc, fc, oc = (base + h * TRIO + g * LANES for g in range(3))
                    z = jnp.tanh(gates[sl, zc : zc + LANES] + bias_z[h])
                    f = 0.5 * jnp.tanh(0.5 * gates[sl, fc : fc + LANES] + bias_f[h]) + 0.5
                    o = 0.5 * jnp.tanh(0.5 * gates[sl, oc : oc + LANES] + bias_o[h]) + 0.5
                    gates[sl, zc : zc + LANES] = z
                    gates[sl, fc : fc + LANES] = f
                    gates[sl, oc : oc + LANES] = o
                    g = upt[sl, at + h * LANES : at + (h + 1) * LANES].astype(F32)
                    eff = f * k
                    fresh = (1.0 - f) * z
                    src = g * o
                    gain, state, back = carry[h]
                    for m in (0, seqs):
                        gain = gain * eff[m : m + seqs]
                        state = state * eff[m : m + seqs] + fresh[m : m + seqs]
                        back = back + gain * src[m : m + seqs]
                    carry[h] = [gain, state, back]
            return tuple(tuple(v) for v in carry)

        zero = jnp.zeros((seqs, LANES), F32)
        one = jnp.ones((seqs, LANES), F32)
        done = lax.fori_loop(0, rows // size, body, tuple((one, zero, zero) for _ in halves))
        for h in halves:
            cols = slice(at + h * LANES, at + (h + 1) * LANES)
            for v in range(3):
                summ[me, v * seqs : (v + 1) * seqs, cols] = done[h][v]
        for k in range(1, span):
            exchange(c, k).start()

    def exchange(c, k):
        at, cw = chunks[c]
        here = summ.at[me, :, pl.ds(at, cw)]
        return remote(
            here, here, sum_send.at[c, k - 1], sum_recv.at[c, k - 1], (lax.rem(me + k, span), col)
        )

    def pass_b(c):
        at, cw = chunks[c]
        base = 3 * at
        halves = range(cw // LANES)
        for k in range(1, span):
            exchange(c, k).wait()
        enter, leave = [], []
        for h in halves:
            cols = slice(at + h * LANES, at + (h + 1) * LANES)
            state = jnp.zeros((seqs, LANES), F32)
            for s in range(span - 1):
                new = summ[s, seqs : 2 * seqs, cols] + summ[s, :seqs, cols] * state
                state = jnp.where(s < me, new, state)
            enter.append(state)
            back = jnp.zeros((seqs, LANES), F32)
            for s in range(span - 1, 0, -1):
                new = summ[s, 2 * seqs :, cols] + summ[s, :seqs, cols] * back
                back = jnp.where(s > me, new, back)
            leave.append(back)

        def forward(i, carry):
            cells, sums = list(carry[0]), list(carry[1])
            r0 = mult(i * block, block)
            for j in range(block // TWO):
                sl = pl.ds(r0 + j * TWO, TWO)
                k = keepb[sl, :]
                for h in halves:
                    zc, fc, oc = (base + h * TRIO + g * LANES for g in range(3))
                    z = gates[sl, zc : zc + LANES]
                    f = gates[sl, fc : fc + LANES]
                    o = gates[sl, oc : oc + LANES]
                    g = upt[sl, at + h * LANES : at + (h + 1) * LANES].astype(F32)
                    eff = f * k
                    rest = 1.0 - f
                    fresh = rest * z
                    c0 = eff[:seqs] * cells[h] + fresh[:seqs]
                    c1 = eff[seqs:] * c0 + fresh[seqs:]
                    cell = jnp.concatenate([c0, c1], axis=0)
                    prev = jnp.concatenate([cells[h], c0], axis=0)
                    cells[h] = c1
                    hb[j * TWO : (j + 1) * TWO, h * LANES : (h + 1) * LANES] = (o * cell).astype(BF)
                    src = g * o
                    go = src * cell * (1.0 - o)
                    gp[sl, oc : oc + LANES] = go.astype(BF)
                    sums[h] = sums[h] + go
                    gates[sl, zc : zc + LANES] = rest * (1.0 - z * z)
                    gates[sl, fc : fc + LANES] = eff
                    gates[sl, oc : oc + LANES] = src
                    qf[sl, h * LANES : (h + 1) * LANES] = (prev * k - z) * (f * rest)
            out = dot(pinv[...], hb[:, :cw]).astype(BF).reshape(seqs, STEPS, cw)
            raw_t[:, pl.ds(mult(i * STEPS, STEPS), STEPS), at : at + cw] = out
            return tuple(cells), tuple(sums)

        zero = jnp.zeros((TWO, LANES), F32)
        zeros = tuple(zero for _ in halves)
        _, sum_o = lax.fori_loop(0, blocks, forward, (tuple(enter), zeros))

        def backward(n, carry):
            heads, sums_z, sums_f = (list(v) for v in carry)
            r0 = mult((blocks - 1 - n) * block, block)
            for j in range(block // TWO - 1, -1, -1):
                sl = pl.ds(r0 + j * TWO, TWO)
                for h in halves:
                    zc, fc, oc = (base + h * TRIO + g * LANES for g in range(3))
                    eff = gates[sl, fc : fc + LANES]
                    src = gates[sl, oc : oc + LANES]
                    g1 = src[seqs:] + heads[h]
                    g0 = src[:seqs] + eff[seqs:] * g1
                    heads[h] = eff[:seqs] * g0
                    gc = jnp.concatenate([g0, g1], axis=0)
                    gz = gc * gates[sl, zc : zc + LANES]
                    gf = gc * qf[sl, h * LANES : (h + 1) * LANES]
                    gp[sl, zc : zc + LANES] = gz.astype(BF)
                    gp[sl, fc : fc + LANES] = gf.astype(BF)
                    sums_z[h] = sums_z[h] + gz
                    sums_f[h] = sums_f[h] + gf
            return tuple(heads), tuple(sums_z), tuple(sums_f)

        _, sum_z, sum_f = lax.fori_loop(0, blocks, backward, (tuple(leave), zeros, zeros))
        for h in halves:
            for g, total in enumerate((sum_z, sum_f, sum_o)):
                line = jnp.sum(total[h], axis=0, keepdims=True)
                if fused:
                    tile = g * (width // LANES) + at // LANES + h
                    gbs[0, tile : tile + 1, :] = line
                else:
                    lane = g * width + at + h * LANES
                    gb[0:1, lane : lane + LANES] = line

    def gw_copies(c, turn):
        at, cw = chunks[c]
        return [
            pltpu.make_async_copy(
                cbuf.at[turn, :, pl.ds(h * TRIO + g * LANES, LANES)],
                gw.at[pl.ds(turn * half_rows, half_rows), pl.ds(g * width + at + h * LANES, LANES)],
                w_sem.at[c, g, h],
            )
            for g in range(3)
            for h in range(cw // LANES)
        ]

    def pass_c(c, turn):
        at, cw = chunks[c]
        base = 3 * at
        if fused:
            r0 = mult(((me // (span // 2)) ^ 1 ^ turn) * half_rows, LANES)
            result = dot_rows(joined[:, pl.ds(r0, half_rows)], gp[:, base : base + 3 * cw])
            cbuf[turn, :, :, : 3 * cw] = result.reshape(-1, slab, 3 * cw)
            r1(c, turn)
        else:
            if c:
                for copy in gw_copies(c - 1, turn):
                    copy.wait()
            cbuf[turn, :, : 3 * cw] = dot_rows(
                joined[:, turn * half_rows : (turn + 1) * half_rows], gp[:, base : base + 3 * cw]
            )
            for copy in gw_copies(c, turn):
                copy.start()

    def own_part(c, who):
        count, r0, _ = carried(c, who)
        c0 = 0 if chunks[c][1] == LANES else mult(TRIO * who, LANES)
        return pl.ds(r0, count), pl.ds(c0, TRIO)

    def part_rows(c):
        return pl.ds(0, carried(c, 0)[0])

    def orders(turn):
        half = span // 2
        return list(range(half, span)) if turn == 0 else list(range(half - 1, -1, -1))

    def r1_copy(c, turn):
        k = part_rows(c)
        return remote(
            sb1.at[turn, :, k], rb1.at[c, turn, :, k], r1_send.at[c, turn], r1_recv.at[c, turn],
            partner,
        )

    def r1(c, turn):
        if c:
            r1_copy(c - 1, turn).wait_send()
        rs, cs = own_part(c, 1 - core)
        sb1[turn, :, part_rows(c), :] = cbuf[turn, :, rs, cs].astype(BF)
        r1_copy(c, turn).start()

    def r2_copy(c, turn, n, y):
        k = part_rows(c)
        x = orders(turn)[n]
        index = ((me ^ x) % (span // 2)) * plane + (place ^ y)
        return remote(
            rb1.at[c, turn, index, k], rb2.at[c, turn, n, y - 1, k],
            r2_send.at[c, turn, n, y - 1], r2_recv.at[c, turn, n, y - 1], (me, col ^ (2 * y)),
        )

    def r2(c, turn):
        r1_copy(c, turn).wait_recv()
        k = part_rows(c)
        rs, cs = own_part(c, core)
        for n, x in enumerate(orders(turn)):
            for y in range(plane - 1, -1, -1):
                index = ((me ^ x) % (span // 2)) * plane + (place ^ y)
                total = cbuf[turn, index, rs, cs] + rb1[c, turn, index, k].astype(F32)
                if y:
                    rb1[c, turn, index, k] = total.astype(BF)
                    r2_copy(c, turn, n, y).start()
                else:
                    own2[c, turn, n, k] = total

    def r3_copy(c, turn, n):
        k = part_rows(c)
        x = orders(turn)[n]
        return remote(
            rb2.at[c, turn, n, 0, k], rb3.at[c, x - 1, k], r3_send.at[c, x - 1],
            r3_recv.at[c, x - 1], (me ^ x, col),
        )

    def r3(c, turn):
        k = part_rows(c)
        for n, x in enumerate(orders(turn)):
            total = own2[c, turn, n, k]
            for y in range(1, plane):
                r2_copy(c, turn, n, y).wait_recv()
                total = total + rb2[c, turn, n, y - 1, k].astype(F32)
            if x:
                rb2[c, turn, n, 0, k] = total.astype(BF)
                r3_copy(c, turn, n).start()
            else:
                own2[c, turn, n, k] = total

    def r4_copy(c):
        return remote(
            fin.at[c, pl.ds(mult(shard * (1 - core), 8), shard)], fin_rx.at[c],
            r4_sem.at[c, 0], r4_sem.at[c, 1], partner,
        )

    def put_gw(c, tile, value):
        at, cw = chunks[c]
        for g in range(3):
            lane = mult(g * width + at + tile * LANES, LANES)
            gw[:, pl.ds(lane, LANES)] = value[:, g * LANES : (g + 1) * LANES]

    def each_seq_peer(c):
        return [(turn, n, x) for turn in (0, 1) for n, x in enumerate(orders(turn)) if x]

    def r4(c):
        k = part_rows(c)
        total = own2[c, 1, span // 2 - 1, k]
        for turn, n, x in each_seq_peer(c):
            r3_copy(c, turn, n).wait_recv()
            total = total + rb3[c, x - 1, k].astype(F32)
        fin[c, k] = total
        if chunks[c][1] == LANES:
            off = (slab - over) * core
            put_gw(c, 0, fin[c, pl.ds(mult(shard * core - off, 8), shard)])
        else:
            r4_copy(c).start()
            put_gw(c, core, fin[c, pl.ds(mult(shard * core, 8), shard)])

    def r5(c):
        if chunks[c][1] != LANES:
            r4_copy(c).wait_recv()
            put_gw(c, 1 - core, fin_rx[c])

    def gb_stage(stage):
        if stage == 0:
            peer = [((me ^ x, col), x - 1) for x in range(1, span)]
        elif stage == 1:
            peer = [((me, col ^ (2 * y)), span - 1 + y - 1) for y in range(1, plane)]
        else:
            peer = [(partner, span + plane - 2)]
        src = gbs.at[stage]
        return [(remote(src, gbs.at[4 + k], gb_send.at[k], gb_recv.at[k], to), k) for to, k in peer]

    def gb_go(stage):
        for copy, _ in gb_stage(stage):
            copy.start()

    def gb_sum(stage):
        total = gbs[stage]
        for copy, k in gb_stage(stage):
            copy.wait_recv()
            total = total + gbs[4 + k]
        gbs[stage + 1] = total

    def gathered(c):
        if not fused:
            for copy in w_copies(c):
                copy.wait()
            return
        for y in range(1, plane):
            a2(c, y).wait_recv()
        a3(c).start()
        if c + 1 < n_chunks:
            for x in range(1, span):
                a1(c + 1, x).wait_recv()
            for y in range(1, plane):
                a2(c + 1, y).start()
        a3(c).wait_recv()

    for c in range(n_chunks):
        gathered(c)
        pass_a(c)
    if fused:
        gbs[0] = jnp.zeros(gbs.shape[1:], F32)
    for c in range(n_chunks):
        pass_b(c)
        if fused and c:
            r2(c - 1, 1)
        if fused and c == n_chunks - 1:
            gb_go(0)
        pass_c(c, 0)
        if fused and c:
            r3(c - 1, 0)
        pass_c(c, 1)
        if fused:
            if c:
                r3(c - 1, 1)
            r2(c, 0)
            if c > 1:
                r4(c - 2)
    out_h = pltpu.make_async_copy(raw_t, hid, out_sem.at[0])
    out_h.start()

    to_left = remote(edge.at[2], edge.at[3], edge_send.at[1], edge_recv.at[1], (me - 1, col))

    @pl.when(me == span - 1)
    def _():
        edge[3] = jnp.zeros((seqs, width), F32)

    def put(b):
        at = mult(b * block, block)
        out = dot(pinv[...], gates[pl.ds(at, block), :width].astype(BF)).astype(BF)
        raw_u[:, pl.ds(mult(b * STEPS, STEPS), STEPS), :] = out.reshape(seqs, STEPS, width)

    def late_links(i):
        last = n_chunks - 1
        plan = {
            1: [lambda: r2(last, 1), lambda: r5(max(0, last - 2)), lambda: gb_sum(0), lambda: gb_go(1)],
            3: [lambda: r3(last, 0), lambda: r4(last - 1), lambda: gb_sum(1), lambda: gb_go(2)],
            5: [lambda: r3(last, 1), lambda: r5(last - 1), lambda: gb_sum(2)],
        }
        for when, todo in plan.items():

            @pl.when(i == when)
            def _(todo=todo):
                for step in todo:
                    step()

    def inputs(i, pend):
        r0 = mult(i * block, block)
        both = dot_columns(gp[pl.ds(r0, block), :], weights_of(0, 3 * width))
        own = both[:, :width]
        late = both[:, width:] * wide_keep(r0, block, width)
        gates[pl.ds(r0, block - seqs), :width] = own[: block - seqs] + late[seqs:]

        @pl.when(i == 0)
        def _():
            edge[2] = late[:seqs]

            @pl.when(me > 0)
            def _():
                to_left.start()

        @pl.when(i > 0)
        def _():
            gates[pl.ds(mult(r0 - seqs, seqs), seqs), :width] = pend + late[:seqs]
            put(i - 1)

        if fused:
            late_links(i)
        return own[block - seqs :]

    pend = lax.fori_loop(0, blocks, inputs, jnp.zeros((seqs, width), F32))

    @pl.when(me < span - 1)
    def _():
        to_left.wait_recv()

    @pl.when(me > 0)
    def _():
        to_left.wait_send()

    gates[rows - seqs :, :width] = pend + edge[3]
    put(blocks - 1)
    out_t = pltpu.make_async_copy(raw_u, gtok, out_sem.at[1])
    out_t.start()
    if not fused:
        for turn in (0, 1):
            for copy in gw_copies(n_chunks - 1, turn):
                copy.wait()
    else:
        last = n_chunks - 1
        r4(last)
        for g in range(3 * width // LANES):
            gb[0:1, g * LANES : (g + 1) * LANES] = gbs[3, g : g + 1, :]
        r5(last)
        a0.wait_send()
        for c in range(n_chunks):
            a3(c).wait_send()
            for x in range(1, span):
                a1(c, x).wait_send()
            for y in range(1, plane):
                a2(c, y).wait_send()
            for turn in (0, 1):
                for n, x in enumerate(orders(turn)):
                    for y in range(1, plane):
                        r2_copy(c, turn, n, y).wait_send()
                    if x:
                        r3_copy(c, turn, n).wait_send()
            if chunks[c][1] != LANES:
                r4_copy(c).wait_send()
        for turn in (0, 1):
            r1_copy(last, turn).wait_send()
        for stage_index in range(3):
            for copy, _ in gb_stage(stage_index):
                copy.wait_send()
    out_h.wait()
    out_t.wait()


def per_device(tokens, weights, bias, resets, upstream):
    seqs, steps, width = tokens.shape
    rows = seqs * steps
    span, peers = lax.axis_size("seq"), lax.axis_size("dp")
    chunks = cut_chunks(width)
    n_chunks = len(chunks)
    block = seqs * STEPS
    depth = 2 * width
    shard = weights.shape[0]
    slab = 2 * shard
    plane = peers // 2
    half = span // 2
    fused = shard % 8 == 0 and slab % 16 == 0 and n_chunks >= 3 and steps // STEPS >= 6
    any_spec = pl.BlockSpec(memory_space=pl.ANY)
    vmem = pl.BlockSpec(memory_space=pltpu.VMEM)
    dma = pltpu.SemaphoreType.DMA
    if fused:
        w_shape, c_shape, w_sems = (span, plane, slab, 3 * width), (2, half * plane, slab, 2 * TRIO), (1,)
        gw_shape, gw_spec = (shard, 3 * width), vmem
        links = [
            pltpu.VMEM((shard, 3 * width), BF),
            pltpu.VMEM((2, shard, 3 * width), F32),
            pltpu.VMEM((2, half * plane, slab, TRIO), BF),
            pltpu.VMEM((n_chunks, 2, half * plane, slab, TRIO), BF),
            pltpu.VMEM((n_chunks, 2, half, plane - 1, slab, TRIO), BF),
            pltpu.VMEM((n_chunks, 2, half, slab, TRIO), F32),
            pltpu.VMEM((n_chunks, span - 1, slab, TRIO), BF),
            pltpu.VMEM((n_chunks, slab, TRIO), F32),
            pltpu.VMEM((n_chunks, shard, TRIO), F32),
            pltpu.VMEM((4 + span + plane - 1, 16, LANES), F32),
            dma((2,)),
            dma((n_chunks, span - 1)),
            dma((n_chunks, span - 1)),
            dma((n_chunks, plane - 1)),
            dma((n_chunks, plane - 1)),
            dma((n_chunks, 2)),
            dma((n_chunks, 2)),
            dma((n_chunks, 2)),
            dma((n_chunks, 2, half, plane - 1)),
            dma((n_chunks, 2, half, plane - 1)),
            dma((n_chunks, span - 1)),
            dma((n_chunks, span - 1)),
            dma((n_chunks, 2)),
            dma((span + plane - 1,)),
            dma((span + plane - 1,)),
        ]
    else:
        weights = lax.all_gather(weights, ("seq", "dp"), axis=0, tiled=True)
        w_shape, c_shape, w_sems = (depth, 3 * width), (2, depth // 2, 2 * TRIO), (n_chunks, 3, 2)
        gw_shape, gw_spec = (depth, 3 * width), any_spec
        links = []
    hid, gtok, gw, gb = pl.pallas_call(
        functools.partial(layer_kernel, span, peers, fused, chunks),
        out_shape=(
            jax.ShapeDtypeStruct(tokens.shape, BF),
            jax.ShapeDtypeStruct(tokens.shape, BF),
            jax.ShapeDtypeStruct(gw_shape, F32),
            jax.ShapeDtypeStruct((1, 3 * width), F32),
        ),
        in_specs=[any_spec, any_spec, vmem, vmem, any_spec],
        out_specs=(any_spec, any_spec, gw_spec, vmem),
        scratch_shapes=[
            pltpu.VMEM(tokens.shape, BF),
            pltpu.VMEM(tokens.shape, BF),
            pltpu.VMEM((rows, depth), BF),
            pltpu.VMEM((rows, width), BF),
            pltpu.VMEM(w_shape, BF),
            pltpu.VMEM((rows, 3 * width), F32),
            pltpu.VMEM((rows, 2 * LANES), F32),
            pltpu.VMEM((rows, 3 * width), BF),
            pltpu.VMEM((rows, LANES), F32),
            pltpu.VMEM((block, block), BF),
            pltpu.VMEM((block, block), BF),
            pltpu.VMEM((block, 2 * LANES), BF),
            pltpu.VMEM(c_shape, F32),
            pltpu.VMEM((span, 3 * seqs, width), F32),
            pltpu.VMEM((4, seqs, width), F32),
            dma((2,)),
            dma(w_sems),
            dma((2,)),
            dma((n_chunks, span - 1)),
            dma((n_chunks, span - 1)),
            dma((2,)),
            dma((2,)),
        ]
        + links,
        compiler_params=pltpu.CompilerParams(
            collective_id=0, has_side_effects=True, vmem_limit_bytes=62 << 20
        ),
        name="layer",
    )(tokens, weights, bias.reshape(1, -1), resets, upstream)
    if not fused:
        gw = lax.psum_scatter(gw, ("seq", "dp"), scatter_dimension=0, tiled=True)
        gb = lax.psum(gb, ("seq", "dp"))
    return hid, gtok, gw, gb[0]


def solution(mesh):
    spread = P("dp", "seq", None)
    rows = P(("seq", "dp"), None)
    return jax.shard_map(
        per_device,
        mesh=mesh,
        in_specs=(spread, rows, P(), P("dp", "seq"), spread),
        out_specs=(spread, spread, rows, P()),
        check_vma=False,
    )
```

```python
import functools
import types

import jax
import jax.numpy as jnp
from jax import lax
from jax.experimental import pallas as pl
from jax.experimental.pallas import tpu as pltpu
from jax.sharding import PartitionSpec as P

MESH = pl.DeviceIdType.MESH
BF = jnp.bfloat16
F32 = jnp.float32
LANES = 128
TRIO = 3 * LANES
STEPS = 32
TWO = 16
VMEM_BYTES = 56 << 20


def cut_chunks(width):
    tiles = width // LANES
    chunks, at = [], 0
    if tiles % 2:
        chunks.append((0, LANES))
        at = LANES
    while at < width:
        chunks.append((at, 2 * LANES))
        at += 2 * LANES
    return chunks


def dot(a, b):
    return jnp.dot(a, b, preferred_element_type=F32)


def dot_rows(a, b):
    return lax.dot_general(a, b, (((0,), (0,)), ((), ())), preferred_element_type=F32)


def dot_columns(a, b):
    return lax.dot_general(a, b, (((1,), (1,)), ((), ())), preferred_element_type=F32)


def layer_kernel(
    span, peers, fused, chunks, names,
    tok, wts, bias, resets, up,
    hid, gtok, gw, gb,
    *scratch,
):
    held = types.SimpleNamespace(**dict(zip(names, scratch)))
    joined, upt, wv, qf, keepb = held.joined, held.upt, held.wv, held.qf, held.keepb
    perm, pinv, cbuf, summ, edge = held.perm, held.pinv, held.cbuf, held.summ, held.edge
    in_sem, w_sem = held.in_sem, held.w_sem
    sum_send, sum_recv = held.sum_send, held.sum_recv
    edge_send, edge_recv = held.edge_send, held.edge_recv
    gates = [getattr(held, f"gates{c}") for c in range(len(chunks))]
    gp = [getattr(held, f"gp{c}") for c in range(len(chunks))]
    seqs, steps, width = tok.shape
    rows = seqs * steps
    block = seqs * STEPS
    blocks = steps // STEPS
    depth = 2 * width
    half_rows = depth // 2
    n_chunks = len(chunks)
    me = lax.axis_index("seq")
    col = lax.axis_index("dp")
    core = col & 1
    place = col >> 1
    plane = peers // 2
    slab = depth // (span * plane)
    shard = slab // 2
    over = -(-shard // 16) * 16
    partner = (me, col ^ 1)
    if fused:
        own16, pair, sb1, rb1, rb2 = held.own16, held.pair, held.sb1, held.rb1, held.rb2
        own2, rb3, fin, fin_rx, gbs = held.own2, held.rb3, held.fin, held.fin_rx, held.gbs
        a0_sem, a3_sem, r4_sem = held.a0_sem, held.a3_sem, held.r4_sem
        a1_send, a1_recv, a2_send, a2_recv = held.a1_send, held.a1_recv, held.a2_send, held.a2_recv
        r1_send, r1_recv, r2_send, r2_recv = held.r1_send, held.r1_recv, held.r2_send, held.r2_recv
        r3_send, r3_recv, gb_send, gb_recv = held.r3_send, held.r3_recv, held.gb_send, held.gb_recv

    def remote(src, dst, send, recv, to):
        return pltpu.make_async_remote_copy(
            src_ref=src, dst_ref=dst, send_sem=send, recv_sem=recv,
            device_id=to, device_id_type=MESH,
        )

    def mult(v, m):
        return pl.multiple_of(v, m)

    in_t = pltpu.make_async_copy(tok, hid, in_sem.at[0])
    in_u = pltpu.make_async_copy(up, gtok, in_sem.at[1])
    if fused:
        in_w = pltpu.make_async_copy(wts, own16, w_sem.at[0])
        in_w.start()
    in_t.start()
    in_u.start()

    barrier = pltpu.get_barrier_semaphore()
    friends = [(lax.rem(me + k, span), col) for k in range(1, span)]
    if fused:
        friends += [(me, col ^ (2 * y)) for y in range(1, plane)] + [partner]
    for friend in friends:
        pl.semaphore_signal(barrier, inc=1, device_id=friend, device_id_type=MESH)
    pl.semaphore_wait(barrier, len(friends))

    def carried(c, who):
        at, cw = chunks[c]
        if cw == LANES:
            return over, mult((slab - over) * who, 16), 3 * at
        return slab, 0, mult(3 * at + TRIO * who, LANES)

    def part(c, who, planes, places):
        count, r0, c0 = carried(c, who)
        return wv.at[planes, places, pl.ds(r0, count), pl.ds(c0, TRIO)]

    def a1(c, x):
        here = part(c, core, me, place)
        return remote(here, here, a1_send.at[c, x - 1], a1_recv.at[c, x - 1], (me ^ x, col))

    def a2(c, y):
        here = part(c, core, slice(None), place)
        return remote(here, here, a2_send.at[c, y - 1], a2_recv.at[c, y - 1], (me, col ^ (2 * y)))

    def a3(c):
        if chunks[c][1] == LANES:
            here = wv.at[
                :, :, pl.ds(mult(over * core, 16), slab - over), pl.ds(3 * chunks[c][0], TRIO)
            ]
        else:
            here = part(c, core, slice(None), slice(None))
        return remote(here, here, a3_sem.at[c, 0], a3_sem.at[c, 1], partner)

    def w_copies(c):
        at, cw = chunks[c]
        return [
            pltpu.make_async_copy(
                wts.at[:, pl.ds(g * width + at + h * LANES, LANES)],
                wv.at[:, pl.ds(3 * at + h * TRIO + g * LANES, LANES)],
                w_sem.at[c, g, h],
            )
            for g in range(3)
            for h in range(cw // LANES)
        ]

    if fused:
        in_w.wait()
        pair[core] = own16[...].astype(F32)
        a0 = remote(pair.at[core], pair.at[core], a0_sem.at[0], a0_sem.at[1], partner)
        a0.start()
    else:
        for c in range(n_chunks):
            for copy in w_copies(c):
                copy.start()

    r = lax.broadcasted_iota(jnp.int32, (block, block), 0)
    q = lax.broadcasted_iota(jnp.int32, (block, block), 1)
    perm[...] = (((q & 31) == (r >> 3)) & ((q >> 5) == (r & 7))).astype(F32).astype(BF)
    pinv[...] = (((r & 31) == (q >> 3)) & ((r >> 5) == (q & 7))).astype(F32).astype(BF)

    if fused:
        a0.wait_recv()
        for c, (at, cw) in enumerate(chunks):
            count, top, left = carried(c, core)
            for g in range(3):
                lane = g * width + at + (0 if cw == LANES else core * LANES)
                lanes = pl.ds(mult(lane, LANES), LANES)
                both = jnp.concatenate([pair[0, :, lanes], pair[1, :, lanes]], axis=0)
                if count < slab:
                    both = jnp.where(core == 0, both[:count], both[slab - count :])
                to = pl.ds(mult(left + g * LANES, LANES), LANES)
                wv[me, place, pl.ds(top, count), to] = both.astype(BF)
            for x in range(1, span):
                a1(c, x).start()

    keep = 1.0 - resets[...].astype(F32)
    tiled = jnp.broadcast_to(keep[None], (STEPS, seqs, steps)).reshape(block, steps)
    row_t = lax.broadcasted_iota(jnp.int32, (block, steps), 0) >> 3
    lane_t = lax.broadcasted_iota(jnp.int32, (block, steps), 1)
    ones = jnp.ones((steps, LANES), BF)
    for b in range(blocks):
        picked = jnp.where(lane_t == row_t + b * STEPS, tiled, 0.0).astype(BF)
        keepb[b * block : (b + 1) * block, :] = dot(picked, ones)

    def wide_keep(at, count, lanes):
        k = keepb[pl.ds(at, count), :]
        return jnp.concatenate([k] * (lanes // LANES), axis=1)

    in_t.wait()
    last_rows = hid[:, steps - STEPS :, :].reshape(block, width)
    edge[0] = dot(perm[block - TWO :, :], last_rows)[TWO - seqs :]
    to_right = remote(edge.at[0], edge.at[1], edge_send.at[0], edge_recv.at[0], (me + 1, col))

    @pl.when(me < span - 1)
    def _():
        to_right.start()

    @pl.when(me == 0)
    def _():
        edge[1] = jnp.zeros((seqs, width), F32)

    in_u.wait()
    if fused:
        for x in range(1, span):
            a1(0, x).wait_recv()
        for y in range(1, plane):
            a2(0, y).start()

    def stage(b, last):
        at = mult(b * block, block)
        src = hid[:, pl.ds(mult(b * STEPS, STEPS), STEPS), :].reshape(block, width)
        now = dot(perm[...], src)
        before = jnp.concatenate([last, now[: block - seqs]], axis=0)
        before = before * wide_keep(at, block, width)
        joined[pl.ds(at, block), :width] = now.astype(BF)
        joined[pl.ds(at, block), width:] = before.astype(BF)
        src = gtok[:, pl.ds(mult(b * STEPS, STEPS), STEPS), :].reshape(block, width)
        upt[pl.ds(at, block), :] = dot(perm[...], src).astype(BF)
        return now[block - seqs :]

    lax.fori_loop(0, blocks, stage, jnp.zeros((seqs, width), F32))

    @pl.when(me > 0)
    def _():
        to_right.wait_recv()

    @pl.when(me < span - 1)
    def _():
        to_right.wait_send()

    first = jnp.concatenate([edge[1], joined[:TWO, :width].astype(F32)[:seqs]], axis=0)
    joined[:TWO, width:] = (first * wide_keep(0, TWO, width)).astype(BF)

    def weights_of(base, count):
        if fused:
            return wv[:, :, :, base : base + count].reshape(depth, count)
        return wv[:, base : base + count]

    def pass_a(c):
        at, cw = chunks[c]
        base = 3 * at
        size = 2 * block if blocks % 2 == 0 else block
        halves = range(cw // LANES)

        def bias_rows(g, h):
            lane = g * width + at + h * LANES
            return jnp.broadcast_to(bias[lane : lane + LANES].reshape(1, LANES), (TWO, LANES))

        bias_z = [bias_rows(0, h) for h in halves]
        bias_f = [0.5 * bias_rows(1, h) for h in halves]
        bias_o = [0.5 * bias_rows(2, h) for h in halves]

        def body(i, carry):
            carry = [list(v) for v in carry]
            r0 = mult(i * size, size)
            pre = dot(joined[pl.ds(r0, size), :], weights_of(base, 3 * cw))
            for j in range(size // TWO):
                sl = pl.ds(r0 + j * TWO, TWO)
                k = keepb[sl, :]
                for h in halves:
                    zc, fc, oc = (h * TRIO + g * LANES for g in range(3))
                    now = pre[j * TWO : (j + 1) * TWO]
                    z = jnp.tanh(now[:, zc : zc + LANES] + bias_z[h])
                    f = 0.5 * jnp.tanh(0.5 * now[:, fc : fc + LANES] + bias_f[h]) + 0.5
                    o = 0.5 * jnp.tanh(0.5 * now[:, oc : oc + LANES] + bias_o[h]) + 0.5
                    gates[c][sl, zc : zc + LANES] = z
                    gates[c][sl, fc : fc + LANES] = f
                    gates[c][sl, oc : oc + LANES] = o
                    g = upt[sl, at + h * LANES : at + (h + 1) * LANES].astype(F32)
                    eff = f * k
                    fresh = (1.0 - f) * z
                    src = g * o
                    gain, state, back = carry[h]
                    for m in (0, seqs):
                        gain = gain * eff[m : m + seqs]
                        state = state * eff[m : m + seqs] + fresh[m : m + seqs]
                        back = back + gain * src[m : m + seqs]
                    carry[h] = [gain, state, back]
            return tuple(tuple(v) for v in carry)

        zero = jnp.zeros((seqs, LANES), F32)
        one = jnp.ones((seqs, LANES), F32)
        done = lax.fori_loop(0, rows // size, body, tuple((one, zero, zero) for _ in halves))
        for h in halves:
            cols = slice(at + h * LANES, at + (h + 1) * LANES)
            for v in range(3):
                summ[me, v * seqs : (v + 1) * seqs, cols] = done[h][v]
        for k in range(1, span):
            exchange(c, k).start()

    def exchange(c, k):
        at, cw = chunks[c]
        here = summ.at[me, :, pl.ds(at, cw)]
        return remote(
            here, here, sum_send.at[c, k - 1], sum_recv.at[c, k - 1], (lax.rem(me + k, span), col)
        )

    def pass_b(c):
        at, cw = chunks[c]
        halves = range(cw // LANES)
        for k in range(1, span):
            exchange(c, k).wait()
        enter, leave = [], []
        for h in halves:
            cols = slice(at + h * LANES, at + (h + 1) * LANES)
            state = jnp.zeros((seqs, LANES), F32)
            for s in range(span - 1):
                new = summ[s, seqs : 2 * seqs, cols] + summ[s, :seqs, cols] * state
                state = jnp.where(s < me, new, state)
            enter.append(state)
            back = jnp.zeros((seqs, LANES), F32)
            for s in range(span - 1, 0, -1):
                new = summ[s, 2 * seqs :, cols] + summ[s, :seqs, cols] * back
                back = jnp.where(s > me, new, back)
            leave.append(back)

        def forward(i, carry):
            cells, sums = list(carry[0]), list(carry[1])
            r0 = mult(i * block, block)
            for j in range(block // TWO):
                sl = pl.ds(r0 + j * TWO, TWO)
                k = keepb[sl, :]
                for h in halves:
                    zc, fc, oc = (h * TRIO + g * LANES for g in range(3))
                    z = gates[c][sl, zc : zc + LANES]
                    f = gates[c][sl, fc : fc + LANES]
                    o = gates[c][sl, oc : oc + LANES]
                    lanes = slice(at + h * LANES, at + (h + 1) * LANES)
                    g = upt[sl, lanes].astype(F32)
                    eff = f * k
                    rest = 1.0 - f
                    fresh = rest * z
                    c0 = eff[:seqs] * cells[h] + fresh[:seqs]
                    c1 = eff[seqs:] * c0 + fresh[seqs:]
                    cell = jnp.concatenate([c0, c1], axis=0)
                    prev = jnp.concatenate([cells[h], c0], axis=0)
                    cells[h] = c1
                    hid[j // 2, pl.ds(mult(i * STEPS + j % 2 * TWO, TWO), TWO), lanes] = (
                        o * cell
                    ).astype(BF)
                    src = g * o
                    go = src * cell * (1.0 - o)
                    gp[c][sl, oc : oc + LANES] = go.astype(BF)
                    sums[h] = sums[h] + go
                    gates[c][sl, zc : zc + LANES] = rest * (1.0 - z * z)
                    gates[c][sl, fc : fc + LANES] = eff
                    gates[c][sl, oc : oc + LANES] = src
                    qf[sl, h * LANES : (h + 1) * LANES] = (prev * k - z) * (f * rest)
            return tuple(cells), tuple(sums)

        zero = jnp.zeros((TWO, LANES), F32)
        zeros = tuple(zero for _ in halves)
        _, sum_o = lax.fori_loop(0, blocks, forward, (tuple(enter), zeros))

        def backward(n, carry):
            heads, sums_z, sums_f = (list(v) for v in carry)
            r0 = mult((blocks - 1 - n) * block, block)
            for j in range(block // TWO - 1, -1, -1):
                sl = pl.ds(r0 + j * TWO, TWO)
                for h in halves:
                    zc, fc, oc = (h * TRIO + g * LANES for g in range(3))
                    eff = gates[c][sl, fc : fc + LANES]
                    src = gates[c][sl, oc : oc + LANES]
                    g1 = src[seqs:] + heads[h]
                    g0 = src[:seqs] + eff[seqs:] * g1
                    heads[h] = eff[:seqs] * g0
                    gc = jnp.concatenate([g0, g1], axis=0)
                    gz = gc * gates[c][sl, zc : zc + LANES]
                    gf = gc * qf[sl, h * LANES : (h + 1) * LANES]
                    gp[c][sl, zc : zc + LANES] = gz.astype(BF)
                    gp[c][sl, fc : fc + LANES] = gf.astype(BF)
                    sums_z[h] = sums_z[h] + gz
                    sums_f[h] = sums_f[h] + gf
            return tuple(heads), tuple(sums_z), tuple(sums_f)

        _, sum_z, sum_f = lax.fori_loop(0, blocks, backward, (tuple(leave), zeros, zeros))
        for h in halves:
            for g, total in enumerate((sum_z, sum_f, sum_o)):
                line = jnp.sum(total[h], axis=0, keepdims=True)
                if fused:
                    tile = g * (width // LANES) + at // LANES + h
                    gbs[0, tile : tile + 1, :] = line
                else:
                    lane = g * width + at + h * LANES
                    gb[lane : lane + LANES] = line.reshape(LANES)

    def gw_copies(c, turn):
        at, cw = chunks[c]
        return [
            pltpu.make_async_copy(
                cbuf.at[turn, :, pl.ds(h * TRIO + g * LANES, LANES)],
                gw.at[pl.ds(turn * half_rows, half_rows), pl.ds(g * width + at + h * LANES, LANES)],
                w_sem.at[c, g, h],
            )
            for g in range(3)
            for h in range(cw // LANES)
        ]

    def pass_c(c, turn):
        at, cw = chunks[c]
        if fused:
            r0 = mult(((me // (span // 2)) ^ 1 ^ turn) * half_rows, LANES)
            if c:
                r1_copy(c - 1, turn).wait_send()
            result = dot_rows(joined[:, pl.ds(r0, half_rows)], gp[c][...])
            result = result.reshape(-1, slab, 3 * cw)
            count = carried(c, 0)[0]
            if cw == LANES:
                zero, one = result[:, :count], result[:, slab - count :]
            else:
                zero, one = result[:, :, :TRIO], result[:, :, TRIO:]
            cbuf[turn, :, :count] = jnp.where(core == 0, zero, one)
            sb1[turn, :, :count] = jnp.where(core == 0, one, zero).astype(BF)
            r1_copy(c, turn).start()
        else:
            if c:
                for copy in gw_copies(c - 1, turn):
                    copy.wait()
            cbuf[turn, :, : 3 * cw] = dot_rows(
                joined[:, turn * half_rows : (turn + 1) * half_rows], gp[c][...]
            )
            for copy in gw_copies(c, turn):
                copy.start()

    def part_rows(c):
        return pl.ds(0, carried(c, 0)[0])

    def orders(turn):
        half = span // 2
        return list(range(half, span)) if turn == 0 else list(range(half - 1, -1, -1))

    def r1_copy(c, turn):
        k = part_rows(c)
        return remote(
            sb1.at[turn, :, k], rb1.at[c, turn, :, k], r1_send.at[c, turn], r1_recv.at[c, turn],
            partner,
        )

    def r2_copy(c, turn, n, y):
        k = part_rows(c)
        x = orders(turn)[n]
        index = ((me ^ x) % (span // 2)) * plane + (place ^ y)
        return remote(
            rb1.at[c, turn, index, k], rb2.at[c, turn, n, y - 1, k],
            r2_send.at[c, turn, n, y - 1], r2_recv.at[c, turn, n, y - 1], (me, col ^ (2 * y)),
        )

    def r2(c, turn):
        r1_copy(c, turn).wait_recv()
        k = part_rows(c)
        for n, x in enumerate(orders(turn)):
            for y in range(plane - 1, -1, -1):
                index = ((me ^ x) % (span // 2)) * plane + (place ^ y)
                total = cbuf[turn, index, k] + rb1[c, turn, index, k].astype(F32)
                if y:
                    rb1[c, turn, index, k] = total.astype(BF)
                    r2_copy(c, turn, n, y).start()
                else:
                    own2[c, turn, n, k] = total

    def r3_copy(c, turn, n):
        k = part_rows(c)
        x = orders(turn)[n]
        return remote(
            rb2.at[c, turn, n, 0, k], rb3.at[c, x - 1, k], r3_send.at[c, x - 1],
            r3_recv.at[c, x - 1], (me ^ x, col),
        )

    def r3(c, turn):
        k = part_rows(c)
        for n, x in enumerate(orders(turn)):
            total = own2[c, turn, n, k]
            for y in range(1, plane):
                r2_copy(c, turn, n, y).wait_recv()
                total = total + rb2[c, turn, n, y - 1, k].astype(F32)
            if x:
                rb2[c, turn, n, 0, k] = total.astype(BF)
                r3_copy(c, turn, n).start()
            else:
                own2[c, turn, n, k] = total

    def r4_copy(c):
        return remote(
            fin.at[c, pl.ds(mult(shard * (1 - core), 8), shard)], fin_rx.at[c],
            r4_sem.at[c, 0], r4_sem.at[c, 1], partner,
        )

    def put_gw(c, tile, value):
        at, cw = chunks[c]
        for g in range(3):
            lane = mult(g * width + at + tile * LANES, LANES)
            gw[:, pl.ds(lane, LANES)] = value[:, g * LANES : (g + 1) * LANES]

    def each_seq_peer(c):
        return [(turn, n, x) for turn in (0, 1) for n, x in enumerate(orders(turn)) if x]

    def r4(c):
        k = part_rows(c)
        total = own2[c, 1, span // 2 - 1, k]
        for turn, n, x in each_seq_peer(c):
            r3_copy(c, turn, n).wait_recv()
            total = total + rb3[c, x - 1, k].astype(F32)
        fin[c, k] = total
        if chunks[c][1] == LANES:
            off = (slab - over) * core
            put_gw(c, 0, fin[c, pl.ds(mult(shard * core - off, 8), shard)])
        else:
            r4_copy(c).start()
            put_gw(c, core, fin[c, pl.ds(mult(shard * core, 8), shard)])

    def r5(c):
        if chunks[c][1] != LANES:
            r4_copy(c).wait_recv()
            put_gw(c, 1 - core, fin_rx[c])

    def gb_stage(stage):
        if stage == 0:
            peer = [((me ^ x, col), x - 1) for x in range(1, span)]
        elif stage == 1:
            peer = [((me, col ^ (2 * y)), span - 1 + y - 1) for y in range(1, plane)]
        else:
            peer = [(partner, span + plane - 2)]
        src = gbs.at[stage]
        return [(remote(src, gbs.at[4 + k], gb_send.at[k], gb_recv.at[k], to), k) for to, k in peer]

    def gb_go(stage):
        for copy, _ in gb_stage(stage):
            copy.start()

    def gb_sum(stage):
        total = gbs[stage]
        for copy, k in gb_stage(stage):
            copy.wait_recv()
            total = total + gbs[4 + k]
        gbs[stage + 1] = total

    def gathered(c):
        if not fused:
            for copy in w_copies(c):
                copy.wait()
            return
        for y in range(1, plane):
            a2(c, y).wait_recv()
        a3(c).start()
        if c + 1 < n_chunks:
            for x in range(1, span):
                a1(c + 1, x).wait_recv()
            for y in range(1, plane):
                a2(c + 1, y).start()
        a3(c).wait_recv()

    def gates_of(c):
        gathered(c)
        pass_a(c)

    last = n_chunks - 1
    if fused:
        gbs[0] = jnp.zeros(gbs.shape[1:], F32)
    gates_of(0)
    gates_of(1)
    for c in range(n_chunks):
        pass_b(c)
        if fused and c:
            r2(c - 1, 1)
        if fused and c == last:
            gb_go(0)
        pass_c(c, 0)
        if fused and c:
            r3(c - 1, 0)
        pass_c(c, 1)
        if fused:
            if c:
                r3(c - 1, 1)
            r2(c, 0)
            if c > 1:
                r4(c - 2)
        if c + 2 < n_chunks:
            gates_of(c + 2)

    to_left = remote(edge.at[2], edge.at[3], edge_send.at[1], edge_recv.at[1], (me - 1, col))

    @pl.when(me == span - 1)
    def _():
        edge[3] = jnp.zeros((seqs, width), F32)

    late_gt = gates[last]

    def settle(ref, b, value):
        out = dot(pinv[...], value).astype(BF)
        ref[:, pl.ds(mult(b * STEPS, STEPS), STEPS), :] = out.reshape(seqs, STEPS, width)

    def put(b):
        settle(gtok, b, late_gt[pl.ds(mult(b * block, block), block), :width].astype(BF))

    def put_hidden(b):
        settle(hid, b, hid[:, pl.ds(mult(b * STEPS, STEPS), STEPS), :].reshape(block, width))

    def late_links(i):
        plan = {
            1: [lambda: r2(last, 1), lambda: r5(max(0, last - 2)), lambda: gb_sum(0), lambda: gb_go(1)],
            3: [lambda: r3(last, 0), lambda: r4(last - 1), lambda: gb_sum(1), lambda: gb_go(2)],
            5: [lambda: r3(last, 1), lambda: r5(last - 1), lambda: gb_sum(2)],
        }
        for when, todo in plan.items():

            @pl.when(i == when)
            def _(todo=todo):
                for step in todo:
                    step()

    def inputs(i, pend):
        r0 = mult(i * block, block)
        put_hidden(i)
        put(jnp.maximum(i - 2, 0))
        grads = jnp.concatenate([g[pl.ds(r0, block), :] for g in gp], axis=1)
        both = dot_columns(grads, weights_of(0, 3 * width))
        own = both[:, :width]
        late = both[:, width:] * wide_keep(r0, block, width)
        late_gt[pl.ds(r0, block - seqs), :width] = own[: block - seqs] + late[seqs:]
        before = jnp.where(i == 0, rows - seqs, r0 - seqs)
        late_gt[pl.ds(mult(before, seqs), seqs), :width] = pend + late[:seqs]

        @pl.when(i == 0)
        def _():
            edge[2] = late[:seqs]

            @pl.when(me > 0)
            def _():
                to_left.start()

        if fused:
            late_links(i)
        return own[block - seqs :]

    pend = lax.fori_loop(0, blocks, inputs, jnp.zeros((seqs, width), F32))

    @pl.when(me < span - 1)
    def _():
        to_left.wait_recv()

    @pl.when(me > 0)
    def _():
        to_left.wait_send()

    late_gt[rows - seqs :, :width] = pend + edge[3]
    put(blocks - 2)
    put(blocks - 1)
    if not fused:
        for turn in (0, 1):
            for copy in gw_copies(n_chunks - 1, turn):
                copy.wait()
    else:
        r4(last)
        for g in range(3 * width // LANES):
            gb[g * LANES : (g + 1) * LANES] = gbs[3, g : g + 1, :].reshape(LANES)
        r5(last)
        a0.wait_send()
        for c in range(n_chunks):
            a3(c).wait_send()
            for x in range(1, span):
                a1(c, x).wait_send()
            for y in range(1, plane):
                a2(c, y).wait_send()
            for turn in (0, 1):
                for n, x in enumerate(orders(turn)):
                    for y in range(1, plane):
                        r2_copy(c, turn, n, y).wait_send()
                    if x:
                        r3_copy(c, turn, n).wait_send()
            if chunks[c][1] != LANES:
                r4_copy(c).wait_send()
        for turn in (0, 1):
            r1_copy(last, turn).wait_send()
        for stage_index in range(3):
            for copy, _ in gb_stage(stage_index):
                copy.wait_send()


def per_device(tokens, weights, bias, resets, upstream):
    seqs, steps, width = tokens.shape
    rows = seqs * steps
    span, peers = lax.axis_size("seq"), lax.axis_size("dp")
    chunks = cut_chunks(width)
    n_chunks = len(chunks)
    block = seqs * STEPS
    depth = 2 * width
    shard = weights.shape[0]
    slab = 2 * shard
    plane = peers // 2
    half = span // 2
    fused = shard % 8 == 0 and slab % 16 == 0 and n_chunks >= 3 and steps // STEPS >= 6
    any_spec = pl.BlockSpec(memory_space=pl.ANY)
    vmem = pl.BlockSpec(memory_space=pltpu.VMEM)
    dma = pltpu.SemaphoreType.DMA
    vm = pltpu.VMEM
    held = {
        "joined": vm((rows, depth), BF),
        "upt": vm((rows, width), BF),
        "qf": vm((rows, 2 * LANES), F32),
        "keepb": vm((rows, LANES), F32),
        "perm": vm((block, block), BF),
        "pinv": vm((block, block), BF),
        "summ": vm((span, 3 * seqs, width), F32),
        "edge": vm((4, seqs, width), F32),
        "in_sem": dma((2,)),
        "sum_send": dma((n_chunks, span - 1)),
        "sum_recv": dma((n_chunks, span - 1)),
        "edge_send": dma((2,)),
        "edge_recv": dma((2,)),
    }
    for c, (_, cw) in enumerate(chunks):
        held[f"gates{c}"] = vm((rows, 3 * cw), F32)
        held[f"gp{c}"] = vm((rows, 3 * cw), BF)
    if fused:
        gw_shape, gw_spec = (shard, 3 * width), vmem
        piece = (half * plane, slab, TRIO)
        held |= {
            "wv": vm((span, plane, slab, 3 * width), BF),
            "cbuf": vm((2, *piece), F32),
            "own16": vm((shard, 3 * width), BF),
            "pair": vm((2, shard, 3 * width), F32),
            "sb1": vm((2, *piece), BF),
            "rb1": vm((n_chunks, 2, *piece), BF),
            "rb2": vm((n_chunks, 2, half, plane - 1, slab, TRIO), BF),
            "own2": vm((n_chunks, 2, half, slab, TRIO), F32),
            "rb3": vm((n_chunks, span - 1, slab, TRIO), BF),
            "fin": vm((n_chunks, slab, TRIO), F32),
            "fin_rx": vm((n_chunks, shard, TRIO), F32),
            "gbs": vm((4 + span + plane - 1, 16, LANES), F32),
            "w_sem": dma((1,)),
            "a0_sem": dma((2,)),
            "a1_send": dma((n_chunks, span - 1)),
            "a1_recv": dma((n_chunks, span - 1)),
            "a2_send": dma((n_chunks, plane - 1)),
            "a2_recv": dma((n_chunks, plane - 1)),
            "a3_sem": dma((n_chunks, 2)),
            "r1_send": dma((n_chunks, 2)),
            "r1_recv": dma((n_chunks, 2)),
            "r2_send": dma((n_chunks, 2, half, plane - 1)),
            "r2_recv": dma((n_chunks, 2, half, plane - 1)),
            "r3_send": dma((n_chunks, span - 1)),
            "r3_recv": dma((n_chunks, span - 1)),
            "r4_sem": dma((n_chunks, 2)),
            "gb_send": dma((span + plane - 1,)),
            "gb_recv": dma((span + plane - 1,)),
        }
    else:
        weights = lax.all_gather(weights, ("seq", "dp"), axis=0, tiled=True)
        gw_shape, gw_spec = (depth, 3 * width), any_spec
        held |= {
            "wv": vm((depth, 3 * width), BF),
            "cbuf": vm((2, depth // 2, 2 * TRIO), F32),
            "w_sem": dma((n_chunks, 3, 2)),
        }
    hid, gtok, gw, gb = pl.pallas_call(
        functools.partial(layer_kernel, span, peers, fused, chunks, tuple(held)),
        out_shape=(
            vm(tokens.shape, BF),
            vm(tokens.shape, BF),
            jax.ShapeDtypeStruct(gw_shape, F32),
            jax.ShapeDtypeStruct((3 * width,), F32),
        ),
        in_specs=[any_spec, any_spec, vmem, vmem, any_spec],
        out_specs=(vmem, vmem, gw_spec, vmem),
        scratch_shapes=list(held.values()),
        compiler_params=pltpu.CompilerParams(
            collective_id=0, has_side_effects=True, vmem_limit_bytes=VMEM_BYTES
        ),
        name="layer",
    )(tokens, weights, bias, resets, upstream)
    if not fused:
        gw = lax.psum_scatter(gw, ("seq", "dp"), scatter_dimension=0, tiled=True)
        gb = lax.psum(gb, ("seq", "dp"))
    return hid, gtok, gw, gb


def solution(mesh):
    spread = P("dp", "seq", None)
    rows = P(("seq", "dp"), None)
    return jax.shard_map(
        per_device,
        mesh=mesh,
        in_specs=(spread, rows, P(), P("dp", "seq"), spread),
        out_specs=(spread, spread, rows, P()),
        check_vma=False,
    )
```

```python
import functools
import types

import jax
import jax.numpy as jnp
from jax import lax
from jax.experimental import pallas as pl
from jax.experimental.pallas import tpu as pltpu
from jax.sharding import PartitionSpec as P

MESH = pl.DeviceIdType.MESH
BF = jnp.bfloat16
F32 = jnp.float32
LANES = 128
TRIO = 3 * LANES
STEPS = 32
TWO = 16
VMEM_BYTES = 56 << 20
EARLY = 16


def cut_chunks(width):
    tiles = width // LANES
    chunks, at = [], 0
    if tiles % 2:
        chunks.append((0, LANES))
        at = LANES
    while at < width:
        chunks.append((at, 2 * LANES))
        at += 2 * LANES
    return chunks


def dot(a, b):
    return jnp.dot(a, b, preferred_element_type=F32)


def dot_rows(a, b):
    return lax.dot_general(a, b, (((0,), (0,)), ((), ())), preferred_element_type=F32)


def dot_columns(a, b):
    return lax.dot_general(a, b, (((1,), (1,)), ((), ())), preferred_element_type=F32)


def layer_kernel(
    span, peers, fused, chunks, names,
    tok, wts, bias, resets, up,
    hid, gtok, gw, gb,
    *scratch,
):
    held = types.SimpleNamespace(**dict(zip(names, scratch)))
    joined, upt, wv, qf, keepb = held.joined, held.upt, held.wv, held.qf, held.keepb
    perm, pinv, cbuf, summ, edge = held.perm, held.pinv, held.cbuf, held.summ, held.edge
    in_sem, w_sem = held.in_sem, held.w_sem
    sum_send, sum_recv = held.sum_send, held.sum_recv
    edge_send, edge_recv = held.edge_send, held.edge_recv
    gates = [getattr(held, f"gates{c}") for c in range(len(chunks))]
    gp = [getattr(held, f"gp{c}") for c in range(len(chunks))]
    seqs, steps, width = tok.shape
    rows = seqs * steps
    block = seqs * STEPS
    blocks = steps // STEPS
    depth = 2 * width
    half_rows = depth // 2
    n_chunks = len(chunks)
    me = lax.axis_index("seq")
    col = lax.axis_index("dp")
    core = col & 1
    place = col >> 1
    plane = peers // 2
    slab = depth // (span * plane)
    shard = slab // 2
    over = -(-shard // 16) * 16
    partner = (me, col ^ 1)
    pieces = [(c, 0, TRIO) for c in range(len(chunks))]
    if fused:
        pieces[-1:] = [(len(chunks) - 1, 2 * LANES, LANES), (len(chunks) - 1, 0, 2 * LANES)]
    if fused:
        own16, pair, sb1, rb1, rb2 = held.own16, held.pair, held.sb1, held.rb1, held.rb2
        own2, rb3, fin, fin_rx, gbs = held.own2, held.rb3, held.fin, held.fin_rx, held.gbs
        a0_sem, a3_sem, r4_sem = held.a0_sem, held.a3_sem, held.r4_sem
        b1_send, b1_recv, b2_send, b2_recv = held.b1_send, held.b1_recv, held.b2_send, held.b2_recv
        a1_send, a1_recv, a2_send, a2_recv = held.a1_send, held.a1_recv, held.a2_send, held.a2_recv
        r1_send, r1_recv, r2_send, r2_recv = held.r1_send, held.r1_recv, held.r2_send, held.r2_recv
        r3_send, r3_recv, gb_send, gb_recv = held.r3_send, held.r3_recv, held.gb_send, held.gb_recv

    def remote(src, dst, send, recv, to):
        return pltpu.make_async_remote_copy(
            src_ref=src, dst_ref=dst, send_sem=send, recv_sem=recv,
            device_id=to, device_id_type=MESH,
        )

    def mult(v, m):
        return pl.multiple_of(v, m)

    in_t = pltpu.make_async_copy(tok, hid, in_sem.at[0])
    in_u = pltpu.make_async_copy(up, gtok, in_sem.at[1])
    if fused:
        in_w = pltpu.make_async_copy(wts, own16, w_sem.at[0])
        in_w.start()
    in_t.start()
    in_u.start()

    barrier = pltpu.get_barrier_semaphore()
    friends = [(lax.rem(me + k, span), col) for k in range(1, span)]
    if fused:
        friends += [(me, col ^ (2 * y)) for y in range(1, plane)] + [partner]
    for friend in friends:
        pl.semaphore_signal(barrier, inc=1, device_id=friend, device_id_type=MESH)
    pl.semaphore_wait(barrier, len(friends))

    def carried(c, who):
        at, cw = chunks[c]
        if cw == LANES:
            return over, mult((slab - over) * who, 16), 3 * at
        return slab, 0, mult(3 * at + TRIO * who, LANES)

    def part(c, who, planes, places):
        count, r0, c0 = carried(c, who)
        return wv.at[planes, places, pl.ds(r0, count), pl.ds(c0, TRIO)]

    def early(c, places):
        _, r0, c0 = carried(c, core)
        return wv.at[me, places, pl.ds(r0, EARLY), pl.ds(c0, TRIO)]

    def rest(c, planes):
        count, r0, c0 = carried(c, core)
        return wv.at[planes, place, pl.ds(mult(r0 + EARLY, 16), count - EARLY), pl.ds(c0, TRIO)]

    def a1(c, x):
        here = rest(c, me)
        return remote(here, here, a1_send.at[c, x - 1], a1_recv.at[c, x - 1], (me ^ x, col))

    def a2(c, y):
        here = rest(c, slice(None))
        return remote(here, here, a2_send.at[c, y - 1], a2_recv.at[c, y - 1], (me, col ^ (2 * y)))

    def b1(c, y):
        here = early(c, place)
        return remote(here, here, b1_send.at[c, y - 1], b1_recv.at[c, y - 1], (me, col ^ (2 * y)))

    def b2(c, x):
        here = early(c, slice(None))
        return remote(here, here, b2_send.at[c, x - 1], b2_recv.at[c, x - 1], (me ^ x, col))

    def a3(c):
        if chunks[c][1] == LANES:
            here = wv.at[
                :, :, pl.ds(mult(over * core, 16), slab - over), pl.ds(3 * chunks[c][0], TRIO)
            ]
        else:
            here = part(c, core, slice(None), slice(None))
        return remote(here, here, a3_sem.at[c, 0], a3_sem.at[c, 1], partner)

    def early_go(c):
        for y in range(1, plane):
            b1(c, y).wait_recv()
        for x in range(1, span):
            b2(c, x).start()

    def plane_go(c):
        for x in range(1, span):
            a1(c, x).wait_recv()
        if c < n_chunks - 1:
            for x in range(1, span):
                a1(c + 1, x).start()
        for y in range(1, plane):
            if c:
                a2(c - 1, y).wait_send()
        for y in range(1, plane):
            a2(c, y).start()

    def cores_go(c):
        for y in range(1, plane):
            a2(c, y).wait_recv()
        for x in range(1, span):
            b2(c, x).wait_recv()
        a3(c).start()

    def w_copies(c):
        at, cw = chunks[c]
        return [
            pltpu.make_async_copy(
                wts.at[:, pl.ds(g * width + at + h * LANES, LANES)],
                wv.at[:, pl.ds(3 * at + h * TRIO + g * LANES, LANES)],
                w_sem.at[c, g, h],
            )
            for g in range(3)
            for h in range(cw // LANES)
        ]

    if fused:
        in_w.wait()
        pair[core] = own16[...].astype(F32)
        a0 = remote(pair.at[core], pair.at[core], a0_sem.at[0], a0_sem.at[1], partner)
        a0.start()
    else:
        for c in range(n_chunks):
            for copy in w_copies(c):
                copy.start()

    r = lax.broadcasted_iota(jnp.int32, (block, block), 0)
    q = lax.broadcasted_iota(jnp.int32, (block, block), 1)
    perm[...] = (((q & 31) == (r >> 3)) & ((q >> 5) == (r & 7))).astype(F32).astype(BF)
    pinv[...] = (((r & 31) == (q >> 3)) & ((r >> 5) == (q & 7))).astype(F32).astype(BF)

    if fused:
        a0.wait_recv()
        for c, (at, cw) in enumerate(chunks):
            count, top, left = carried(c, core)
            for g in range(3):
                lane = g * width + at + (0 if cw == LANES else core * LANES)
                lanes = pl.ds(mult(lane, LANES), LANES)
                both = jnp.concatenate([pair[0, :, lanes], pair[1, :, lanes]], axis=0)
                if count < slab:
                    both = jnp.where(core == 0, both[:count], both[slab - count :])
                to = pl.ds(mult(left + g * LANES, LANES), LANES)
                wv[me, place, pl.ds(top, count), to] = both.astype(BF)
            if c == 0:
                for x in range(1, span):
                    a1(0, x).start()
            for y in range(1, plane):
                b1(c, y).start()

    keep = 1.0 - resets[...].astype(F32)
    tiled = jnp.broadcast_to(keep[None], (STEPS, seqs, steps)).reshape(block, steps)
    row_t = lax.broadcasted_iota(jnp.int32, (block, steps), 0) >> 3
    lane_t = lax.broadcasted_iota(jnp.int32, (block, steps), 1)
    ones = jnp.ones((steps, LANES), BF)
    for b in range(blocks):
        picked = jnp.where(lane_t == row_t + b * STEPS, tiled, 0.0).astype(BF)
        keepb[b * block : (b + 1) * block, :] = dot(picked, ones)

    def wide_keep(at, count, lanes):
        k = keepb[pl.ds(at, count), :]
        return jnp.concatenate([k] * (lanes // LANES), axis=1)

    in_t.wait()
    last_rows = hid[:, steps - STEPS :, :].reshape(block, width)
    edge[0] = dot(perm[block - TWO :, :], last_rows)[TWO - seqs :]
    to_right = remote(edge.at[0], edge.at[1], edge_send.at[0], edge_recv.at[0], (me + 1, col))

    @pl.when(me < span - 1)
    def _():
        to_right.start()

    @pl.when(me == 0)
    def _():
        edge[1] = jnp.zeros((seqs, width), F32)

    in_u.wait()
    if fused:
        early_go(0)
        plane_go(0)
        early_go(1)

    def stage(b, last):
        at = mult(b * block, block)
        src = hid[:, pl.ds(mult(b * STEPS, STEPS), STEPS), :].reshape(block, width)
        now = dot(perm[...], src)
        before = jnp.concatenate([last, now[: block - seqs]], axis=0)
        before = before * wide_keep(at, block, width)
        joined[pl.ds(at, block), :width] = now.astype(BF)
        joined[pl.ds(at, block), width:] = before.astype(BF)
        src = gtok[:, pl.ds(mult(b * STEPS, STEPS), STEPS), :].reshape(block, width)
        upt[pl.ds(at, block), :] = dot(perm[...], src).astype(BF)
        return now[block - seqs :]

    lax.fori_loop(0, blocks, stage, jnp.zeros((seqs, width), F32))

    @pl.when(me > 0)
    def _():
        to_right.wait_recv()

    @pl.when(me < span - 1)
    def _():
        to_right.wait_send()

    first = jnp.concatenate([edge[1], joined[:TWO, :width].astype(F32)[:seqs]], axis=0)
    joined[:TWO, width:] = (first * wide_keep(0, TWO, width)).astype(BF)

    def weights_of(base, count):
        if fused:
            return wv[:, :, :, base : base + count].reshape(depth, count)
        return wv[:, base : base + count]

    def pass_a(c):
        at, cw = chunks[c]
        base = 3 * at
        size = 2 * block if blocks % 2 == 0 else block
        halves = range(cw // LANES)

        def bias_rows(g, h):
            lane = g * width + at + h * LANES
            return jnp.broadcast_to(bias[lane : lane + LANES].reshape(1, LANES), (TWO, LANES))

        bias_z = [bias_rows(0, h) for h in halves]
        bias_f = [0.5 * bias_rows(1, h) for h in halves]
        bias_o = [0.5 * bias_rows(2, h) for h in halves]

        def body(i, carry):
            carry = [list(v) for v in carry]
            r0 = mult(i * size, size)
            pre = dot(joined[pl.ds(r0, size), :], weights_of(base, 3 * cw))
            for j in range(size // TWO):
                sl = pl.ds(r0 + j * TWO, TWO)
                k = keepb[sl, :]
                for h in halves:
                    zc, fc, oc = (h * TRIO + g * LANES for g in range(3))
                    now = pre[j * TWO : (j + 1) * TWO]
                    z = jnp.tanh(now[:, zc : zc + LANES] + bias_z[h])
                    f = 0.5 * jnp.tanh(0.5 * now[:, fc : fc + LANES] + bias_f[h]) + 0.5
                    o = 0.5 * jnp.tanh(0.5 * now[:, oc : oc + LANES] + bias_o[h]) + 0.5
                    gates[c][sl, zc : zc + LANES] = z
                    gates[c][sl, fc : fc + LANES] = f
                    gates[c][sl, oc : oc + LANES] = o
                    g = upt[sl, at + h * LANES : at + (h + 1) * LANES].astype(F32)
                    eff = f * k
                    fresh = (1.0 - f) * z
                    src = g * o
                    gain, state, back = carry[h]
                    for m in (0, seqs):
                        gain = gain * eff[m : m + seqs]
                        state = state * eff[m : m + seqs] + fresh[m : m + seqs]
                        back = back + gain * src[m : m + seqs]
                    carry[h] = [gain, state, back]
            return tuple(tuple(v) for v in carry)

        zero = jnp.zeros((seqs, LANES), F32)
        one = jnp.ones((seqs, LANES), F32)
        done = lax.fori_loop(0, rows // size, body, tuple((one, zero, zero) for _ in halves))
        for h in halves:
            cols = slice(at + h * LANES, at + (h + 1) * LANES)
            for v in range(3):
                summ[me, v * seqs : (v + 1) * seqs, cols] = done[h][v]
        for k in range(1, span):
            exchange(c, k).start()

    def exchange(c, k):
        at, cw = chunks[c]
        here = summ.at[me, :, pl.ds(at, cw)]
        return remote(
            here, here, sum_send.at[c, k - 1], sum_recv.at[c, k - 1], (lax.rem(me + k, span), col)
        )

    def pass_b(c, between=()):
        at, cw = chunks[c]
        halves = range(cw // LANES)
        for k in range(1, span):
            exchange(c, k).wait()
        enter, leave = [], []
        for h in halves:
            cols = slice(at + h * LANES, at + (h + 1) * LANES)
            state = jnp.zeros((seqs, LANES), F32)
            for s in range(span - 1):
                new = summ[s, seqs : 2 * seqs, cols] + summ[s, :seqs, cols] * state
                state = jnp.where(s < me, new, state)
            enter.append(state)
            back = jnp.zeros((seqs, LANES), F32)
            for s in range(span - 1, 0, -1):
                new = summ[s, 2 * seqs :, cols] + summ[s, :seqs, cols] * back
                back = jnp.where(s > me, new, back)
            leave.append(back)

        def forward(i, carry):
            cells, sums = list(carry[0]), list(carry[1])
            r0 = mult(i * block, block)
            for j in range(block // TWO):
                sl = pl.ds(r0 + j * TWO, TWO)
                k = keepb[sl, :]
                for h in halves:
                    zc, fc, oc = (h * TRIO + g * LANES for g in range(3))
                    z = gates[c][sl, zc : zc + LANES]
                    f = gates[c][sl, fc : fc + LANES]
                    o = gates[c][sl, oc : oc + LANES]
                    lanes = slice(at + h * LANES, at + (h + 1) * LANES)
                    g = upt[sl, lanes].astype(F32)
                    eff = f * k
                    rest = 1.0 - f
                    fresh = rest * z
                    c0 = eff[:seqs] * cells[h] + fresh[:seqs]
                    c1 = eff[seqs:] * c0 + fresh[seqs:]
                    cell = jnp.concatenate([c0, c1], axis=0)
                    prev = jnp.concatenate([cells[h], c0], axis=0)
                    cells[h] = c1
                    hid[j // 2, pl.ds(mult(i * STEPS + j % 2 * TWO, TWO), TWO), lanes] = (
                        o * cell
                    ).astype(BF)
                    src = g * o
                    go = src * cell * (1.0 - o)
                    gp[c][sl, oc : oc + LANES] = go.astype(BF)
                    sums[h] = sums[h] + go
                    gates[c][sl, zc : zc + LANES] = rest * (1.0 - z * z)
                    gates[c][sl, fc : fc + LANES] = eff
                    gates[c][sl, oc : oc + LANES] = src
                    qf[sl, h * LANES : (h + 1) * LANES] = (prev * k - z) * (f * rest)
            return tuple(cells), tuple(sums)

        zero = jnp.zeros((TWO, LANES), F32)
        zeros = tuple(zero for _ in halves)
        _, sum_o = lax.fori_loop(0, blocks, forward, (tuple(enter), zeros))

        for step in between:
            step()

        def backward(n, carry):
            heads, sums_z, sums_f = (list(v) for v in carry)
            r0 = mult((blocks - 1 - n) * block, block)
            for j in range(block // TWO - 1, -1, -1):
                sl = pl.ds(r0 + j * TWO, TWO)
                for h in halves:
                    zc, fc, oc = (h * TRIO + g * LANES for g in range(3))
                    eff = gates[c][sl, fc : fc + LANES]
                    src = gates[c][sl, oc : oc + LANES]
                    g1 = src[seqs:] + heads[h]
                    g0 = src[:seqs] + eff[seqs:] * g1
                    heads[h] = eff[:seqs] * g0
                    gc = jnp.concatenate([g0, g1], axis=0)
                    gz = gc * gates[c][sl, zc : zc + LANES]
                    gf = gc * qf[sl, h * LANES : (h + 1) * LANES]
                    gp[c][sl, zc : zc + LANES] = gz.astype(BF)
                    gp[c][sl, fc : fc + LANES] = gf.astype(BF)
                    sums_z[h] = sums_z[h] + gz
                    sums_f[h] = sums_f[h] + gf
            return tuple(heads), tuple(sums_z), tuple(sums_f)

        _, sum_z, sum_f = lax.fori_loop(0, blocks, backward, (tuple(leave), zeros, zeros))
        for h in halves:
            for g, total in enumerate((sum_z, sum_f, sum_o)):
                line = jnp.sum(total[h], axis=0, keepdims=True)
                if fused:
                    tile = g * (width // LANES) + at // LANES + h
                    gbs[0, tile : tile + 1, :] = line
                else:
                    lane = g * width + at + h * LANES
                    gb[lane : lane + LANES] = line.reshape(LANES)

    def gw_copies(c, turn):
        at, cw = chunks[c]
        return [
            pltpu.make_async_copy(
                cbuf.at[turn, :, pl.ds(h * TRIO + g * LANES, LANES)],
                gw.at[pl.ds(turn * half_rows, half_rows), pl.ds(g * width + at + h * LANES, LANES)],
                w_sem.at[c, g, h],
            )
            for g in range(3)
            for h in range(cw // LANES)
        ]

    def pass_c(p, turn):
        c, lane, lanes = pieces[p]
        at, cw = chunks[c]
        if fused:
            r0 = mult(((me // (span // 2)) ^ 1 ^ turn) * half_rows, LANES)
            if p and pieces[p - 1][0] != c:
                r1_copy(p - 1, turn).wait_send()
            right = [
                gp[c][:, h * TRIO + lane : h * TRIO + lane + lanes] for h in range(cw // LANES)
            ]
            result = dot_rows(joined[:, pl.ds(r0, half_rows)], jnp.concatenate(right, axis=1))
            result = result.reshape(-1, slab, result.shape[-1])
            count = carried(c, 0)[0]
            if cw == LANES:
                zero, one = result[:, :count], result[:, slab - count :]
            else:
                zero, one = result[:, :, :lanes], result[:, :, lanes:]
            cols = slice(lane, lane + lanes)
            cbuf[turn, :, :count, cols] = jnp.where(core == 0, zero, one)
            sb1[turn, :, :count, cols] = jnp.where(core == 0, one, zero).astype(BF)
            r1_copy(p, turn).start()
        else:
            if c:
                for copy in gw_copies(c - 1, turn):
                    copy.wait()
            cbuf[turn, :, : 3 * cw] = dot_rows(
                joined[:, turn * half_rows : (turn + 1) * half_rows], gp[c][...]
            )
            for copy in gw_copies(c, turn):
                copy.start()

    def spot(p):
        c, lane, lanes = pieces[p]
        return c, pl.ds(0, carried(c, 0)[0]), pl.ds(lane, lanes)

    def orders(turn):
        half = span // 2
        return list(range(half, span)) if turn == 0 else list(range(half - 1, -1, -1))

    def r1_copy(p, turn):
        c, k, l = spot(p)
        return remote(
            sb1.at[turn, :, k, l], rb1.at[c, turn, :, k, l],
            r1_send.at[p, turn], r1_recv.at[p, turn], partner,
        )

    def r2_copy(p, turn, n, y):
        c, k, l = spot(p)
        x = orders(turn)[n]
        index = ((me ^ x) % (span // 2)) * plane + (place ^ y)
        return remote(
            rb1.at[c, turn, index, k, l], rb2.at[c, turn, n, y - 1, k, l],
            r2_send.at[p, turn, n, y - 1], r2_recv.at[p, turn, n, y - 1], (me, col ^ (2 * y)),
        )

    def r2(p, turn):
        r1_copy(p, turn).wait_recv()
        c, k, l = spot(p)
        for n, x in enumerate(orders(turn)):
            for y in range(plane - 1, -1, -1):
                index = ((me ^ x) % (span // 2)) * plane + (place ^ y)
                total = cbuf[turn, index, k, l] + rb1[c, turn, index, k, l].astype(F32)
                if y:
                    rb1[c, turn, index, k, l] = total.astype(BF)
                    r2_copy(p, turn, n, y).start()
                else:
                    own2[c, turn, n, k, l] = total

    def r3_copy(p, turn, n):
        c, k, l = spot(p)
        x = orders(turn)[n]
        return remote(
            rb2.at[c, turn, n, 0, k, l], rb3.at[c, x - 1, k, l], r3_send.at[p, x - 1],
            r3_recv.at[p, x - 1], (me ^ x, col),
        )

    def r3(p, turn):
        c, k, l = spot(p)
        for n, x in enumerate(orders(turn)):
            total = own2[c, turn, n, k, l]
            for y in range(1, plane):
                r2_copy(p, turn, n, y).wait_recv()
                total = total + rb2[c, turn, n, y - 1, k, l].astype(F32)
            if x:
                rb2[c, turn, n, 0, k, l] = total.astype(BF)
                r3_copy(p, turn, n).start()
            else:
                own2[c, turn, n, k, l] = total

    def r4_copy(p):
        c, _, l = spot(p)
        return remote(
            fin.at[c, pl.ds(mult(shard * (1 - core), 8), shard), l], fin_rx.at[c, :, l],
            r4_sem.at[p, 0], r4_sem.at[p, 1], partner,
        )

    def put_gw(p, tile, value):
        c, first, lanes = pieces[p]
        for g in range(lanes // LANES):
            gate = first // LANES + g
            lane = mult(gate * width + chunks[c][0] + tile * LANES, LANES)
            gw[:, pl.ds(lane, LANES)] = value[:, g * LANES : (g + 1) * LANES]

    def each_seq_peer():
        return [(turn, n, x) for turn in (0, 1) for n, x in enumerate(orders(turn)) if x]

    def r4(p):
        c, k, l = spot(p)
        total = own2[c, 1, span // 2 - 1, k, l]
        for turn, n, x in each_seq_peer():
            r3_copy(p, turn, n).wait_recv()
            total = total + rb3[c, x - 1, k, l].astype(F32)
        fin[c, k, l] = total
        if chunks[c][1] == LANES:
            off = (slab - over) * core
            put_gw(p, 0, fin[c, pl.ds(mult(shard * core - off, 8), shard), l])
        else:
            r4_copy(p).start()
            put_gw(p, core, fin[c, pl.ds(mult(shard * core, 8), shard), l])

    def r5(p):
        c, _, l = spot(p)
        r4_copy(p).wait_recv()
        put_gw(p, 1 - core, fin_rx[c, :, l])

    def gb_stage(stage):
        if stage == 0:
            peer = [((me ^ x, col), x - 1) for x in range(1, span)]
        elif stage == 1:
            peer = [((me, col ^ (2 * y)), span - 1 + y - 1) for y in range(1, plane)]
        else:
            peer = [(partner, span + plane - 2)]
        src = gbs.at[stage]
        return [(remote(src, gbs.at[4 + k], gb_send.at[k], gb_recv.at[k], to), k) for to, k in peer]

    def gb_go(stage):
        for copy, _ in gb_stage(stage):
            copy.start()

    def gb_sum(stage):
        total = gbs[stage]
        for copy, k in gb_stage(stage):
            copy.wait_recv()
            total = total + gbs[4 + k]
        gbs[stage + 1] = total

    last = n_chunks - 1
    if not fused:
        for c in range(n_chunks):
            for copy in w_copies(c):
                copy.wait()
            pass_a(c)
        for c in range(n_chunks):
            pass_b(c)
            pass_c(c, 0)
            pass_c(c, 1)
    else:
        gbs[0] = jnp.zeros(gbs.shape[1:], F32)
        plane_go(1)
        cores_go(0)
        a3(0).wait_recv()
        pass_a(0)
        early_go(2)
        cores_go(1)
        plane_go(2)
        pass_b(0)
        a3(1).wait_recv()
        pass_a(1)
        pass_c(0, 0)
        cores_go(2)
        pass_c(0, 1)
        r2(0, 0)
        a3(2).wait_recv()
        pass_a(2)
        r2(0, 1)
        pass_b(1, [lambda: r3(0, 0)])
        pass_c(1, 0)
        r3(0, 1)
        pass_c(1, 1)
        r2(1, 0)
        pass_b(
            2, [lambda: r2(1, 1), lambda: pass_c(2, 0), lambda: r4(0), lambda: pass_c(2, 1), lambda: r2(2, 0)]
        )
        gb_go(0)
        r3(1, 0)
        r2(2, 1)
        pass_c(3, 0)
        r3(1, 1)
        pass_c(3, 1)
        r2(3, 0)

    to_left = remote(edge.at[2], edge.at[3], edge_send.at[1], edge_recv.at[1], (me - 1, col))

    @pl.when(me == span - 1)
    def _():
        edge[3] = jnp.zeros((seqs, width), F32)

    late_gt = gates[last]

    def settle(ref, b, value):
        out = dot(pinv[...], value).astype(BF)
        ref[:, pl.ds(mult(b * STEPS, STEPS), STEPS), :] = out.reshape(seqs, STEPS, width)

    def put(b):
        settle(gtok, b, late_gt[pl.ds(mult(b * block, block), block), :width].astype(BF))

    def put_hidden(b):
        settle(hid, b, hid[:, pl.ds(mult(b * STEPS, STEPS), STEPS), :].reshape(block, width))

    def late_links(i):
        plan = {
            0: [lambda: r2(3, 1), lambda: gb_sum(0), lambda: gb_go(1)],
            1: [lambda: r3(2, 0)],
            2: [lambda: r4(1), lambda: r3(2, 1), lambda: gb_sum(1), lambda: gb_go(2)],
            4: [lambda: r3(3, 0), lambda: r5(1), lambda: gb_sum(2)],
            5: [lambda: r4(2)],
            6: [lambda: r3(3, 1)],
            7: [lambda: r5(2)],
        }
        for when, todo in plan.items():

            @pl.when(i == when)
            def _(todo=todo):
                for step in todo:
                    step()

    def inputs(i, pend):
        r0 = mult(i * block, block)
        put_hidden(i)
        put(jnp.maximum(i - 2, 0))
        grads = jnp.concatenate([g[pl.ds(r0, block), :] for g in gp], axis=1)
        both = dot_columns(grads, weights_of(0, 3 * width))
        own = both[:, :width]
        late = both[:, width:] * wide_keep(r0, block, width)
        late_gt[pl.ds(r0, block - seqs), :width] = own[: block - seqs] + late[seqs:]
        before = jnp.where(i == 0, rows - seqs, r0 - seqs)
        late_gt[pl.ds(mult(before, seqs), seqs), :width] = pend + late[:seqs]

        @pl.when(i == 0)
        def _():
            edge[2] = late[:seqs]

            @pl.when(me > 0)
            def _():
                to_left.start()

        if fused:
            late_links(i)
        return own[block - seqs :]

    pend = lax.fori_loop(0, blocks, inputs, jnp.zeros((seqs, width), F32))

    @pl.when(me < span - 1)
    def _():
        to_left.wait_recv()

    @pl.when(me > 0)
    def _():
        to_left.wait_send()

    late_gt[rows - seqs :, :width] = pend + edge[3]
    put(blocks - 2)
    put(blocks - 1)
    if not fused:
        for turn in (0, 1):
            for copy in gw_copies(n_chunks - 1, turn):
                copy.wait()
    else:
        for g in range(3 * width // LANES):
            gb[g * LANES : (g + 1) * LANES] = gbs[3, g : g + 1, :].reshape(LANES)
        r4(3)
        a0.wait_send()
        for c in range(n_chunks):
            a3(c).wait_send()
            for x in range(1, span):
                a1(c, x).wait_send()
                b2(c, x).wait_send()
            for y in range(1, plane):
                b1(c, y).wait_send()
        for y in range(1, plane):
            a2(last, y).wait_send()
        for p in range(len(pieces)):
            for turn in (0, 1):
                if pieces[p][0] == last:
                    r1_copy(p, turn).wait_send()
                for n, x in enumerate(orders(turn)):
                    for y in range(1, plane):
                        r2_copy(p, turn, n, y).wait_send()
                    if x:
                        r3_copy(p, turn, n).wait_send()
            if chunks[pieces[p][0]][1] != LANES:
                r4_copy(p).wait_send()
        for stage_index in range(3):
            for copy, _ in gb_stage(stage_index):
                copy.wait_send()
        r5(3)


def per_device(tokens, weights, bias, resets, upstream):
    seqs, steps, width = tokens.shape
    rows = seqs * steps
    span, peers = lax.axis_size("seq"), lax.axis_size("dp")
    chunks = cut_chunks(width)
    n_chunks = len(chunks)
    block = seqs * STEPS
    depth = 2 * width
    shard = weights.shape[0]
    slab = 2 * shard
    plane = peers // 2
    half = span // 2
    fused = shard % 8 == 0 and slab % 16 == 0 and n_chunks == 3 and steps // STEPS >= 8
    any_spec = pl.BlockSpec(memory_space=pl.ANY)
    vmem = pl.BlockSpec(memory_space=pltpu.VMEM)
    dma = pltpu.SemaphoreType.DMA
    vm = pltpu.VMEM
    held = {
        "joined": vm((rows, depth), BF),
        "upt": vm((rows, width), BF),
        "qf": vm((rows, 2 * LANES), F32),
        "keepb": vm((rows, LANES), F32),
        "perm": vm((block, block), BF),
        "pinv": vm((block, block), BF),
        "summ": vm((span, 3 * seqs, width), F32),
        "edge": vm((4, seqs, width), F32),
        "in_sem": dma((2,)),
        "sum_send": dma((n_chunks, span - 1)),
        "sum_recv": dma((n_chunks, span - 1)),
        "edge_send": dma((2,)),
        "edge_recv": dma((2,)),
    }
    for c, (_, cw) in enumerate(chunks):
        held[f"gates{c}"] = vm((rows, 3 * cw), F32)
        held[f"gp{c}"] = vm((rows, 3 * cw), BF)
    if fused:
        gw_shape, gw_spec = (shard, 3 * width), vmem
        piece = (half * plane, slab, TRIO)
        held |= {
            "wv": vm((span, plane, slab, 3 * width), BF),
            "cbuf": vm((2, *piece), F32),
            "own16": vm((shard, 3 * width), BF),
            "pair": vm((2, shard, 3 * width), F32),
            "sb1": vm((2, *piece), BF),
            "rb1": vm((n_chunks, 2, *piece), BF),
            "rb2": vm((n_chunks, 2, half, plane - 1, slab, TRIO), BF),
            "own2": vm((n_chunks, 2, half, slab, TRIO), F32),
            "rb3": vm((n_chunks, span - 1, slab, TRIO), BF),
            "fin": vm((n_chunks, slab, TRIO), F32),
            "fin_rx": vm((n_chunks, shard, TRIO), F32),
            "gbs": vm((4 + span + plane - 1, 16, LANES), F32),
            "w_sem": dma((1,)),
            "a0_sem": dma((2,)),
            "a1_send": dma((n_chunks, span - 1)),
            "a1_recv": dma((n_chunks, span - 1)),
            "a2_send": dma((n_chunks, plane - 1)),
            "a2_recv": dma((n_chunks, plane - 1)),
            "b1_send": dma((n_chunks, plane - 1)),
            "b1_recv": dma((n_chunks, plane - 1)),
            "b2_send": dma((n_chunks, span - 1)),
            "b2_recv": dma((n_chunks, span - 1)),
            "a3_sem": dma((n_chunks, 2)),
            "r1_send": dma((n_chunks + 1, 2)),
            "r1_recv": dma((n_chunks + 1, 2)),
            "r2_send": dma((n_chunks + 1, 2, half, plane - 1)),
            "r2_recv": dma((n_chunks + 1, 2, half, plane - 1)),
            "r3_send": dma((n_chunks + 1, span - 1)),
            "r3_recv": dma((n_chunks + 1, span - 1)),
            "r4_sem": dma((n_chunks + 1, 2)),
            "gb_send": dma((span + plane - 1,)),
            "gb_recv": dma((span + plane - 1,)),
        }
    else:
        weights = lax.all_gather(weights, ("seq", "dp"), axis=0, tiled=True)
        gw_shape, gw_spec = (depth, 3 * width), any_spec
        held |= {
            "wv": vm((depth, 3 * width), BF),
            "cbuf": vm((2, depth // 2, 2 * TRIO), F32),
            "w_sem": dma((n_chunks, 3, 2)),
        }
    hid, gtok, gw, gb = pl.pallas_call(
        functools.partial(layer_kernel, span, peers, fused, chunks, tuple(held)),
        out_shape=(
            vm(tokens.shape, BF),
            vm(tokens.shape, BF),
            jax.ShapeDtypeStruct(gw_shape, F32),
            jax.ShapeDtypeStruct((3 * width,), F32),
        ),
        in_specs=[any_spec, any_spec, vmem, vmem, any_spec],
        out_specs=(vmem, vmem, gw_spec, vmem),
        scratch_shapes=list(held.values()),
        compiler_params=pltpu.CompilerParams(
            collective_id=0, has_side_effects=True, vmem_limit_bytes=VMEM_BYTES
        ),
        name="layer",
    )(tokens, weights, bias, resets, upstream)
    if not fused:
        gw = lax.psum_scatter(gw, ("seq", "dp"), scatter_dimension=0, tiled=True)
        gb = lax.psum(gb, ("seq", "dp"))
    return hid, gtok, gw, gb


def solution(mesh):
    spread = P("dp", "seq", None)
    rows = P(("seq", "dp"), None)
    return jax.shard_map(
        per_device,
        mesh=mesh,
        in_specs=(spread, rows, P(), P("dp", "seq"), spread),
        out_specs=(spread, spread, rows, P()),
        check_vma=False,
    )
```

```python
import functools
import types

import jax
import jax.numpy as jnp
from jax import lax
from jax.experimental import pallas as pl
from jax.experimental.pallas import tpu as pltpu
from jax.sharding import PartitionSpec as P

MESH = pl.DeviceIdType.MESH
BF = jnp.bfloat16
F32 = jnp.float32
LANES = 128
TRIO = 3 * LANES
STEPS = 32
TWO = 16
VMEM_BYTES = 56 << 20
EARLY = 16


def cut_chunks(width):
    tiles = width // LANES
    chunks, at = [], 0
    if tiles % 2:
        chunks.append((0, LANES))
        at = LANES
    while at < width:
        chunks.append((at, 2 * LANES))
        at += 2 * LANES
    return chunks


def dot(a, b):
    return jnp.dot(a, b, preferred_element_type=F32)


def dot_rows(a, b):
    return lax.dot_general(a, b, (((0,), (0,)), ((), ())), preferred_element_type=F32)


def dot_columns(a, b):
    return lax.dot_general(a, b, (((1,), (1,)), ((), ())), preferred_element_type=F32)


def layer_kernel(
    span, peers, fused, chunks, names,
    tok, wts, bias, resets, up,
    hid, gtok, gw, gb,
    *scratch,
):
    held = types.SimpleNamespace(**dict(zip(names, scratch)))
    joined, upt, wv, qf, keepb = held.joined, held.upt, held.wv, held.qf, held.keepb
    perm, pinv, cbuf, summ, edge = held.perm, held.pinv, held.cbuf, held.summ, held.edge
    in_sem, w_sem = held.in_sem, held.w_sem
    sum_send, sum_recv = held.sum_send, held.sum_recv
    edge_send, edge_recv = held.edge_send, held.edge_recv
    gates = [getattr(held, f"gates{c}") for c in range(len(chunks))]
    gp = [getattr(held, f"gp{c}") for c in range(len(chunks))]
    seqs, steps, width = tok.shape
    rows = seqs * steps
    block = seqs * STEPS
    blocks = steps // STEPS
    depth = 2 * width
    half_rows = depth // 2
    n_chunks = len(chunks)
    me = lax.axis_index("seq")
    col = lax.axis_index("dp")
    core = col & 1
    place = col >> 1
    plane = peers // 2
    slab = depth // (span * plane)
    shard = slab // 2
    over = -(-shard // 16) * 16
    partner = (me, col ^ 1)
    pieces = [(c, 0, TRIO) for c in range(len(chunks))]
    if fused:
        pieces[-1:] = [(len(chunks) - 1, 2 * LANES, LANES), (len(chunks) - 1, 0, 2 * LANES)]
    if fused:
        own16, pair, sb1, rb1, rb2 = held.own16, held.pair, held.sb1, held.rb1, held.rb2
        own2, rb3, fin, fin_rx, gbs = held.own2, held.rb3, held.fin, held.fin_rx, held.gbs
        a0_sem, a3_sem, r4_sem = held.a0_sem, held.a3_sem, held.r4_sem
        b1_send, b1_recv, b2_send, b2_recv = held.b1_send, held.b1_recv, held.b2_send, held.b2_recv
        a1_send, a1_recv, a2_send, a2_recv = held.a1_send, held.a1_recv, held.a2_send, held.a2_recv
        r1_send, r1_recv, r2_send, r2_recv = held.r1_send, held.r1_recv, held.r2_send, held.r2_recv
        r3_send, r3_recv, gb_send, gb_recv = held.r3_send, held.r3_recv, held.gb_send, held.gb_recv

    def remote(src, dst, send, recv, to):
        return pltpu.make_async_remote_copy(
            src_ref=src, dst_ref=dst, send_sem=send, recv_sem=recv,
            device_id=to, device_id_type=MESH,
        )

    def mult(v, m):
        return pl.multiple_of(v, m)

    in_t = pltpu.make_async_copy(tok, hid, in_sem.at[0])
    in_u = pltpu.make_async_copy(up, gtok, in_sem.at[1])
    if fused:
        in_w = pltpu.make_async_copy(wts, own16, w_sem.at[0])
        in_w.start()
    in_t.start()
    in_u.start()

    barrier = pltpu.get_barrier_semaphore()
    friends = [(lax.rem(me + k, span), col) for k in range(1, span)]
    if fused:
        friends += [(me, col ^ (2 * y)) for y in range(1, plane)] + [partner]
    for friend in friends:
        pl.semaphore_signal(barrier, inc=1, device_id=friend, device_id_type=MESH)
    pl.semaphore_wait(barrier, len(friends))

    def carried(c, who):
        at, cw = chunks[c]
        if cw == LANES:
            return over, mult((slab - over) * who, 16), 3 * at
        return slab, 0, mult(3 * at + TRIO * who, LANES)

    def part(c, who, planes, places):
        count, r0, c0 = carried(c, who)
        return wv.at[planes, places, pl.ds(r0, count), pl.ds(c0, TRIO)]

    def early(c, places):
        _, r0, c0 = carried(c, core)
        return wv.at[me, places, pl.ds(r0, EARLY), pl.ds(c0, TRIO)]

    def rest(c, planes):
        count, r0, c0 = carried(c, core)
        return wv.at[planes, place, pl.ds(mult(r0 + EARLY, 16), count - EARLY), pl.ds(c0, TRIO)]

    def a1(c, x):
        here = rest(c, me)
        return remote(here, here, a1_send.at[c, x - 1], a1_recv.at[c, x - 1], (me ^ x, col))

    def a2(c, y):
        here = rest(c, slice(None))
        return remote(here, here, a2_send.at[c, y - 1], a2_recv.at[c, y - 1], (me, col ^ (2 * y)))

    def b1(c, y):
        here = early(c, place)
        return remote(here, here, b1_send.at[c, y - 1], b1_recv.at[c, y - 1], (me, col ^ (2 * y)))

    def b2(c, x):
        here = early(c, slice(None))
        return remote(here, here, b2_send.at[c, x - 1], b2_recv.at[c, x - 1], (me ^ x, col))

    def a3(c):
        if chunks[c][1] == LANES:
            here = wv.at[
                :, :, pl.ds(mult(over * core, 16), slab - over), pl.ds(3 * chunks[c][0], TRIO)
            ]
        else:
            here = part(c, core, slice(None), slice(None))
        return remote(here, here, a3_sem.at[c, 0], a3_sem.at[c, 1], partner)

    def early_go(c):
        for y in range(1, plane):
            b1(c, y).wait_recv()
        for x in range(1, span):
            b2(c, x).start()

    def plane_go(c):
        for x in range(1, span):
            a1(c, x).wait_recv()
        if c < n_chunks - 1:
            for x in range(1, span):
                a1(c + 1, x).start()
        for y in range(1, plane):
            if c:
                a2(c - 1, y).wait_send()
        for y in range(1, plane):
            a2(c, y).start()

    def cores_go(c):
        for y in range(1, plane):
            a2(c, y).wait_recv()
        for x in range(1, span):
            b2(c, x).wait_recv()
        a3(c).start()

    def w_copies(c):
        at, cw = chunks[c]
        return [
            pltpu.make_async_copy(
                wts.at[:, pl.ds(g * width + at + h * LANES, LANES)],
                wv.at[:, pl.ds(3 * at + h * TRIO + g * LANES, LANES)],
                w_sem.at[c, g, h],
            )
            for g in range(3)
            for h in range(cw // LANES)
        ]

    if fused:
        in_w.wait()
        pair[core] = own16[...].astype(F32)
        a0 = remote(pair.at[core], pair.at[core], a0_sem.at[0], a0_sem.at[1], partner)
        a0.start()
    else:
        for c in range(n_chunks):
            for copy in w_copies(c):
                copy.start()

    r = lax.broadcasted_iota(jnp.int32, (block, block), 0)
    q = lax.broadcasted_iota(jnp.int32, (block, block), 1)
    perm[...] = (((q & 31) == (r >> 3)) & ((q >> 5) == (r & 7))).astype(F32).astype(BF)
    pinv[...] = (((r & 31) == (q >> 3)) & ((r >> 5) == (q & 7))).astype(F32).astype(BF)

    if fused:
        a0.wait_recv()
        for c, (at, cw) in enumerate(chunks):
            count, top, left = carried(c, core)
            for g in range(3):
                lane = g * width + at + (0 if cw == LANES else core * LANES)
                lanes = pl.ds(mult(lane, LANES), LANES)
                both = jnp.concatenate([pair[0, :, lanes], pair[1, :, lanes]], axis=0)
                if count < slab:
                    both = jnp.where(core == 0, both[:count], both[slab - count :])
                to = pl.ds(mult(left + g * LANES, LANES), LANES)
                wv[me, place, pl.ds(top, count), to] = both.astype(BF)
            if c == 0:
                for x in range(1, span):
                    a1(0, x).start()
            for y in range(1, plane):
                b1(c, y).start()

    keep = 1.0 - resets[...].astype(F32)
    tiled = jnp.broadcast_to(keep[None], (STEPS, seqs, steps)).reshape(block, steps)
    row_t = lax.broadcasted_iota(jnp.int32, (block, steps), 0) >> 3
    lane_t = lax.broadcasted_iota(jnp.int32, (block, steps), 1)
    ones = jnp.ones((steps, LANES), BF)
    for b in range(blocks):
        picked = jnp.where(lane_t == row_t + b * STEPS, tiled, 0.0).astype(BF)
        keepb[b * block : (b + 1) * block, :] = dot(picked, ones)

    def wide_keep(at, count, lanes):
        k = keepb[pl.ds(at, count), :]
        return jnp.concatenate([k] * (lanes // LANES), axis=1)

    in_t.wait()
    last_rows = hid[:, steps - STEPS :, :].reshape(block, width)
    edge[0] = dot(perm[block - TWO :, :], last_rows)[TWO - seqs :]
    to_right = remote(edge.at[0], edge.at[1], edge_send.at[0], edge_recv.at[0], (me + 1, col))

    @pl.when(me < span - 1)
    def _():
        to_right.start()

    @pl.when(me == 0)
    def _():
        edge[1] = jnp.zeros((seqs, width), F32)

    in_u.wait()
    if fused:
        early_go(0)
        plane_go(0)
        early_go(1)

    def stage(b, last):
        at = mult(b * block, block)
        src = hid[:, pl.ds(mult(b * STEPS, STEPS), STEPS), :].reshape(block, width)
        now = dot(perm[...], src)
        before = jnp.concatenate([last, now[: block - seqs]], axis=0)
        before = before * wide_keep(at, block, width)
        joined[pl.ds(at, block), :width] = now.astype(BF)
        joined[pl.ds(at, block), width:] = before.astype(BF)
        src = gtok[:, pl.ds(mult(b * STEPS, STEPS), STEPS), :].reshape(block, width)
        upt[pl.ds(at, block), :] = dot(perm[...], src).astype(BF)
        return now[block - seqs :]

    lax.fori_loop(0, blocks, stage, jnp.zeros((seqs, width), F32))

    @pl.when(me > 0)
    def _():
        to_right.wait_recv()

    @pl.when(me < span - 1)
    def _():
        to_right.wait_send()

    first = jnp.concatenate([edge[1], joined[:TWO, :width].astype(F32)[:seqs]], axis=0)
    joined[:TWO, width:] = (first * wide_keep(0, TWO, width)).astype(BF)

    def weights_of(base, count):
        if fused:
            return wv[:, :, :, base : base + count].reshape(depth, count)
        return wv[:, base : base + count]

    def pass_a(c):
        at, cw = chunks[c]
        base = 3 * at
        size = 2 * block if blocks % 2 == 0 else block
        halves = range(cw // LANES)

        def bias_rows(g, h):
            lane = g * width + at + h * LANES
            return jnp.broadcast_to(bias[lane : lane + LANES].reshape(1, LANES), (TWO, LANES))

        bias_z = [bias_rows(0, h) for h in halves]
        bias_f = [0.5 * bias_rows(1, h) for h in halves]
        bias_o = [0.5 * bias_rows(2, h) for h in halves]

        def body(i, carry):
            carry = [list(v) for v in carry]
            r0 = mult(i * size, size)
            pre = dot(joined[pl.ds(r0, size), :], weights_of(base, 3 * cw))
            for j in range(size // TWO):
                sl = pl.ds(r0 + j * TWO, TWO)
                k = keepb[sl, :]
                for h in halves:
                    zc, fc, oc = (h * TRIO + g * LANES for g in range(3))
                    now = pre[j * TWO : (j + 1) * TWO]
                    z = jnp.tanh(now[:, zc : zc + LANES] + bias_z[h])
                    f = 0.5 * jnp.tanh(0.5 * now[:, fc : fc + LANES] + bias_f[h]) + 0.5
                    o = 0.5 * jnp.tanh(0.5 * now[:, oc : oc + LANES] + bias_o[h]) + 0.5
                    gates[c][sl, zc : zc + LANES] = z
                    gates[c][sl, fc : fc + LANES] = f
                    gates[c][sl, oc : oc + LANES] = o
                    g = upt[sl, at + h * LANES : at + (h + 1) * LANES].astype(F32)
                    eff = f * k
                    fresh = (1.0 - f) * z
                    src = g * o
                    gain, state, back = carry[h]
                    for m in (0, seqs):
                        gain = gain * eff[m : m + seqs]
                        state = state * eff[m : m + seqs] + fresh[m : m + seqs]
                        back = back + gain * src[m : m + seqs]
                    carry[h] = [gain, state, back]
            return tuple(tuple(v) for v in carry)

        zero = jnp.zeros((seqs, LANES), F32)
        one = jnp.ones((seqs, LANES), F32)
        done = lax.fori_loop(0, rows // size, body, tuple((one, zero, zero) for _ in halves))
        for h in halves:
            cols = slice(at + h * LANES, at + (h + 1) * LANES)
            for v in range(3):
                summ[me, v * seqs : (v + 1) * seqs, cols] = done[h][v]
        for k in range(1, span):
            exchange(c, k).start()

    def exchange(c, k):
        at, cw = chunks[c]
        here = summ.at[me, :, pl.ds(at, cw)]
        return remote(
            here, here, sum_send.at[c, k - 1], sum_recv.at[c, k - 1], (lax.rem(me + k, span), col)
        )

    def pass_b(c, between=()):
        at, cw = chunks[c]
        halves = range(cw // LANES)
        for k in range(1, span):
            exchange(c, k).wait()
        enter, leave = [], []
        for h in halves:
            cols = slice(at + h * LANES, at + (h + 1) * LANES)
            state = jnp.zeros((seqs, LANES), F32)
            for s in range(span - 1):
                new = summ[s, seqs : 2 * seqs, cols] + summ[s, :seqs, cols] * state
                state = jnp.where(s < me, new, state)
            enter.append(state)
            back = jnp.zeros((seqs, LANES), F32)
            for s in range(span - 1, 0, -1):
                new = summ[s, 2 * seqs :, cols] + summ[s, :seqs, cols] * back
                back = jnp.where(s > me, new, back)
            leave.append(back)

        def forward(i, carry):
            cells, sums = list(carry[0]), list(carry[1])
            r0 = mult(i * block, block)
            for j in range(block // TWO):
                sl = pl.ds(r0 + j * TWO, TWO)
                k = keepb[sl, :]
                for h in halves:
                    zc, fc, oc = (h * TRIO + g * LANES for g in range(3))
                    z = gates[c][sl, zc : zc + LANES]
                    f = gates[c][sl, fc : fc + LANES]
                    o = gates[c][sl, oc : oc + LANES]
                    lanes = slice(at + h * LANES, at + (h + 1) * LANES)
                    g = upt[sl, lanes].astype(F32)
                    eff = f * k
                    rest = 1.0 - f
                    fresh = rest * z
                    c0 = eff[:seqs] * cells[h] + fresh[:seqs]
                    c1 = eff[seqs:] * c0 + fresh[seqs:]
                    cell = jnp.concatenate([c0, c1], axis=0)
                    prev = jnp.concatenate([cells[h], c0], axis=0)
                    cells[h] = c1
                    hid[j // 2, pl.ds(mult(i * STEPS + j % 2 * TWO, TWO), TWO), lanes] = (
                        o * cell
                    ).astype(BF)
                    src = g * o
                    go = src * cell * (1.0 - o)
                    gp[c][sl, oc : oc + LANES] = go.astype(BF)
                    sums[h] = sums[h] + go
                    gates[c][sl, zc : zc + LANES] = rest * (1.0 - z * z)
                    gates[c][sl, fc : fc + LANES] = eff
                    gates[c][sl, oc : oc + LANES] = src
                    qf[sl, h * LANES : (h + 1) * LANES] = (prev * k - z) * (f * rest)
            return tuple(cells), tuple(sums)

        zero = jnp.zeros((TWO, LANES), F32)
        zeros = tuple(zero for _ in halves)
        _, sum_o = lax.fori_loop(0, blocks, forward, (tuple(enter), zeros))

        for step in between:
            step()

        def backward(n, carry):
            heads, sums_z, sums_f = (list(v) for v in carry)
            r0 = mult((blocks - 1 - n) * block, block)
            for j in range(block // TWO - 1, -1, -1):
                sl = pl.ds(r0 + j * TWO, TWO)
                for h in halves:
                    zc, fc, oc = (h * TRIO + g * LANES for g in range(3))
                    eff = gates[c][sl, fc : fc + LANES]
                    src = gates[c][sl, oc : oc + LANES]
                    g1 = src[seqs:] + heads[h]
                    g0 = src[:seqs] + eff[seqs:] * g1
                    heads[h] = eff[:seqs] * g0
                    gc = jnp.concatenate([g0, g1], axis=0)
                    gz = gc * gates[c][sl, zc : zc + LANES]
                    gf = gc * qf[sl, h * LANES : (h + 1) * LANES]
                    gp[c][sl, zc : zc + LANES] = gz.astype(BF)
                    gp[c][sl, fc : fc + LANES] = gf.astype(BF)
                    sums_z[h] = sums_z[h] + gz
                    sums_f[h] = sums_f[h] + gf
            return tuple(heads), tuple(sums_z), tuple(sums_f)

        _, sum_z, sum_f = lax.fori_loop(0, blocks, backward, (tuple(leave), zeros, zeros))
        for h in halves:
            for g, total in enumerate((sum_z, sum_f, sum_o)):
                line = jnp.sum(total[h], axis=0, keepdims=True)
                if fused:
                    tile = g * (width // LANES) + at // LANES + h
                    gbs[0, tile : tile + 1, :] = line
                else:
                    lane = g * width + at + h * LANES
                    gb[lane : lane + LANES] = line.reshape(LANES)

    def gw_copies(c, turn):
        at, cw = chunks[c]
        return [
            pltpu.make_async_copy(
                cbuf.at[turn, :, pl.ds(h * TRIO + g * LANES, LANES)],
                gw.at[pl.ds(turn * half_rows, half_rows), pl.ds(g * width + at + h * LANES, LANES)],
                w_sem.at[c, g, h],
            )
            for g in range(3)
            for h in range(cw // LANES)
        ]

    def pass_c(p, turn):
        c, lane, lanes = pieces[p]
        at, cw = chunks[c]
        if fused:
            r0 = mult(((me // (span // 2)) ^ 1 ^ turn) * half_rows, LANES)
            if p and pieces[p - 1][0] != c:
                r1_copy(p - 1, turn).wait_send()
            right = [
                gp[c][:, h * TRIO + lane : h * TRIO + lane + lanes] for h in range(cw // LANES)
            ]
            result = dot_rows(joined[:, pl.ds(r0, half_rows)], jnp.concatenate(right, axis=1))
            result = result.reshape(-1, slab, result.shape[-1])
            count = carried(c, 0)[0]
            if cw == LANES:
                zero, one = result[:, :count], result[:, slab - count :]
            else:
                zero, one = result[:, :, :lanes], result[:, :, lanes:]
            cols = slice(lane, lane + lanes)
            cbuf[turn, :, :count, cols] = jnp.where(core == 0, zero, one)
            sb1[turn, :, :count, cols] = jnp.where(core == 0, one, zero).astype(BF)
            r1_copy(p, turn).start()
        else:
            if c:
                for copy in gw_copies(c - 1, turn):
                    copy.wait()
            cbuf[turn, :, : 3 * cw] = dot_rows(
                joined[:, turn * half_rows : (turn + 1) * half_rows], gp[c][...]
            )
            for copy in gw_copies(c, turn):
                copy.start()

    def spot(p):
        c, lane, lanes = pieces[p]
        return c, pl.ds(0, carried(c, 0)[0]), pl.ds(lane, lanes)

    def orders(turn):
        half = span // 2
        return list(range(half, span)) if turn == 0 else list(range(half - 1, -1, -1))

    def r1_copy(p, turn):
        c, k, l = spot(p)
        return remote(
            sb1.at[turn, :, k, l], rb1.at[c, turn, :, k, l],
            r1_send.at[p, turn], r1_recv.at[p, turn], partner,
        )

    def r2_copy(p, turn, n, y):
        c, k, l = spot(p)
        x = orders(turn)[n]
        index = ((me ^ x) % (span // 2)) * plane + (place ^ y)
        return remote(
            rb1.at[c, turn, index, k, l], rb2.at[c, turn, n, y - 1, k, l],
            r2_send.at[p, turn, n, y - 1], r2_recv.at[p, turn, n, y - 1], (me, col ^ (2 * y)),
        )

    def r2(p, turn):
        r1_copy(p, turn).wait_recv()
        c, k, l = spot(p)
        for n, x in enumerate(orders(turn)):
            for y in range(plane - 1, -1, -1):
                index = ((me ^ x) % (span // 2)) * plane + (place ^ y)
                total = cbuf[turn, index, k, l] + rb1[c, turn, index, k, l].astype(F32)
                if y:
                    rb1[c, turn, index, k, l] = total.astype(BF)
                    r2_copy(p, turn, n, y).start()
                else:
                    own2[c, turn, n, k, l] = total

    def r3_copy(p, turn, n):
        c, k, l = spot(p)
        x = orders(turn)[n]
        return remote(
            rb2.at[c, turn, n, 0, k, l], rb3.at[c, x - 1, k, l], r3_send.at[p, x - 1],
            r3_recv.at[p, x - 1], (me ^ x, col),
        )

    def r3(p, turn):
        c, k, l = spot(p)
        for n, x in enumerate(orders(turn)):
            total = own2[c, turn, n, k, l]
            for y in range(1, plane):
                r2_copy(p, turn, n, y).wait_recv()
                total = total + rb2[c, turn, n, y - 1, k, l].astype(F32)
            if x:
                rb2[c, turn, n, 0, k, l] = total.astype(BF)
                r3_copy(p, turn, n).start()
            else:
                own2[c, turn, n, k, l] = total

    def r4_copy(p):
        c, _, l = spot(p)
        return remote(
            fin.at[c, pl.ds(mult(shard * (1 - core), 8), shard), l], fin_rx.at[c, :, l],
            r4_sem.at[p, 0], r4_sem.at[p, 1], partner,
        )

    def put_gw(p, tile, value):
        c, first, lanes = pieces[p]
        for g in range(lanes // LANES):
            gate = first // LANES + g
            lane = mult(gate * width + chunks[c][0] + tile * LANES, LANES)
            gw[:, pl.ds(lane, LANES)] = value[:, g * LANES : (g + 1) * LANES]

    def each_seq_peer():
        return [(turn, n, x) for turn in (0, 1) for n, x in enumerate(orders(turn)) if x]

    def r4(p):
        c, k, l = spot(p)
        total = own2[c, 1, span // 2 - 1, k, l]
        for turn, n, x in each_seq_peer():
            r3_copy(p, turn, n).wait_recv()
            total = total + rb3[c, x - 1, k, l].astype(F32)
        fin[c, k, l] = total
        if chunks[c][1] == LANES:
            off = (slab - over) * core
            put_gw(p, 0, fin[c, pl.ds(mult(shard * core - off, 8), shard), l])
        else:
            r4_copy(p).start()
            put_gw(p, core, fin[c, pl.ds(mult(shard * core, 8), shard), l])

    def r5(p):
        c, _, l = spot(p)
        r4_copy(p).wait_recv()
        put_gw(p, 1 - core, fin_rx[c, :, l])

    def gb_stage(stage):
        if stage == 0:
            peer = [((me ^ x, col), x - 1) for x in range(1, span)]
        elif stage == 1:
            peer = [((me, col ^ (2 * y)), span - 1 + y - 1) for y in range(1, plane)]
        else:
            peer = [(partner, span + plane - 2)]
        src = gbs.at[stage]
        return [(remote(src, gbs.at[4 + k], gb_send.at[k], gb_recv.at[k], to), k) for to, k in peer]

    def gb_go(stage):
        for copy, _ in gb_stage(stage):
            copy.start()

    def gb_sum(stage):
        total = gbs[stage]
        for copy, k in gb_stage(stage):
            copy.wait_recv()
            total = total + gbs[4 + k]
        gbs[stage + 1] = total

    last = n_chunks - 1
    if not fused:
        for c in range(n_chunks):
            for copy in w_copies(c):
                copy.wait()
            pass_a(c)
        for c in range(n_chunks):
            pass_b(c)
            pass_c(c, 0)
            pass_c(c, 1)
    else:
        gbs[0] = jnp.zeros(gbs.shape[1:], F32)
        plane_go(1)
        cores_go(0)
        a3(0).wait_recv()
        pass_a(0)
        cores_go(1)
        plane_go(2)
        pass_b(0)
        early_go(2)
        a3(1).wait_recv()
        pass_a(1)
        pass_c(0, 0)
        cores_go(2)
        pass_c(0, 1)
        r2(0, 0)
        a3(2).wait_recv()
        pass_a(2)
        r2(0, 1)
        pass_b(1, [lambda: r3(0, 0)])
        pass_c(1, 0)
        r3(0, 1)
        pass_c(1, 1)
        r2(1, 0)
        pass_b(
            2, [lambda: r2(1, 1), lambda: pass_c(2, 0), lambda: r4(0), lambda: pass_c(2, 1), lambda: r2(2, 0)]
        )
        gb_go(0)
        r3(1, 0)
        r2(2, 1)
        pass_c(3, 0)
        r3(1, 1)
        pass_c(3, 1)
        r2(3, 0)

    to_left = remote(edge.at[2], edge.at[3], edge_send.at[1], edge_recv.at[1], (me - 1, col))

    @pl.when(me == span - 1)
    def _():
        edge[3] = jnp.zeros((seqs, width), F32)

    late_gt = gates[last]

    def settle(ref, b, value):
        out = dot(pinv[...], value).astype(BF)
        ref[:, pl.ds(mult(b * STEPS, STEPS), STEPS), :] = out.reshape(seqs, STEPS, width)

    def put(b):
        settle(gtok, b, late_gt[pl.ds(mult(b * block, block), block), :width].astype(BF))

    def put_hidden(b):
        settle(hid, b, hid[:, pl.ds(mult(b * STEPS, STEPS), STEPS), :].reshape(block, width))

    def late_links(i):
        plan = {
            0: [lambda: r2(3, 1), lambda: gb_sum(0), lambda: gb_go(1)],
            1: [lambda: r3(2, 0)],
            2: [lambda: r3(2, 1), lambda: gb_sum(1), lambda: gb_go(2)],
            3: [lambda: r4(1)],
            4: [lambda: r3(3, 0), lambda: gb_sum(2)],
            5: [lambda: r3(3, 1), lambda: r5(1)],
            6: [lambda: r4(2)],
            7: [lambda: r5(2)],
        }
        for when, todo in plan.items():

            @pl.when(i == when)
            def _(todo=todo):
                for step in todo:
                    step()

    def inputs(i, pend):
        r0 = mult(i * block, block)
        put_hidden(i)
        put(jnp.maximum(i - 2, 0))
        grads = jnp.concatenate([g[pl.ds(r0, block), :] for g in gp], axis=1)
        both = dot_columns(grads, weights_of(0, 3 * width))
        own = both[:, :width]
        late = both[:, width:] * wide_keep(r0, block, width)
        late_gt[pl.ds(r0, block - seqs), :width] = own[: block - seqs] + late[seqs:]
        before = jnp.where(i == 0, rows - seqs, r0 - seqs)
        late_gt[pl.ds(mult(before, seqs), seqs), :width] = pend + late[:seqs]

        @pl.when(i == 0)
        def _():
            edge[2] = late[:seqs]

            @pl.when(me > 0)
            def _():
                to_left.start()

        if fused:
            late_links(i)
        return own[block - seqs :]

    pend = lax.fori_loop(0, blocks, inputs, jnp.zeros((seqs, width), F32))

    @pl.when(me < span - 1)
    def _():
        to_left.wait_recv()

    @pl.when(me > 0)
    def _():
        to_left.wait_send()

    late_gt[rows - seqs :, :width] = pend + edge[3]
    put(blocks - 2)
    put(blocks - 1)
    if not fused:
        for turn in (0, 1):
            for copy in gw_copies(n_chunks - 1, turn):
                copy.wait()
    else:
        for g in range(3 * width // LANES):
            gb[g * LANES : (g + 1) * LANES] = gbs[3, g : g + 1, :].reshape(LANES)
        r4(3)
        a0.wait_send()
        for c in range(n_chunks):
            a3(c).wait_send()
            for x in range(1, span):
                a1(c, x).wait_send()
                b2(c, x).wait_send()
            for y in range(1, plane):
                b1(c, y).wait_send()
        for y in range(1, plane):
            a2(last, y).wait_send()
        for p in range(len(pieces)):
            for turn in (0, 1):
                if pieces[p][0] == last:
                    r1_copy(p, turn).wait_send()
                for n, x in enumerate(orders(turn)):
                    for y in range(1, plane):
                        r2_copy(p, turn, n, y).wait_send()
                    if x:
                        r3_copy(p, turn, n).wait_send()
            if chunks[pieces[p][0]][1] != LANES:
                r4_copy(p).wait_send()
        for stage_index in range(3):
            for copy, _ in gb_stage(stage_index):
                copy.wait_send()
        r5(3)


def per_device(tokens, weights, bias, resets, upstream):
    seqs, steps, width = tokens.shape
    rows = seqs * steps
    span, peers = lax.axis_size("seq"), lax.axis_size("dp")
    chunks = cut_chunks(width)
    n_chunks = len(chunks)
    block = seqs * STEPS
    depth = 2 * width
    shard = weights.shape[0]
    slab = 2 * shard
    plane = peers // 2
    half = span // 2
    fused = shard % 8 == 0 and slab % 16 == 0 and n_chunks == 3 and steps // STEPS >= 8
    any_spec = pl.BlockSpec(memory_space=pl.ANY)
    vmem = pl.BlockSpec(memory_space=pltpu.VMEM)
    dma = pltpu.SemaphoreType.DMA
    vm = pltpu.VMEM
    held = {
        "joined": vm((rows, depth), BF),
        "upt": vm((rows, width), BF),
        "qf": vm((rows, 2 * LANES), F32),
        "keepb": vm((rows, LANES), F32),
        "perm": vm((block, block), BF),
        "pinv": vm((block, block), BF),
        "summ": vm((span, 3 * seqs, width), F32),
        "edge": vm((4, seqs, width), F32),
        "in_sem": dma((2,)),
        "sum_send": dma((n_chunks, span - 1)),
        "sum_recv": dma((n_chunks, span - 1)),
        "edge_send": dma((2,)),
        "edge_recv": dma((2,)),
    }
    for c, (_, cw) in enumerate(chunks):
        held[f"gates{c}"] = vm((rows, 3 * cw), F32)
        held[f"gp{c}"] = vm((rows, 3 * cw), BF)
    if fused:
        gw_shape, gw_spec = (shard, 3 * width), vmem
        piece = (half * plane, slab, TRIO)
        held |= {
            "wv": vm((span, plane, slab, 3 * width), BF),
            "cbuf": vm((2, *piece), F32),
            "own16": vm((shard, 3 * width), BF),
            "pair": vm((2, shard, 3 * width), F32),
            "sb1": vm((2, *piece), BF),
            "rb1": vm((n_chunks, 2, *piece), BF),
            "rb2": vm((n_chunks, 2, half, plane - 1, slab, TRIO), BF),
            "own2": vm((n_chunks, 2, half, slab, TRIO), F32),
            "rb3": vm((n_chunks, span - 1, slab, TRIO), BF),
            "fin": vm((n_chunks, slab, TRIO), F32),
            "fin_rx": vm((n_chunks, shard, TRIO), F32),
            "gbs": vm((4 + span + plane - 1, 16, LANES), F32),
            "w_sem": dma((1,)),
            "a0_sem": dma((2,)),
            "a1_send": dma((n_chunks, span - 1)),
            "a1_recv": dma((n_chunks, span - 1)),
            "a2_send": dma((n_chunks, plane - 1)),
            "a2_recv": dma((n_chunks, plane - 1)),
            "b1_send": dma((n_chunks, plane - 1)),
            "b1_recv": dma((n_chunks, plane - 1)),
            "b2_send": dma((n_chunks, span - 1)),
            "b2_recv": dma((n_chunks, span - 1)),
            "a3_sem": dma((n_chunks, 2)),
            "r1_send": dma((n_chunks + 1, 2)),
            "r1_recv": dma((n_chunks + 1, 2)),
            "r2_send": dma((n_chunks + 1, 2, half, plane - 1)),
            "r2_recv": dma((n_chunks + 1, 2, half, plane - 1)),
            "r3_send": dma((n_chunks + 1, span - 1)),
            "r3_recv": dma((n_chunks + 1, span - 1)),
            "r4_sem": dma((n_chunks + 1, 2)),
            "gb_send": dma((span + plane - 1,)),
            "gb_recv": dma((span + plane - 1,)),
        }
    else:
        weights = lax.all_gather(weights, ("seq", "dp"), axis=0, tiled=True)
        gw_shape, gw_spec = (depth, 3 * width), any_spec
        held |= {
            "wv": vm((depth, 3 * width), BF),
            "cbuf": vm((2, depth // 2, 2 * TRIO), F32),
            "w_sem": dma((n_chunks, 3, 2)),
        }
    hid, gtok, gw, gb = pl.pallas_call(
        functools.partial(layer_kernel, span, peers, fused, chunks, tuple(held)),
        out_shape=(
            vm(tokens.shape, BF),
            vm(tokens.shape, BF),
            vm(gw_shape, F32) if fused else jax.ShapeDtypeStruct(gw_shape, F32),
            vm((3 * width,), F32) if fused else jax.ShapeDtypeStruct((3 * width,), F32),
        ),
        in_specs=[any_spec, any_spec, vmem, vmem, any_spec],
        out_specs=(vmem, vmem, gw_spec, vmem),
        scratch_shapes=list(held.values()),
        compiler_params=pltpu.CompilerParams(
            collective_id=0, has_side_effects=True, vmem_limit_bytes=VMEM_BYTES
        ),
        name="layer",
    )(tokens, weights, bias, resets, upstream)
    if not fused:
        gw = lax.psum_scatter(gw, ("seq", "dp"), scatter_dimension=0, tiled=True)
        gb = lax.psum(gb, ("seq", "dp"))
    return hid, gtok, gw, gb


def solution(mesh):
    spread = P("dp", "seq", None)
    rows = P(("seq", "dp"), None)
    return jax.shard_map(
        per_device,
        mesh=mesh,
        in_specs=(spread, rows, P(), P("dp", "seq"), spread),
        out_specs=(spread, spread, rows, P()),
        check_vma=False,
    )
```

```python
import functools
import types

import jax
import jax.numpy as jnp
from jax import lax
from jax.experimental import pallas as pl
from jax.experimental.pallas import tpu as pltpu
from jax.sharding import PartitionSpec as P

MESH = pl.DeviceIdType.MESH
BF = jnp.bfloat16
F32 = jnp.float32
LANES = 128
TRIO = 3 * LANES
STEPS = 32
TWO = 16
VMEM_BYTES = 56 << 20
EARLY = (0, 16, 16)


def cut_chunks(width):
    tiles = width // LANES
    chunks, at = [], 0
    if tiles % 2:
        chunks.append((0, LANES))
        at = LANES
    while at < width:
        chunks.append((at, 2 * LANES))
        at += 2 * LANES
    return chunks


def dot(a, b):
    return jnp.dot(a, b, preferred_element_type=F32)


def dot_rows(a, b):
    return lax.dot_general(a, b, (((0,), (0,)), ((), ())), preferred_element_type=F32)


def dot_columns(a, b):
    return lax.dot_general(a, b, (((1,), (1,)), ((), ())), preferred_element_type=F32)


def layer_kernel(
    span, peers, fused, chunks, names,
    tok, wts, bias, resets, up,
    hid, gtok, gw, gb,
    *scratch,
):
    held = types.SimpleNamespace(**dict(zip(names, scratch)))
    joined, upt, wv, qf, keepb = held.joined, held.upt, held.wv, held.qf, held.keepb
    perm, pinv, cbuf, summ, edge = held.perm, held.pinv, held.cbuf, held.summ, held.edge
    in_sem, w_sem = held.in_sem, held.w_sem
    sum_send, sum_recv = held.sum_send, held.sum_recv
    edge_send, edge_recv = held.edge_send, held.edge_recv
    gates = [getattr(held, f"gates{c}") for c in range(len(chunks))]
    gp = [getattr(held, f"gp{c}") for c in range(len(chunks))]
    seqs, steps, width = tok.shape
    rows = seqs * steps
    block = seqs * STEPS
    blocks = steps // STEPS
    depth = 2 * width
    half_rows = depth // 2
    n_chunks = len(chunks)
    me = lax.axis_index("seq")
    col = lax.axis_index("dp")
    core = col & 1
    place = col >> 1
    plane = peers // 2
    slab = depth // (span * plane)
    shard = slab // 2
    over = -(-shard // 16) * 16
    partner = (me, col ^ 1)
    pieces = [(c, 0, TRIO) for c in range(len(chunks))]
    if fused:
        pieces[-1:] = [(len(chunks) - 1, 2 * LANES, LANES), (len(chunks) - 1, 0, 2 * LANES)]
    if fused:
        own16, pair, sb1, rb1, rb2 = held.own16, held.pair, held.sb1, held.rb1, held.rb2
        own2, rb3, fin, fin_rx, gbs = held.own2, held.rb3, held.fin, held.fin_rx, held.gbs
        a0_sem, a3_sem, r4_sem = held.a0_sem, held.a3_sem, held.r4_sem
        b1_send, b1_recv, b2_send, b2_recv = held.b1_send, held.b1_recv, held.b2_send, held.b2_recv
        a1_send, a1_recv, a2_send, a2_recv = held.a1_send, held.a1_recv, held.a2_send, held.a2_recv
        r1_send, r1_recv, r2_send, r2_recv = held.r1_send, held.r1_recv, held.r2_send, held.r2_recv
        r3_send, r3_recv, gb_send, gb_recv = held.r3_send, held.r3_recv, held.gb_send, held.gb_recv

    def remote(src, dst, send, recv, to):
        return pltpu.make_async_remote_copy(
            src_ref=src, dst_ref=dst, send_sem=send, recv_sem=recv,
            device_id=to, device_id_type=MESH,
        )

    def mult(v, m):
        return pl.multiple_of(v, m)

    in_t = pltpu.make_async_copy(tok, hid, in_sem.at[0])
    in_u = pltpu.make_async_copy(up, gtok, in_sem.at[1])
    if fused:
        in_w = pltpu.make_async_copy(wts, own16, w_sem.at[0])
        in_w.start()
    in_t.start()
    in_u.start()

    barrier = pltpu.get_barrier_semaphore()
    friends = [(lax.rem(me + k, span), col) for k in range(1, span)]
    if fused:
        friends += [(me, col ^ (2 * y)) for y in range(1, plane)] + [partner]
    for friend in friends:
        pl.semaphore_signal(barrier, inc=1, device_id=friend, device_id_type=MESH)
    pl.semaphore_wait(barrier, len(friends))

    def carried(c, who):
        at, cw = chunks[c]
        if cw == LANES:
            return over, mult((slab - over) * who, 16), 3 * at
        return slab, 0, mult(3 * at + TRIO * who, LANES)

    def part(c, who, planes, places):
        count, r0, c0 = carried(c, who)
        return wv.at[planes, places, pl.ds(r0, count), pl.ds(c0, TRIO)]

    def early(c, places):
        _, r0, c0 = carried(c, core)
        return wv.at[me, places, pl.ds(r0, EARLY[c]), pl.ds(c0, TRIO)]

    def rest(c, planes):
        count, r0, c0 = carried(c, core)
        return wv.at[planes, place, pl.ds(mult(r0 + EARLY[c], 16), count - EARLY[c]), pl.ds(c0, TRIO)]

    def a1(c, x):
        here = rest(c, me)
        return remote(here, here, a1_send.at[c, x - 1], a1_recv.at[c, x - 1], (me ^ x, col))

    def a2(c, y):
        here = rest(c, slice(None))
        return remote(here, here, a2_send.at[c, y - 1], a2_recv.at[c, y - 1], (me, col ^ (2 * y)))

    def b1(c, y):
        here = early(c, place)
        return remote(here, here, b1_send.at[c, y - 1], b1_recv.at[c, y - 1], (me, col ^ (2 * y)))

    def b2(c, x):
        here = early(c, slice(None))
        return remote(here, here, b2_send.at[c, x - 1], b2_recv.at[c, x - 1], (me ^ x, col))

    def a3(c):
        if chunks[c][1] == LANES:
            here = wv.at[
                :, :, pl.ds(mult(over * core, 16), slab - over), pl.ds(3 * chunks[c][0], TRIO)
            ]
        else:
            here = part(c, core, slice(None), slice(None))
        return remote(here, here, a3_sem.at[c, 0], a3_sem.at[c, 1], partner)

    def early_go(c):
        if not EARLY[c]:
            return
        for y in range(1, plane):
            b1(c, y).wait_recv()
        for x in range(1, span):
            b2(c, x).start()

    def plane_go(c):
        for x in range(1, span):
            a1(c, x).wait_recv()
        if c < n_chunks - 1:
            for x in range(1, span):
                a1(c + 1, x).start()
        for y in range(1, plane):
            if c:
                a2(c - 1, y).wait_send()
        for y in range(1, plane):
            a2(c, y).start()

    def cores_go(c):
        for y in range(1, plane):
            a2(c, y).wait_recv()
        for x in range(1, span):
            if EARLY[c]:
                b2(c, x).wait_recv()
        a3(c).start()

    def w_copies(c):
        at, cw = chunks[c]
        return [
            pltpu.make_async_copy(
                wts.at[:, pl.ds(g * width + at + h * LANES, LANES)],
                wv.at[:, pl.ds(3 * at + h * TRIO + g * LANES, LANES)],
                w_sem.at[c, g, h],
            )
            for g in range(3)
            for h in range(cw // LANES)
        ]

    if fused:
        in_w.wait()
        pair[core] = own16[...].astype(F32)
        a0 = remote(pair.at[core], pair.at[core], a0_sem.at[0], a0_sem.at[1], partner)
        a0.start()
    else:
        for c in range(n_chunks):
            for copy in w_copies(c):
                copy.start()

    r = lax.broadcasted_iota(jnp.int32, (block, block), 0)
    q = lax.broadcasted_iota(jnp.int32, (block, block), 1)
    perm[...] = (((q & 31) == (r >> 3)) & ((q >> 5) == (r & 7))).astype(F32).astype(BF)
    pinv[...] = (((r & 31) == (q >> 3)) & ((r >> 5) == (q & 7))).astype(F32).astype(BF)

    if fused:
        a0.wait_recv()
        for c, (at, cw) in enumerate(chunks):
            count, top, left = carried(c, core)
            for g in range(3):
                lane = g * width + at + (0 if cw == LANES else core * LANES)
                lanes = pl.ds(mult(lane, LANES), LANES)
                both = jnp.concatenate([pair[0, :, lanes], pair[1, :, lanes]], axis=0)
                if count < slab:
                    both = jnp.where(core == 0, both[:count], both[slab - count :])
                to = pl.ds(mult(left + g * LANES, LANES), LANES)
                wv[me, place, pl.ds(top, count), to] = both.astype(BF)
            if c == 0:
                for x in range(1, span):
                    a1(0, x).start()
            if EARLY[c]:
                for y in range(1, plane):
                    b1(c, y).start()

    keep = 1.0 - resets[...].astype(F32)
    tiled = jnp.broadcast_to(keep[None], (STEPS, seqs, steps)).reshape(block, steps)
    row_t = lax.broadcasted_iota(jnp.int32, (block, steps), 0) >> 3
    lane_t = lax.broadcasted_iota(jnp.int32, (block, steps), 1)
    ones = jnp.ones((steps, LANES), BF)
    for b in range(blocks):
        picked = jnp.where(lane_t == row_t + b * STEPS, tiled, 0.0).astype(BF)
        keepb[b * block : (b + 1) * block, :] = dot(picked, ones)

    def wide_keep(at, count, lanes):
        k = keepb[pl.ds(at, count), :]
        return jnp.concatenate([k] * (lanes // LANES), axis=1)

    in_t.wait()
    last_rows = hid[:, steps - STEPS :, :].reshape(block, width)
    edge[0] = dot(perm[block - TWO :, :], last_rows)[TWO - seqs :]
    to_right = remote(edge.at[0], edge.at[1], edge_send.at[0], edge_recv.at[0], (me + 1, col))

    @pl.when(me < span - 1)
    def _():
        to_right.start()

    @pl.when(me == 0)
    def _():
        edge[1] = jnp.zeros((seqs, width), F32)

    in_u.wait()
    if fused:
        early_go(0)
        plane_go(0)
        early_go(1)

    def stage(b, last):
        at = mult(b * block, block)
        src = hid[:, pl.ds(mult(b * STEPS, STEPS), STEPS), :].reshape(block, width)
        now = dot(perm[...], src)
        before = jnp.concatenate([last, now[: block - seqs]], axis=0)
        before = before * wide_keep(at, block, width)
        joined[pl.ds(at, block), :width] = now.astype(BF)
        joined[pl.ds(at, block), width:] = before.astype(BF)
        src = gtok[:, pl.ds(mult(b * STEPS, STEPS), STEPS), :].reshape(block, width)
        upt[pl.ds(at, block), :] = dot(perm[...], src).astype(BF)
        return now[block - seqs :]

    lax.fori_loop(0, blocks, stage, jnp.zeros((seqs, width), F32))

    @pl.when(me > 0)
    def _():
        to_right.wait_recv()

    @pl.when(me < span - 1)
    def _():
        to_right.wait_send()

    first = jnp.concatenate([edge[1], joined[:TWO, :width].astype(F32)[:seqs]], axis=0)
    joined[:TWO, width:] = (first * wide_keep(0, TWO, width)).astype(BF)

    def weights_of(base, count):
        if fused:
            return wv[:, :, :, base : base + count].reshape(depth, count)
        return wv[:, base : base + count]

    def pass_a(c):
        at, cw = chunks[c]
        base = 3 * at
        size = 2 * block if blocks % 2 == 0 else block
        halves = range(cw // LANES)

        def bias_rows(g, h):
            lane = g * width + at + h * LANES
            return jnp.broadcast_to(bias[lane : lane + LANES].reshape(1, LANES), (TWO, LANES))

        bias_z = [bias_rows(0, h) for h in halves]
        bias_f = [0.5 * bias_rows(1, h) for h in halves]
        bias_o = [0.5 * bias_rows(2, h) for h in halves]

        def body(i, carry):
            carry = [list(v) for v in carry]
            r0 = mult(i * size, size)
            pre = dot(joined[pl.ds(r0, size), :], weights_of(base, 3 * cw))
            for j in range(size // TWO):
                sl = pl.ds(r0 + j * TWO, TWO)
                k = keepb[sl, :]
                for h in halves:
                    zc, fc, oc = (h * TRIO + g * LANES for g in range(3))
                    now = pre[j * TWO : (j + 1) * TWO]
                    z = jnp.tanh(now[:, zc : zc + LANES] + bias_z[h])
                    f = 0.5 * jnp.tanh(0.5 * now[:, fc : fc + LANES] + bias_f[h]) + 0.5
                    o = 0.5 * jnp.tanh(0.5 * now[:, oc : oc + LANES] + bias_o[h]) + 0.5
                    gates[c][sl, zc : zc + LANES] = z
                    gates[c][sl, fc : fc + LANES] = f
                    gates[c][sl, oc : oc + LANES] = o
                    g = upt[sl, at + h * LANES : at + (h + 1) * LANES].astype(F32)
                    eff = f * k
                    fresh = (1.0 - f) * z
                    src = g * o
                    gain, state, back = carry[h]
                    for m in (0, seqs):
                        gain = gain * eff[m : m + seqs]
                        state = state * eff[m : m + seqs] + fresh[m : m + seqs]
                        back = back + gain * src[m : m + seqs]
                    carry[h] = [gain, state, back]
            return tuple(tuple(v) for v in carry)

        zero = jnp.zeros((seqs, LANES), F32)
        one = jnp.ones((seqs, LANES), F32)
        done = lax.fori_loop(0, rows // size, body, tuple((one, zero, zero) for _ in halves))
        for h in halves:
            cols = slice(at + h * LANES, at + (h + 1) * LANES)
            for v in range(3):
                summ[me, v * seqs : (v + 1) * seqs, cols] = done[h][v]
        for k in range(1, span):
            exchange(c, k).start()

    def exchange(c, k):
        at, cw = chunks[c]
        here = summ.at[me, :, pl.ds(at, cw)]
        return remote(
            here, here, sum_send.at[c, k - 1], sum_recv.at[c, k - 1], (lax.rem(me + k, span), col)
        )

    def pass_b(c, between=()):
        at, cw = chunks[c]
        halves = range(cw // LANES)
        for k in range(1, span):
            exchange(c, k).wait()
        enter, leave = [], []
        for h in halves:
            cols = slice(at + h * LANES, at + (h + 1) * LANES)
            state = jnp.zeros((seqs, LANES), F32)
            for s in range(span - 1):
                new = summ[s, seqs : 2 * seqs, cols] + summ[s, :seqs, cols] * state
                state = jnp.where(s < me, new, state)
            enter.append(state)
            back = jnp.zeros((seqs, LANES), F32)
            for s in range(span - 1, 0, -1):
                new = summ[s, 2 * seqs :, cols] + summ[s, :seqs, cols] * back
                back = jnp.where(s > me, new, back)
            leave.append(back)

        def forward(i, carry):
            cells, sums = list(carry[0]), list(carry[1])
            r0 = mult(i * block, block)
            for j in range(block // TWO):
                sl = pl.ds(r0 + j * TWO, TWO)
                k = keepb[sl, :]
                for h in halves:
                    zc, fc, oc = (h * TRIO + g * LANES for g in range(3))
                    z = gates[c][sl, zc : zc + LANES]
                    f = gates[c][sl, fc : fc + LANES]
                    o = gates[c][sl, oc : oc + LANES]
                    lanes = slice(at + h * LANES, at + (h + 1) * LANES)
                    g = upt[sl, lanes].astype(F32)
                    eff = f * k
                    rest = 1.0 - f
                    fresh = rest * z
                    c0 = eff[:seqs] * cells[h] + fresh[:seqs]
                    c1 = eff[seqs:] * c0 + fresh[seqs:]
                    cell = jnp.concatenate([c0, c1], axis=0)
                    prev = jnp.concatenate([cells[h], c0], axis=0)
                    cells[h] = c1
                    hid[j // 2, pl.ds(mult(i * STEPS + j % 2 * TWO, TWO), TWO), lanes] = (
                        o * cell
                    ).astype(BF)
                    src = g * o
                    go = src * cell * (1.0 - o)
                    gp[c][sl, oc : oc + LANES] = go.astype(BF)
                    sums[h] = sums[h] + go
                    gates[c][sl, zc : zc + LANES] = rest * (1.0 - z * z)
                    gates[c][sl, fc : fc + LANES] = eff
                    gates[c][sl, oc : oc + LANES] = src
                    qf[sl, h * LANES : (h + 1) * LANES] = (prev * k - z) * (f * rest)
            return tuple(cells), tuple(sums)

        zero = jnp.zeros((TWO, LANES), F32)
        zeros = tuple(zero for _ in halves)
        _, sum_o = lax.fori_loop(0, blocks, forward, (tuple(enter), zeros))

        for step in between:
            step()

        def backward(n, carry):
            heads, sums_z, sums_f = (list(v) for v in carry)
            r0 = mult((blocks - 1 - n) * block, block)
            for j in range(block // TWO - 1, -1, -1):
                sl = pl.ds(r0 + j * TWO, TWO)
                for h in halves:
                    zc, fc, oc = (h * TRIO + g * LANES for g in range(3))
                    eff = gates[c][sl, fc : fc + LANES]
                    src = gates[c][sl, oc : oc + LANES]
                    g1 = src[seqs:] + heads[h]
                    g0 = src[:seqs] + eff[seqs:] * g1
                    heads[h] = eff[:seqs] * g0
                    gc = jnp.concatenate([g0, g1], axis=0)
                    gz = gc * gates[c][sl, zc : zc + LANES]
                    gf = gc * qf[sl, h * LANES : (h + 1) * LANES]
                    gp[c][sl, zc : zc + LANES] = gz.astype(BF)
                    gp[c][sl, fc : fc + LANES] = gf.astype(BF)
                    sums_z[h] = sums_z[h] + gz
                    sums_f[h] = sums_f[h] + gf
            return tuple(heads), tuple(sums_z), tuple(sums_f)

        _, sum_z, sum_f = lax.fori_loop(0, blocks, backward, (tuple(leave), zeros, zeros))
        for h in halves:
            for g, total in enumerate((sum_z, sum_f, sum_o)):
                line = jnp.sum(total[h], axis=0, keepdims=True)
                if fused:
                    tile = g * (width // LANES) + at // LANES + h
                    gbs[0, tile : tile + 1, :] = line
                else:
                    lane = g * width + at + h * LANES
                    gb[lane : lane + LANES] = line.reshape(LANES)

    def gw_copies(c, turn):
        at, cw = chunks[c]
        return [
            pltpu.make_async_copy(
                cbuf.at[turn, :, pl.ds(h * TRIO + g * LANES, LANES)],
                gw.at[pl.ds(turn * half_rows, half_rows), pl.ds(g * width + at + h * LANES, LANES)],
                w_sem.at[c, g, h],
            )
            for g in range(3)
            for h in range(cw // LANES)
        ]

    def pass_c(p, turn):
        c, lane, lanes = pieces[p]
        at, cw = chunks[c]
        if fused:
            r0 = mult(((me // (span // 2)) ^ 1 ^ turn) * half_rows, LANES)
            if p and pieces[p - 1][0] != c:
                r1_copy(p - 1, turn).wait_send()
            right = [
                gp[c][:, h * TRIO + lane : h * TRIO + lane + lanes] for h in range(cw // LANES)
            ]
            result = dot_rows(joined[:, pl.ds(r0, half_rows)], jnp.concatenate(right, axis=1))
            result = result.reshape(-1, slab, result.shape[-1])
            count = carried(c, 0)[0]
            if cw == LANES:
                zero, one = result[:, :count], result[:, slab - count :]
            else:
                zero, one = result[:, :, :lanes], result[:, :, lanes:]
            cols = slice(lane, lane + lanes)
            cbuf[turn, :, :count, cols] = jnp.where(core == 0, zero, one)
            sb1[turn, :, :count, cols] = jnp.where(core == 0, one, zero).astype(BF)
            r1_copy(p, turn).start()
        else:
            if c:
                for copy in gw_copies(c - 1, turn):
                    copy.wait()
            cbuf[turn, :, : 3 * cw] = dot_rows(
                joined[:, turn * half_rows : (turn + 1) * half_rows], gp[c][...]
            )
            for copy in gw_copies(c, turn):
                copy.start()

    def spot(p):
        c, lane, lanes = pieces[p]
        return c, pl.ds(0, carried(c, 0)[0]), pl.ds(lane, lanes)

    def orders(turn):
        half = span // 2
        return list(range(half, span)) if turn == 0 else list(range(half - 1, -1, -1))

    def r1_copy(p, turn):
        c, k, l = spot(p)
        return remote(
            sb1.at[turn, :, k, l], rb1.at[c, turn, :, k, l],
            r1_send.at[p, turn], r1_recv.at[p, turn], partner,
        )

    def r2_copy(p, turn, n, y):
        c, k, l = spot(p)
        x = orders(turn)[n]
        index = ((me ^ x) % (span // 2)) * plane + (place ^ y)
        return remote(
            rb1.at[c, turn, index, k, l], rb2.at[c, turn, n, y - 1, k, l],
            r2_send.at[p, turn, n, y - 1], r2_recv.at[p, turn, n, y - 1], (me, col ^ (2 * y)),
        )

    def r2(p, turn):
        r1_copy(p, turn).wait_recv()
        c, k, l = spot(p)
        for n, x in enumerate(orders(turn)):
            for y in range(plane - 1, -1, -1):
                index = ((me ^ x) % (span // 2)) * plane + (place ^ y)
                total = cbuf[turn, index, k, l] + rb1[c, turn, index, k, l].astype(F32)
                if y:
                    rb1[c, turn, index, k, l] = total.astype(BF)
                    r2_copy(p, turn, n, y).start()
                else:
                    own2[c, turn, n, k, l] = total

    def r3_copy(p, turn, n):
        c, k, l = spot(p)
        x = orders(turn)[n]
        return remote(
            rb2.at[c, turn, n, 0, k, l], rb3.at[c, x - 1, k, l], r3_send.at[p, x - 1],
            r3_recv.at[p, x - 1], (me ^ x, col),
        )

    def r3(p, turn):
        c, k, l = spot(p)
        for n, x in enumerate(orders(turn)):
            total = own2[c, turn, n, k, l]
            for y in range(1, plane):
                r2_copy(p, turn, n, y).wait_recv()
                total = total + rb2[c, turn, n, y - 1, k, l].astype(F32)
            if x:
                rb2[c, turn, n, 0, k, l] = total.astype(BF)
                r3_copy(p, turn, n).start()
            else:
                own2[c, turn, n, k, l] = total

    def r4_copy(p):
        c, _, l = spot(p)
        return remote(
            fin.at[c, pl.ds(mult(shard * (1 - core), 8), shard), l], fin_rx.at[c, :, l],
            r4_sem.at[p, 0], r4_sem.at[p, 1], partner,
        )

    def put_gw(p, tile, value):
        c, first, lanes = pieces[p]
        for g in range(lanes // LANES):
            gate = first // LANES + g
            lane = mult(gate * width + chunks[c][0] + tile * LANES, LANES)
            gw[:, pl.ds(lane, LANES)] = value[:, g * LANES : (g + 1) * LANES]

    def each_seq_peer():
        return [(turn, n, x) for turn in (0, 1) for n, x in enumerate(orders(turn)) if x]

    def r4(p):
        c, k, l = spot(p)
        total = own2[c, 1, span // 2 - 1, k, l]
        for turn, n, x in each_seq_peer():
            r3_copy(p, turn, n).wait_recv()
            total = total + rb3[c, x - 1, k, l].astype(F32)
        fin[c, k, l] = total
        if chunks[c][1] == LANES:
            off = (slab - over) * core
            put_gw(p, 0, fin[c, pl.ds(mult(shard * core - off, 8), shard), l])
        else:
            r4_copy(p).start()
            put_gw(p, core, fin[c, pl.ds(mult(shard * core, 8), shard), l])

    def r5(p):
        c, _, l = spot(p)
        r4_copy(p).wait_recv()
        put_gw(p, 1 - core, fin_rx[c, :, l])

    def gb_stage(stage):
        if stage == 0:
            peer = [((me ^ x, col), x - 1) for x in range(1, span)]
        elif stage == 1:
            peer = [((me, col ^ (2 * y)), span - 1 + y - 1) for y in range(1, plane)]
        else:
            peer = [(partner, span + plane - 2)]
        src = gbs.at[stage]
        return [(remote(src, gbs.at[4 + k], gb_send.at[k], gb_recv.at[k], to), k) for to, k in peer]

    def gb_go(stage):
        for copy, _ in gb_stage(stage):
            copy.start()

    def gb_sum(stage):
        total = gbs[stage]
        for copy, k in gb_stage(stage):
            copy.wait_recv()
            total = total + gbs[4 + k]
        gbs[stage + 1] = total

    last = n_chunks - 1
    if not fused:
        for c in range(n_chunks):
            for copy in w_copies(c):
                copy.wait()
            pass_a(c)
        for c in range(n_chunks):
            pass_b(c)
            pass_c(c, 0)
            pass_c(c, 1)
    else:
        gbs[0] = jnp.zeros(gbs.shape[1:], F32)
        plane_go(1)
        cores_go(0)
        a3(0).wait_recv()
        pass_a(0)
        cores_go(1)
        plane_go(2)
        pass_b(0)
        early_go(2)
        a3(1).wait_recv()
        pass_a(1)
        pass_c(0, 0)
        cores_go(2)
        pass_c(0, 1)
        r2(0, 0)
        a3(2).wait_recv()
        pass_a(2)
        r2(0, 1)
        pass_b(1, [lambda: r3(0, 0)])
        pass_c(1, 0)
        r3(0, 1)
        pass_c(1, 1)
        r2(1, 0)
        pass_b(
            2, [lambda: r2(1, 1), lambda: pass_c(2, 0), lambda: r4(0), lambda: pass_c(2, 1), lambda: r2(2, 0)]
        )
        gb_go(0)
        r3(1, 0)
        r2(2, 1)
        pass_c(3, 0)
        r3(1, 1)
        pass_c(3, 1)
        r2(3, 0)

    to_left = remote(edge.at[2], edge.at[3], edge_send.at[1], edge_recv.at[1], (me - 1, col))

    @pl.when(me == span - 1)
    def _():
        edge[3] = jnp.zeros((seqs, width), F32)

    late_gt = gates[last]

    def settle(ref, b, value):
        out = dot(pinv[...], value).astype(BF)
        ref[:, pl.ds(mult(b * STEPS, STEPS), STEPS), :] = out.reshape(seqs, STEPS, width)

    def put(b):
        settle(gtok, b, late_gt[pl.ds(mult(b * block, block), block), :width].astype(BF))

    def put_hidden(b):
        settle(hid, b, hid[:, pl.ds(mult(b * STEPS, STEPS), STEPS), :].reshape(block, width))

    def late_links(i):
        plan = {
            0: [lambda: r2(3, 1), lambda: gb_sum(0), lambda: gb_go(1)],
            1: [lambda: r3(2, 0)],
            2: [lambda: r3(2, 1), lambda: gb_sum(1), lambda: gb_go(2)],
            3: [lambda: r4(1)],
            4: [lambda: r3(3, 0), lambda: gb_sum(2)],
            5: [lambda: r3(3, 1), lambda: r5(1)],
            6: [lambda: r4(2)],
            7: [lambda: r5(2)],
        }
        for when, todo in plan.items():

            @pl.when(i == when)
            def _(todo=todo):
                for step in todo:
                    step()

    def inputs(i, pend):
        r0 = mult(i * block, block)
        put_hidden(i)
        put(jnp.maximum(i - 2, 0))
        grads = jnp.concatenate([g[pl.ds(r0, block), :] for g in gp], axis=1)
        both = dot_columns(grads, weights_of(0, 3 * width))
        own = both[:, :width]
        late = both[:, width:] * wide_keep(r0, block, width)
        late_gt[pl.ds(r0, block - seqs), :width] = own[: block - seqs] + late[seqs:]
        before = jnp.where(i == 0, rows - seqs, r0 - seqs)
        late_gt[pl.ds(mult(before, seqs), seqs), :width] = pend + late[:seqs]

        @pl.when(i == 0)
        def _():
            edge[2] = late[:seqs]

            @pl.when(me > 0)
            def _():
                to_left.start()

        if fused:
            late_links(i)
        return own[block - seqs :]

    pend = lax.fori_loop(0, blocks, inputs, jnp.zeros((seqs, width), F32))

    @pl.when(me < span - 1)
    def _():
        to_left.wait_recv()

    @pl.when(me > 0)
    def _():
        to_left.wait_send()

    late_gt[rows - seqs :, :width] = pend + edge[3]
    put(blocks - 2)
    put(blocks - 1)
    if not fused:
        for turn in (0, 1):
            for copy in gw_copies(n_chunks - 1, turn):
                copy.wait()
    else:
        for g in range(3 * width // LANES):
            gb[g * LANES : (g + 1) * LANES] = gbs[3, g : g + 1, :].reshape(LANES)
        r4(3)
        a0.wait_send()
        for c in range(n_chunks):
            a3(c).wait_send()
            for x in range(1, span):
                a1(c, x).wait_send()
                if EARLY[c]:
                    b2(c, x).wait_send()
            for y in range(1, plane):
                if EARLY[c]:
                    b1(c, y).wait_send()
        for y in range(1, plane):
            a2(last, y).wait_send()
        for p in range(len(pieces)):
            for turn in (0, 1):
                if pieces[p][0] == last:
                    r1_copy(p, turn).wait_send()
                for n, x in enumerate(orders(turn)):
                    for y in range(1, plane):
                        r2_copy(p, turn, n, y).wait_send()
                    if x:
                        r3_copy(p, turn, n).wait_send()
            if chunks[pieces[p][0]][1] != LANES:
                r4_copy(p).wait_send()
        for stage_index in range(3):
            for copy, _ in gb_stage(stage_index):
                copy.wait_send()
        r5(3)


def per_device(tokens, weights, bias, resets, upstream):
    seqs, steps, width = tokens.shape
    rows = seqs * steps
    span, peers = lax.axis_size("seq"), lax.axis_size("dp")
    chunks = cut_chunks(width)
    n_chunks = len(chunks)
    block = seqs * STEPS
    depth = 2 * width
    shard = weights.shape[0]
    slab = 2 * shard
    plane = peers // 2
    half = span // 2
    fused = shard % 8 == 0 and slab % 16 == 0 and n_chunks == 3 and steps // STEPS >= 8
    any_spec = pl.BlockSpec(memory_space=pl.ANY)
    vmem = pl.BlockSpec(memory_space=pltpu.VMEM)
    dma = pltpu.SemaphoreType.DMA
    vm = pltpu.VMEM
    held = {
        "joined": vm((rows, depth), BF),
        "upt": vm((rows, width), BF),
        "qf": vm((rows, 2 * LANES), F32),
        "keepb": vm((rows, LANES), F32),
        "perm": vm((block, block), BF),
        "pinv": vm((block, block), BF),
        "summ": vm((span, 3 * seqs, width), F32),
        "edge": vm((4, seqs, width), F32),
        "in_sem": dma((2,)),
        "sum_send": dma((n_chunks, span - 1)),
        "sum_recv": dma((n_chunks, span - 1)),
        "edge_send": dma((2,)),
        "edge_recv": dma((2,)),
    }
    for c, (_, cw) in enumerate(chunks):
        held[f"gates{c}"] = vm((rows, 3 * cw), F32)
        held[f"gp{c}"] = vm((rows, 3 * cw), BF)
    if fused:
        gw_shape, gw_spec = (shard, 3 * width), vmem
        piece = (half * plane, slab, TRIO)
        held |= {
            "wv": vm((span, plane, slab, 3 * width), BF),
            "cbuf": vm((2, *piece), F32),
            "own16": vm((shard, 3 * width), BF),
            "pair": vm((2, shard, 3 * width), F32),
            "sb1": vm((2, *piece), BF),
            "rb1": vm((n_chunks, 2, *piece), BF),
            "rb2": vm((n_chunks, 2, half, plane - 1, slab, TRIO), BF),
            "own2": vm((n_chunks, 2, half, slab, TRIO), F32),
            "rb3": vm((n_chunks, span - 1, slab, TRIO), BF),
            "fin": vm((n_chunks, slab, TRIO), F32),
            "fin_rx": vm((n_chunks, shard, TRIO), F32),
            "gbs": vm((4 + span + plane - 1, 16, LANES), F32),
            "w_sem": dma((1,)),
            "a0_sem": dma((2,)),
            "a1_send": dma((n_chunks, span - 1)),
            "a1_recv": dma((n_chunks, span - 1)),
            "a2_send": dma((n_chunks, plane - 1)),
            "a2_recv": dma((n_chunks, plane - 1)),
            "b1_send": dma((n_chunks, plane - 1)),
            "b1_recv": dma((n_chunks, plane - 1)),
            "b2_send": dma((n_chunks, span - 1)),
            "b2_recv": dma((n_chunks, span - 1)),
            "a3_sem": dma((n_chunks, 2)),
            "r1_send": dma((n_chunks + 1, 2)),
            "r1_recv": dma((n_chunks + 1, 2)),
            "r2_send": dma((n_chunks + 1, 2, half, plane - 1)),
            "r2_recv": dma((n_chunks + 1, 2, half, plane - 1)),
            "r3_send": dma((n_chunks + 1, span - 1)),
            "r3_recv": dma((n_chunks + 1, span - 1)),
            "r4_sem": dma((n_chunks + 1, 2)),
            "gb_send": dma((span + plane - 1,)),
            "gb_recv": dma((span + plane - 1,)),
        }
    else:
        weights = lax.all_gather(weights, ("seq", "dp"), axis=0, tiled=True)
        gw_shape, gw_spec = (depth, 3 * width), any_spec
        held |= {
            "wv": vm((depth, 3 * width), BF),
            "cbuf": vm((2, depth // 2, 2 * TRIO), F32),
            "w_sem": dma((n_chunks, 3, 2)),
        }
    hid, gtok, gw, gb = pl.pallas_call(
        functools.partial(layer_kernel, span, peers, fused, chunks, tuple(held)),
        out_shape=(
            vm(tokens.shape, BF),
            vm(tokens.shape, BF),
            vm(gw_shape, F32) if fused else jax.ShapeDtypeStruct(gw_shape, F32),
            vm((3 * width,), F32) if fused else jax.ShapeDtypeStruct((3 * width,), F32),
        ),
        in_specs=[any_spec, any_spec, vmem, vmem, any_spec],
        out_specs=(vmem, vmem, gw_spec, vmem),
        scratch_shapes=list(held.values()),
        compiler_params=pltpu.CompilerParams(
            collective_id=0, has_side_effects=True, vmem_limit_bytes=VMEM_BYTES
        ),
        name="layer",
    )(tokens, weights, bias, resets, upstream)
    if not fused:
        gw = lax.psum_scatter(gw, ("seq", "dp"), scatter_dimension=0, tiled=True)
        gb = lax.psum(gb, ("seq", "dp"))
    return hid, gtok, gw, gb


def solution(mesh):
    spread = P("dp", "seq", None)
    rows = P(("seq", "dp"), None)
    return jax.shard_map(
        per_device,
        mesh=mesh,
        in_specs=(spread, rows, P(), P("dp", "seq"), spread),
        out_specs=(spread, spread, rows, P()),
        check_vma=False,
    )
```

```python
import functools
import types

import jax
import jax.numpy as jnp
from jax import lax
from jax.experimental import pallas as pl
from jax.experimental.pallas import tpu as pltpu
from jax.sharding import PartitionSpec as P

MESH = pl.DeviceIdType.MESH
BF = jnp.bfloat16
F32 = jnp.float32
LANES = 128
TRIO = 3 * LANES
STEPS = 32
TWO = 16
VMEM_BYTES = 56 << 20
EARLY = (0, 16, 16)


def cut_chunks(width):
    tiles = width // LANES
    chunks, at = [], 0
    if tiles % 2:
        chunks.append((0, LANES))
        at = LANES
    while at < width:
        chunks.append((at, 2 * LANES))
        at += 2 * LANES
    return chunks


def dot(a, b):
    return jnp.dot(a, b, preferred_element_type=F32)


def dot_rows(a, b):
    return lax.dot_general(a, b, (((0,), (0,)), ((), ())), preferred_element_type=F32)


def dot_columns(a, b):
    return lax.dot_general(a, b, (((1,), (1,)), ((), ())), preferred_element_type=F32)


def layer_kernel(
    span, peers, fused, chunks, names,
    tok, wts, bias, resets, up,
    hid, gtok, gw, gb,
    *scratch,
):
    held = types.SimpleNamespace(**dict(zip(names, scratch)))
    joined, upt, wv, qf, keepb = held.joined, held.upt, held.wv, held.qf, held.keepb
    perm, pinv, cbuf, summ, edge = held.perm, held.pinv, held.cbuf, held.summ, held.edge
    in_sem, w_sem = held.in_sem, held.w_sem
    sum_send, sum_recv = held.sum_send, held.sum_recv
    edge_send, edge_recv = held.edge_send, held.edge_recv
    gates = [getattr(held, f"gates{c}") for c in range(len(chunks))]
    gp = [getattr(held, f"gp{c}") for c in range(len(chunks))]
    seqs, steps, width = tok.shape
    rows = seqs * steps
    block = seqs * STEPS
    blocks = steps // STEPS
    depth = 2 * width
    half_rows = depth // 2
    n_chunks = len(chunks)
    me = lax.axis_index("seq")
    col = lax.axis_index("dp")
    core = col & 1
    place = col >> 1
    plane = peers // 2
    slab = depth // (span * plane)
    shard = slab // 2
    over = -(-shard // 16) * 16
    partner = (me, col ^ 1)
    pieces = [(c, 0, TRIO) for c in range(len(chunks))]
    if fused:
        pieces[-1:] = [(len(chunks) - 1, 2 * LANES, LANES), (len(chunks) - 1, 0, 2 * LANES)]
    if fused:
        own16, pair, sb1, rb1, rb2 = held.own16, held.pair, held.sb1, held.rb1, held.rb2
        own2, rb3, fin, fin_rx, gbs = held.own2, held.rb3, held.fin, held.fin_rx, held.gbs
        a0_sem, a3_sem, r4_sem = held.a0_sem, held.a3_sem, held.r4_sem
        b1_send, b1_recv, b2_send, b2_recv = held.b1_send, held.b1_recv, held.b2_send, held.b2_recv
        a1_send, a1_recv, a2_send, a2_recv = held.a1_send, held.a1_recv, held.a2_send, held.a2_recv
        r1_send, r1_recv, r2_send, r2_recv = held.r1_send, held.r1_recv, held.r2_send, held.r2_recv
        r3_send, r3_recv, gb_send, gb_recv = held.r3_send, held.r3_recv, held.gb_send, held.gb_recv

    def remote(src, dst, send, recv, to):
        return pltpu.make_async_remote_copy(
            src_ref=src, dst_ref=dst, send_sem=send, recv_sem=recv,
            device_id=to, device_id_type=MESH,
        )

    def mult(v, m):
        return pl.multiple_of(v, m)

    in_t = pltpu.make_async_copy(tok, hid, in_sem.at[0])
    in_u = pltpu.make_async_copy(up, gtok, in_sem.at[1])
    if fused:
        in_w = pltpu.make_async_copy(wts, own16, w_sem.at[0])
        in_w.start()
    in_t.start()
    in_u.start()

    barrier = pltpu.get_barrier_semaphore()
    friends = [(lax.rem(me + k, span), col) for k in range(1, span)]
    if fused:
        friends += [(me, col ^ (2 * y)) for y in range(1, plane)] + [partner]
    for friend in friends:
        pl.semaphore_signal(barrier, inc=1, device_id=friend, device_id_type=MESH)
    pl.semaphore_wait(barrier, len(friends))

    def carried(c, who):
        at, cw = chunks[c]
        if cw == LANES:
            return over, mult((slab - over) * who, 16), 3 * at
        return slab, 0, mult(3 * at + TRIO * who, LANES)

    def part(c, who, planes, places):
        count, r0, c0 = carried(c, who)
        return wv.at[planes, places, pl.ds(r0, count), pl.ds(c0, TRIO)]

    def early(c, places):
        _, r0, c0 = carried(c, core)
        return wv.at[me, places, pl.ds(r0, EARLY[c]), pl.ds(c0, TRIO)]

    def rest(c, planes):
        count, r0, c0 = carried(c, core)
        return wv.at[planes, place, pl.ds(mult(r0 + EARLY[c], 16), count - EARLY[c]), pl.ds(c0, TRIO)]

    def a1(c, x):
        here = rest(c, me)
        return remote(here, here, a1_send.at[c, x - 1], a1_recv.at[c, x - 1], (me ^ x, col))

    def a2(c, y):
        here = rest(c, slice(None))
        return remote(here, here, a2_send.at[c, y - 1], a2_recv.at[c, y - 1], (me, col ^ (2 * y)))

    def b1(c, y):
        here = early(c, place)
        return remote(here, here, b1_send.at[c, y - 1], b1_recv.at[c, y - 1], (me, col ^ (2 * y)))

    def b2(c, x):
        here = early(c, slice(None))
        return remote(here, here, b2_send.at[c, x - 1], b2_recv.at[c, x - 1], (me ^ x, col))

    def a3(c):
        if chunks[c][1] == LANES:
            here = wv.at[
                :, :, pl.ds(mult(over * core, 16), slab - over), pl.ds(3 * chunks[c][0], TRIO)
            ]
        else:
            here = part(c, core, slice(None), slice(None))
        return remote(here, here, a3_sem.at[c, 0], a3_sem.at[c, 1], partner)

    def early_go(c):
        if not EARLY[c]:
            return
        for y in range(1, plane):
            b1(c, y).wait_recv()
        for x in range(1, span):
            b2(c, x).start()

    def plane_go(c):
        for x in range(1, span):
            a1(c, x).wait_recv()
        if c < n_chunks - 1:
            for x in range(1, span):
                a1(c + 1, x).start()
        for y in range(1, plane):
            if c:
                a2(c - 1, y).wait_send()
        for y in range(1, plane):
            a2(c, y).start()

    def cores_go(c):
        for y in range(1, plane):
            a2(c, y).wait_recv()
        for x in range(1, span):
            if EARLY[c]:
                b2(c, x).wait_recv()
        a3(c).start()

    def w_copies(c):
        at, cw = chunks[c]
        return [
            pltpu.make_async_copy(
                wts.at[:, pl.ds(g * width + at + h * LANES, LANES)],
                wv.at[:, pl.ds(3 * at + h * TRIO + g * LANES, LANES)],
                w_sem.at[c, g, h],
            )
            for g in range(3)
            for h in range(cw // LANES)
        ]

    if fused:
        in_w.wait()
        pair[core] = own16[...].astype(F32)
        a0 = remote(pair.at[core], pair.at[core], a0_sem.at[0], a0_sem.at[1], partner)
        a0.start()
    else:
        for c in range(n_chunks):
            for copy in w_copies(c):
                copy.start()

    r = lax.broadcasted_iota(jnp.int32, (block, block), 0)
    q = lax.broadcasted_iota(jnp.int32, (block, block), 1)
    perm[...] = (((q & 31) == (r >> 3)) & ((q >> 5) == (r & 7))).astype(F32).astype(BF)
    pinv[...] = (((r & 31) == (q >> 3)) & ((r >> 5) == (q & 7))).astype(F32).astype(BF)

    if fused:
        a0.wait_recv()
        for c, (at, cw) in enumerate(chunks):
            count, top, left = carried(c, core)
            for g in range(3):
                lane = g * width + at + (0 if cw == LANES else core * LANES)
                lanes = pl.ds(mult(lane, LANES), LANES)
                both = jnp.concatenate([pair[0, :, lanes], pair[1, :, lanes]], axis=0)
                if count < slab:
                    both = jnp.where(core == 0, both[:count], both[slab - count :])
                to = pl.ds(mult(left + g * LANES, LANES), LANES)
                wv[me, place, pl.ds(top, count), to] = both.astype(BF)
            if c == 0:
                for x in range(1, span):
                    a1(0, x).start()
            if EARLY[c]:
                for y in range(1, plane):
                    b1(c, y).start()

    keep = 1.0 - resets[...].astype(F32)
    tiled = jnp.broadcast_to(keep[None], (STEPS, seqs, steps)).reshape(block, steps)
    row_t = lax.broadcasted_iota(jnp.int32, (block, steps), 0) >> 3
    lane_t = lax.broadcasted_iota(jnp.int32, (block, steps), 1)
    ones = jnp.ones((steps, LANES), BF)
    for b in range(blocks):
        picked = jnp.where(lane_t == row_t + b * STEPS, tiled, 0.0).astype(BF)
        keepb[b * block : (b + 1) * block, :] = dot(picked, ones)

    def wide_keep(at, count, lanes):
        k = keepb[pl.ds(at, count), :]
        return jnp.concatenate([k] * (lanes // LANES), axis=1)

    in_t.wait()
    last_rows = hid[:, steps - STEPS :, :].reshape(block, width)
    edge[0] = dot(perm[block - TWO :, :], last_rows)[TWO - seqs :]
    to_right = remote(edge.at[0], edge.at[1], edge_send.at[0], edge_recv.at[0], (me + 1, col))

    @pl.when(me < span - 1)
    def _():
        to_right.start()

    @pl.when(me == 0)
    def _():
        edge[1] = jnp.zeros((seqs, width), F32)

    in_u.wait()
    if fused:
        early_go(0)
        early_go(1)
        plane_go(0)

    def stage(b, last):
        at = mult(b * block, block)
        src = hid[:, pl.ds(mult(b * STEPS, STEPS), STEPS), :].reshape(block, width)
        now = dot(perm[...], src)
        before = jnp.concatenate([last, now[: block - seqs]], axis=0)
        before = before * wide_keep(at, block, width)
        joined[pl.ds(at, block), :width] = now.astype(BF)
        joined[pl.ds(at, block), width:] = before.astype(BF)
        src = gtok[:, pl.ds(mult(b * STEPS, STEPS), STEPS), :].reshape(block, width)
        upt[pl.ds(at, block), :] = dot(perm[...], src).astype(BF)
        return now[block - seqs :]

    lax.fori_loop(0, blocks, stage, jnp.zeros((seqs, width), F32))

    @pl.when(me > 0)
    def _():
        to_right.wait_recv()

    @pl.when(me < span - 1)
    def _():
        to_right.wait_send()

    first = jnp.concatenate([edge[1], joined[:TWO, :width].astype(F32)[:seqs]], axis=0)
    joined[:TWO, width:] = (first * wide_keep(0, TWO, width)).astype(BF)

    def weights_of(base, count):
        if fused:
            return wv[:, :, :, base : base + count].reshape(depth, count)
        return wv[:, base : base + count]

    def pass_a(c):
        at, cw = chunks[c]
        base = 3 * at
        size = 2 * block if blocks % 2 == 0 else block
        halves = range(cw // LANES)

        def bias_rows(g, h):
            lane = g * width + at + h * LANES
            return jnp.broadcast_to(bias[lane : lane + LANES].reshape(1, LANES), (TWO, LANES))

        bias_z = [bias_rows(0, h) for h in halves]
        bias_f = [0.5 * bias_rows(1, h) for h in halves]
        bias_o = [0.5 * bias_rows(2, h) for h in halves]

        def body(i, carry):
            carry = [list(v) for v in carry]
            r0 = mult(i * size, size)
            pre = dot(joined[pl.ds(r0, size), :], weights_of(base, 3 * cw))
            for j in range(size // TWO):
                sl = pl.ds(r0 + j * TWO, TWO)
                k = keepb[sl, :]
                for h in halves:
                    zc, fc, oc = (h * TRIO + g * LANES for g in range(3))
                    now = pre[j * TWO : (j + 1) * TWO]
                    z = jnp.tanh(now[:, zc : zc + LANES] + bias_z[h])
                    f = 0.5 * jnp.tanh(0.5 * now[:, fc : fc + LANES] + bias_f[h]) + 0.5
                    o = 0.5 * jnp.tanh(0.5 * now[:, oc : oc + LANES] + bias_o[h]) + 0.5
                    gates[c][sl, zc : zc + LANES] = z
                    gates[c][sl, fc : fc + LANES] = f
                    gates[c][sl, oc : oc + LANES] = o
                    g = upt[sl, at + h * LANES : at + (h + 1) * LANES].astype(F32)
                    eff = f * k
                    fresh = (1.0 - f) * z
                    src = g * o
                    gain, state, back = carry[h]
                    for m in (0, seqs):
                        gain = gain * eff[m : m + seqs]
                        state = state * eff[m : m + seqs] + fresh[m : m + seqs]
                        back = back + gain * src[m : m + seqs]
                    carry[h] = [gain, state, back]
            return tuple(tuple(v) for v in carry)

        zero = jnp.zeros((seqs, LANES), F32)
        one = jnp.ones((seqs, LANES), F32)
        done = lax.fori_loop(0, rows // size, body, tuple((one, zero, zero) for _ in halves))
        for h in halves:
            cols = slice(at + h * LANES, at + (h + 1) * LANES)
            for v in range(3):
                summ[me, v * seqs : (v + 1) * seqs, cols] = done[h][v]
        for k in range(1, span):
            exchange(c, k).start()

    def exchange(c, k):
        at, cw = chunks[c]
        here = summ.at[me, :, pl.ds(at, cw)]
        return remote(
            here, here, sum_send.at[c, k - 1], sum_recv.at[c, k - 1], (lax.rem(me + k, span), col)
        )

    def pass_b(c, between=()):
        at, cw = chunks[c]
        halves = range(cw // LANES)
        for k in range(1, span):
            exchange(c, k).wait()
        enter, leave = [], []
        for h in halves:
            cols = slice(at + h * LANES, at + (h + 1) * LANES)
            state = jnp.zeros((seqs, LANES), F32)
            for s in range(span - 1):
                new = summ[s, seqs : 2 * seqs, cols] + summ[s, :seqs, cols] * state
                state = jnp.where(s < me, new, state)
            enter.append(state)
            back = jnp.zeros((seqs, LANES), F32)
            for s in range(span - 1, 0, -1):
                new = summ[s, 2 * seqs :, cols] + summ[s, :seqs, cols] * back
                back = jnp.where(s > me, new, back)
            leave.append(back)

        def forward(i, carry):
            cells, sums = list(carry[0]), list(carry[1])
            r0 = mult(i * block, block)
            for j in range(block // TWO):
                sl = pl.ds(r0 + j * TWO, TWO)
                k = keepb[sl, :]
                for h in halves:
                    zc, fc, oc = (h * TRIO + g * LANES for g in range(3))
                    z = gates[c][sl, zc : zc + LANES]
                    f = gates[c][sl, fc : fc + LANES]
                    o = gates[c][sl, oc : oc + LANES]
                    lanes = slice(at + h * LANES, at + (h + 1) * LANES)
                    g = upt[sl, lanes].astype(F32)
                    eff = f * k
                    rest = 1.0 - f
                    fresh = rest * z
                    c0 = eff[:seqs] * cells[h] + fresh[:seqs]
                    c1 = eff[seqs:] * c0 + fresh[seqs:]
                    cell = jnp.concatenate([c0, c1], axis=0)
                    prev = jnp.concatenate([cells[h], c0], axis=0)
                    cells[h] = c1
                    hid[j // 2, pl.ds(mult(i * STEPS + j % 2 * TWO, TWO), TWO), lanes] = (
                        o * cell
                    ).astype(BF)
                    src = g * o
                    go = src * cell * (1.0 - o)
                    gp[c][sl, oc : oc + LANES] = go.astype(BF)
                    sums[h] = sums[h] + go
                    gates[c][sl, zc : zc + LANES] = rest * (1.0 - z * z)
                    gates[c][sl, fc : fc + LANES] = eff
                    gates[c][sl, oc : oc + LANES] = src
                    qf[sl, h * LANES : (h + 1) * LANES] = (prev * k - z) * (f * rest)
            return tuple(cells), tuple(sums)

        zero = jnp.zeros((TWO, LANES), F32)
        zeros = tuple(zero for _ in halves)
        _, sum_o = lax.fori_loop(0, blocks, forward, (tuple(enter), zeros))

        for step in between:
            step()

        def backward(n, carry):
            heads, sums_z, sums_f = (list(v) for v in carry)
            r0 = mult((blocks - 1 - n) * block, block)
            for j in range(block // TWO - 1, -1, -1):
                sl = pl.ds(r0 + j * TWO, TWO)
                for h in halves:
                    zc, fc, oc = (h * TRIO + g * LANES for g in range(3))
                    eff = gates[c][sl, fc : fc + LANES]
                    src = gates[c][sl, oc : oc + LANES]
                    g1 = src[seqs:] + heads[h]
                    g0 = src[:seqs] + eff[seqs:] * g1
                    heads[h] = eff[:seqs] * g0
                    gc = jnp.concatenate([g0, g1], axis=0)
                    gz = gc * gates[c][sl, zc : zc + LANES]
                    gf = gc * qf[sl, h * LANES : (h + 1) * LANES]
                    gp[c][sl, zc : zc + LANES] = gz.astype(BF)
                    gp[c][sl, fc : fc + LANES] = gf.astype(BF)
                    sums_z[h] = sums_z[h] + gz
                    sums_f[h] = sums_f[h] + gf
            return tuple(heads), tuple(sums_z), tuple(sums_f)

        _, sum_z, sum_f = lax.fori_loop(0, blocks, backward, (tuple(leave), zeros, zeros))
        for h in halves:
            for g, total in enumerate((sum_z, sum_f, sum_o)):
                line = jnp.sum(total[h], axis=0, keepdims=True)
                if fused:
                    tile = g * (width // LANES) + at // LANES + h
                    gbs[0, tile : tile + 1, :] = line
                else:
                    lane = g * width + at + h * LANES
                    gb[lane : lane + LANES] = line.reshape(LANES)

    def gw_copies(c, turn):
        at, cw = chunks[c]
        return [
            pltpu.make_async_copy(
                cbuf.at[turn, :, pl.ds(h * TRIO + g * LANES, LANES)],
                gw.at[pl.ds(turn * half_rows, half_rows), pl.ds(g * width + at + h * LANES, LANES)],
                w_sem.at[c, g, h],
            )
            for g in range(3)
            for h in range(cw // LANES)
        ]

    def pass_c(p, turn):
        c, lane, lanes = pieces[p]
        at, cw = chunks[c]
        if fused:
            r0 = mult(((me // (span // 2)) ^ 1 ^ turn) * half_rows, LANES)
            if p and pieces[p - 1][0] != c:
                r1_copy(p - 1, turn).wait_send()
            right = [
                gp[c][:, h * TRIO + lane : h * TRIO + lane + lanes] for h in range(cw // LANES)
            ]
            result = dot_rows(joined[:, pl.ds(r0, half_rows)], jnp.concatenate(right, axis=1))
            result = result.reshape(-1, slab, result.shape[-1])
            count = carried(c, 0)[0]
            if cw == LANES:
                zero, one = result[:, :count], result[:, slab - count :]
            else:
                zero, one = result[:, :, :lanes], result[:, :, lanes:]
            cols = slice(lane, lane + lanes)
            cbuf[turn, :, :count, cols] = jnp.where(core == 0, zero, one)
            sb1[turn, :, :count, cols] = jnp.where(core == 0, one, zero).astype(BF)
            r1_copy(p, turn).start()
        else:
            if c:
                for copy in gw_copies(c - 1, turn):
                    copy.wait()
            cbuf[turn, :, : 3 * cw] = dot_rows(
                joined[:, turn * half_rows : (turn + 1) * half_rows], gp[c][...]
            )
            for copy in gw_copies(c, turn):
                copy.start()

    def spot(p):
        c, lane, lanes = pieces[p]
        return c, pl.ds(0, carried(c, 0)[0]), pl.ds(lane, lanes)

    def orders(turn):
        half = span // 2
        return list(range(half, span)) if turn == 0 else list(range(half - 1, -1, -1))

    def r1_copy(p, turn):
        c, k, l = spot(p)
        return remote(
            sb1.at[turn, :, k, l], rb1.at[c, turn, :, k, l],
            r1_send.at[p, turn], r1_recv.at[p, turn], partner,
        )

    def r2_copy(p, turn, n, y):
        c, k, l = spot(p)
        x = orders(turn)[n]
        index = ((me ^ x) % (span // 2)) * plane + (place ^ y)
        return remote(
            rb1.at[c, turn, index, k, l], rb2.at[c, turn, n, y - 1, k, l],
            r2_send.at[p, turn, n, y - 1], r2_recv.at[p, turn, n, y - 1], (me, col ^ (2 * y)),
        )

    def r2(p, turn):
        r1_copy(p, turn).wait_recv()
        c, k, l = spot(p)
        for n, x in enumerate(orders(turn)):
            for y in range(plane - 1, -1, -1):
                index = ((me ^ x) % (span // 2)) * plane + (place ^ y)
                total = cbuf[turn, index, k, l] + rb1[c, turn, index, k, l].astype(F32)
                if y:
                    rb1[c, turn, index, k, l] = total.astype(BF)
                    r2_copy(p, turn, n, y).start()
                else:
                    own2[c, turn, n, k, l] = total

    def r3_copy(p, turn, n):
        c, k, l = spot(p)
        x = orders(turn)[n]
        return remote(
            rb2.at[c, turn, n, 0, k, l], rb3.at[c, x - 1, k, l], r3_send.at[p, x - 1],
            r3_recv.at[p, x - 1], (me ^ x, col),
        )

    def r3(p, turn):
        c, k, l = spot(p)
        for n, x in enumerate(orders(turn)):
            total = own2[c, turn, n, k, l]
            for y in range(1, plane):
                r2_copy(p, turn, n, y).wait_recv()
                total = total + rb2[c, turn, n, y - 1, k, l].astype(F32)
            if x:
                rb2[c, turn, n, 0, k, l] = total.astype(BF)
                r3_copy(p, turn, n).start()
            else:
                own2[c, turn, n, k, l] = total

    def r4_copy(p):
        c, _, l = spot(p)
        return remote(
            fin.at[c, pl.ds(mult(shard * (1 - core), 8), shard), l], fin_rx.at[c, :, l],
            r4_sem.at[p, 0], r4_sem.at[p, 1], partner,
        )

    def put_gw(p, tile, value):
        c, first, lanes = pieces[p]
        for g in range(lanes // LANES):
            gate = first // LANES + g
            lane = mult(gate * width + chunks[c][0] + tile * LANES, LANES)
            gw[:, pl.ds(lane, LANES)] = value[:, g * LANES : (g + 1) * LANES]

    def each_seq_peer():
        return [(turn, n, x) for turn in (0, 1) for n, x in enumerate(orders(turn)) if x]

    def r4(p):
        c, k, l = spot(p)
        total = own2[c, 1, span // 2 - 1, k, l]
        for turn, n, x in each_seq_peer():
            r3_copy(p, turn, n).wait_recv()
            total = total + rb3[c, x - 1, k, l].astype(F32)
        fin[c, k, l] = total
        if chunks[c][1] == LANES:
            off = (slab - over) * core
            put_gw(p, 0, fin[c, pl.ds(mult(shard * core - off, 8), shard), l])
        else:
            r4_copy(p).start()
            put_gw(p, core, fin[c, pl.ds(mult(shard * core, 8), shard), l])

    def r5(p):
        c, _, l = spot(p)
        r4_copy(p).wait_recv()
        put_gw(p, 1 - core, fin_rx[c, :, l])

    def gb_stage(stage):
        if stage == 0:
            peer = [((me ^ x, col), x - 1) for x in range(1, span)]
        elif stage == 1:
            peer = [((me, col ^ (2 * y)), span - 1 + y - 1) for y in range(1, plane)]
        else:
            peer = [(partner, span + plane - 2)]
        src = gbs.at[stage]
        return [(remote(src, gbs.at[4 + k], gb_send.at[k], gb_recv.at[k], to), k) for to, k in peer]

    def gb_go(stage):
        for copy, _ in gb_stage(stage):
            copy.start()

    def gb_sum(stage):
        total = gbs[stage]
        for copy, k in gb_stage(stage):
            copy.wait_recv()
            total = total + gbs[4 + k]
        gbs[stage + 1] = total

    last = n_chunks - 1
    if not fused:
        for c in range(n_chunks):
            for copy in w_copies(c):
                copy.wait()
            pass_a(c)
        for c in range(n_chunks):
            pass_b(c)
            pass_c(c, 0)
            pass_c(c, 1)
    else:
        gbs[0] = jnp.zeros(gbs.shape[1:], F32)
        plane_go(1)
        cores_go(0)
        a3(0).wait_recv()
        pass_a(0)
        cores_go(1)
        plane_go(2)
        pass_b(0)
        early_go(2)
        a3(1).wait_recv()
        pass_a(1)
        pass_c(0, 0)
        cores_go(2)
        pass_c(0, 1)
        r2(0, 0)
        a3(2).wait_recv()
        pass_a(2)
        r2(0, 1)
        pass_b(1, [lambda: r3(0, 0)])
        pass_c(1, 0)
        r3(0, 1)
        pass_c(1, 1)
        r2(1, 0)
        pass_b(
            2, [lambda: r2(1, 1), lambda: pass_c(2, 0), lambda: r4(0), lambda: pass_c(2, 1), lambda: r2(2, 0)]
        )
        gb_go(0)
        r3(1, 0)
        r2(2, 1)
        pass_c(3, 0)
        r3(1, 1)
        pass_c(3, 1)
        r2(3, 0)

    to_left = remote(edge.at[2], edge.at[3], edge_send.at[1], edge_recv.at[1], (me - 1, col))

    @pl.when(me == span - 1)
    def _():
        edge[3] = jnp.zeros((seqs, width), F32)

    late_gt = gates[last]

    def settle(ref, b, value):
        out = dot(pinv[...], value).astype(BF)
        ref[:, pl.ds(mult(b * STEPS, STEPS), STEPS), :] = out.reshape(seqs, STEPS, width)

    def put(b):
        settle(gtok, b, late_gt[pl.ds(mult(b * block, block), block), :width].astype(BF))

    def put_hidden(b):
        settle(hid, b, hid[:, pl.ds(mult(b * STEPS, STEPS), STEPS), :].reshape(block, width))

    def late_links(i):
        plan = {
            0: [lambda: r2(3, 1), lambda: gb_sum(0), lambda: gb_go(1)],
            1: [lambda: r3(2, 0)],
            2: [lambda: r3(2, 1), lambda: gb_sum(1), lambda: gb_go(2)],
            3: [lambda: r4(1)],
            4: [lambda: r3(3, 0), lambda: gb_sum(2)],
            5: [lambda: r3(3, 1), lambda: r5(1)],
            6: [lambda: r4(2)],
            7: [lambda: r5(2)],
        }
        for when, todo in plan.items():

            @pl.when(i == when)
            def _(todo=todo):
                for step in todo:
                    step()

    def inputs(i, pend):
        r0 = mult(i * block, block)
        put_hidden(i)
        put(jnp.maximum(i - 2, 0))
        grads = jnp.concatenate([g[pl.ds(r0, block), :] for g in gp], axis=1)
        both = dot_columns(grads, weights_of(0, 3 * width))
        own = both[:, :width]
        late = both[:, width:] * wide_keep(r0, block, width)
        late_gt[pl.ds(r0, block - seqs), :width] = own[: block - seqs] + late[seqs:]
        before = jnp.where(i == 0, rows - seqs, r0 - seqs)
        late_gt[pl.ds(mult(before, seqs), seqs), :width] = pend + late[:seqs]

        @pl.when(i == 0)
        def _():
            edge[2] = late[:seqs]

            @pl.when(me > 0)
            def _():
                to_left.start()

        if fused:
            late_links(i)
        return own[block - seqs :]

    pend = lax.fori_loop(0, blocks, inputs, jnp.zeros((seqs, width), F32))

    @pl.when(me < span - 1)
    def _():
        to_left.wait_recv()

    @pl.when(me > 0)
    def _():
        to_left.wait_send()

    late_gt[rows - seqs :, :width] = pend + edge[3]
    put(blocks - 2)
    put(blocks - 1)
    if not fused:
        for turn in (0, 1):
            for copy in gw_copies(n_chunks - 1, turn):
                copy.wait()
    else:
        for g in range(3 * width // LANES):
            gb[g * LANES : (g + 1) * LANES] = gbs[3, g : g + 1, :].reshape(LANES)
        r4(3)
        a0.wait_send()
        for c in range(n_chunks):
            a3(c).wait_send()
            for x in range(1, span):
                a1(c, x).wait_send()
                if EARLY[c]:
                    b2(c, x).wait_send()
            for y in range(1, plane):
                if EARLY[c]:
                    b1(c, y).wait_send()
        for y in range(1, plane):
            a2(last, y).wait_send()
        for p in range(len(pieces)):
            for turn in (0, 1):
                if pieces[p][0] == last:
                    r1_copy(p, turn).wait_send()
                for n, x in enumerate(orders(turn)):
                    for y in range(1, plane):
                        r2_copy(p, turn, n, y).wait_send()
                    if x:
                        r3_copy(p, turn, n).wait_send()
            if chunks[pieces[p][0]][1] != LANES:
                r4_copy(p).wait_send()
        for stage_index in range(3):
            for copy, _ in gb_stage(stage_index):
                copy.wait_send()
        r5(3)


def per_device(tokens, weights, bias, resets, upstream):
    seqs, steps, width = tokens.shape
    rows = seqs * steps
    span, peers = lax.axis_size("seq"), lax.axis_size("dp")
    chunks = cut_chunks(width)
    n_chunks = len(chunks)
    block = seqs * STEPS
    depth = 2 * width
    shard = weights.shape[0]
    slab = 2 * shard
    plane = peers // 2
    half = span // 2
    fused = shard % 8 == 0 and slab % 16 == 0 and n_chunks == 3 and steps // STEPS >= 8
    any_spec = pl.BlockSpec(memory_space=pl.ANY)
    vmem = pl.BlockSpec(memory_space=pltpu.VMEM)
    dma = pltpu.SemaphoreType.DMA
    vm = pltpu.VMEM
    held = {
        "joined": vm((rows, depth), BF),
        "upt": vm((rows, width), BF),
        "qf": vm((rows, 2 * LANES), F32),
        "keepb": vm((rows, LANES), F32),
        "perm": vm((block, block), BF),
        "pinv": vm((block, block), BF),
        "summ": vm((span, 3 * seqs, width), F32),
        "edge": vm((4, seqs, width), F32),
        "in_sem": dma((2,)),
        "sum_send": dma((n_chunks, span - 1)),
        "sum_recv": dma((n_chunks, span - 1)),
        "edge_send": dma((2,)),
        "edge_recv": dma((2,)),
    }
    for c, (_, cw) in enumerate(chunks):
        held[f"gates{c}"] = vm((rows, 3 * cw), F32)
        held[f"gp{c}"] = vm((rows, 3 * cw), BF)
    if fused:
        gw_shape, gw_spec = (shard, 3 * width), vmem
        piece = (half * plane, slab, TRIO)
        held |= {
            "wv": vm((span, plane, slab, 3 * width), BF),
            "cbuf": vm((2, *piece), F32),
            "own16": vm((shard, 3 * width), BF),
            "pair": vm((2, shard, 3 * width), F32),
            "sb1": vm((2, *piece), BF),
            "rb1": vm((n_chunks, 2, *piece), BF),
            "rb2": vm((n_chunks, 2, half, plane - 1, slab, TRIO), BF),
            "own2": vm((n_chunks, 2, half, slab, TRIO), F32),
            "rb3": vm((n_chunks, span - 1, slab, TRIO), BF),
            "fin": vm((n_chunks, slab, TRIO), F32),
            "fin_rx": vm((n_chunks, shard, TRIO), F32),
            "gbs": vm((4 + span + plane - 1, 16, LANES), F32),
            "w_sem": dma((1,)),
            "a0_sem": dma((2,)),
            "a1_send": dma((n_chunks, span - 1)),
            "a1_recv": dma((n_chunks, span - 1)),
            "a2_send": dma((n_chunks, plane - 1)),
            "a2_recv": dma((n_chunks, plane - 1)),
            "b1_send": dma((n_chunks, plane - 1)),
            "b1_recv": dma((n_chunks, plane - 1)),
            "b2_send": dma((n_chunks, span - 1)),
            "b2_recv": dma((n_chunks, span - 1)),
            "a3_sem": dma((n_chunks, 2)),
            "r1_send": dma((n_chunks + 1, 2)),
            "r1_recv": dma((n_chunks + 1, 2)),
            "r2_send": dma((n_chunks + 1, 2, half, plane - 1)),
            "r2_recv": dma((n_chunks + 1, 2, half, plane - 1)),
            "r3_send": dma((n_chunks + 1, span - 1)),
            "r3_recv": dma((n_chunks + 1, span - 1)),
            "r4_sem": dma((n_chunks + 1, 2)),
            "gb_send": dma((span + plane - 1,)),
            "gb_recv": dma((span + plane - 1,)),
        }
    else:
        weights = lax.all_gather(weights, ("seq", "dp"), axis=0, tiled=True)
        gw_shape, gw_spec = (depth, 3 * width), any_spec
        held |= {
            "wv": vm((depth, 3 * width), BF),
            "cbuf": vm((2, depth // 2, 2 * TRIO), F32),
            "w_sem": dma((n_chunks, 3, 2)),
        }
    hid, gtok, gw, gb = pl.pallas_call(
        functools.partial(layer_kernel, span, peers, fused, chunks, tuple(held)),
        out_shape=(
            vm(tokens.shape, BF),
            vm(tokens.shape, BF),
            vm(gw_shape, F32) if fused else jax.ShapeDtypeStruct(gw_shape, F32),
            vm((3 * width,), F32) if fused else jax.ShapeDtypeStruct((3 * width,), F32),
        ),
        in_specs=[any_spec, any_spec, vmem, vmem, any_spec],
        out_specs=(vmem, vmem, gw_spec, vmem),
        scratch_shapes=list(held.values()),
        compiler_params=pltpu.CompilerParams(
            collective_id=0, has_side_effects=True, vmem_limit_bytes=VMEM_BYTES
        ),
        name="layer",
    )(tokens, weights, bias, resets, upstream)
    if not fused:
        gw = lax.psum_scatter(gw, ("seq", "dp"), scatter_dimension=0, tiled=True)
        gb = lax.psum(gb, ("seq", "dp"))
    return hid, gtok, gw, gb


def solution(mesh):
    spread = P("dp", "seq", None)
    rows = P(("seq", "dp"), None)
    return jax.shard_map(
        per_device,
        mesh=mesh,
        in_specs=(spread, rows, P(), P("dp", "seq"), spread),
        out_specs=(spread, spread, rows, P()),
        check_vma=False,
    )
```
